32 devices in a mesh: slab: 4 (over z), grp: 8 (over y, x, core).
Axes of the slice: x: 2, y: 2, z: 4, core: 2. Of those that a mesh axis runs over, the one named last changes fastest.
Arguments:
- coords: float32 [3, 262144], P(None, ('slab', 'grp')), may hold values from -1 to 1
- charges: float32 [262144], P(('slab', 'grp')), may hold values from -1.5 to 1.5
- multipoles: float32 [121, 16384], P(None, ('slab', 'grp')), may hold values from -6 to 6
- operators: float32 [8, 121, 121], replicated, may hold values from -0.5 to 0.5
- send_list: int32 [32, 128], P(('slab', 'grp')), may hold values from 0 to 511
- near_list: int32 [16384, 8], P(('slab', 'grp')), may hold values from 0 to 1535
- m2l_source: int32 [32, 4096], P(('slab', 'grp')), may hold values from 0 to 127
- m2l_target: int32 [32, 4096], P(('slab', 'grp')), may hold values from 0 to 512, as said below
- m2l_operator: int32 [32, 4096], P(('slab', 'grp')), may hold values from 0 to 7
Outputs:
- local_exp: float32 [121, 16384], P(None, ('slab', 'grp'))
- near_potential: float32 [262144], P(('slab', 'grp'))
The draws below stay inside these ranges and needn't reach their ends.
Inputs may be any that keep to these rules, and one draw needn't show every extreme that they name: `m2l_target`: entries past a block's count of used slots hold 512, an empty slot; the first block uses all 4096 slots.
All inputs are finite; a program needn't handle non-finite values.
Results may differ from the reference program's by a relative error of at most 0.00011.
Values sent between devices are 32-bit elements; how exact they have to be, the bound alone decides.
No kernel may reach another device: no remote copies, remote signals or barrier semaphores. Data moves between devices by JAX's collectives and lax.ppermute only.
A program may use at most 64 MiB of HBM per device.

```python
import jax
import jax.numpy as jnp
from jax import lax

NCOEF = 121
LEAF_PTS = 16
LEAVES_DEV = 512
NEAR = 8
CAP = 16
OPS = 8
LIST = 4096
TOTAL_LEAVES = 16384
POINTS = 262144
N_SLAB = 4
N_GRP = 8


def draw_m2l_target(key, part):
    key = jax.random.fold_in(key, 7)
    count_key, leaf_key = jax.random.split(key)
    blocks_all = N_SLAB * N_GRP
    counts = jax.random.randint(count_key, (blocks_all, 1), LIST // 4, LIST + 1)
    counts = counts.at[0, 0].set(LIST)
    leaves = jax.random.randint(leaf_key, (blocks_all, LIST), 0, LEAVES_DEV)
    slots = jnp.arange(LIST, dtype=jnp.int32)[None, :]
    return jnp.where(slots < counts, leaves, LEAVES_DEV).astype(jnp.int32)


def plant(array, key, low, largest):
    longest = array.shape.index(max(array.shape))
    spots = []
    for shift in (0, 1):
        where = [jax.random.randint(jax.random.fold_in(key, axis), (), 0, length) for axis, length in enumerate(array.shape)]
        where[longest] = (where[longest] + shift) % array.shape[longest]
        spots.append(tuple(where))
    return array.at[spots[0]].set(low).at[spots[1]].set(largest)


def block_scale(stream_key, extent, cuts, smallest, high):
    factor_of = 1.0
    for position, blocks in cuts:
        heights = jax.random.uniform(jax.random.fold_in(jax.random.fold_in(stream_key, 6), position), (blocks,), jnp.float32, smallest / len(cuts), high / len(cuts))
        factor_of = factor_of * jnp.repeat(jnp.exp(heights), extent[position] // blocks).reshape((-1,) + (1,) * (len(extent) - 1 - position))
    return factor_of


def normal_values(rng, extent, width, reach, cuts=(), kind=jnp.bfloat16):
    entries = jax.random.normal(rng, extent, jnp.float32) * width
    if len(cuts) > 0:
        entries = block_scale(rng, extent, cuts, -0.22, 0.18) * entries
    return jnp.clip(entries, min=-reach, max=reach).astype(kind)


def setup_inputs(seed: int = 0) -> dict:
    key_list = jax.random.split(jax.random.key(seed), 10)
    coords = jnp.clip(jax.random.uniform(key_list[0], (3, POINTS), jnp.float32, -1.0, 1.0) * block_scale(key_list[0], (3, POINTS), ((1, 32),), -0.4, 0.0), -1.0, 1.0)
    charges = normal_values(key_list[1], (POINTS,), 0.1, 1.5, ((0, 32),), jnp.float32)
    multipoles = normal_values(key_list[2], (NCOEF, TOTAL_LEAVES), 1.0, 6.0, ((1, 32),), jnp.float32)
    operators = normal_values(key_list[3], (OPS, NCOEF, NCOEF), NCOEF ** -0.5, 0.5, (), jnp.float32)
    send_list = plant(jax.random.randint(key_list[4], (N_SLAB * N_GRP, N_GRP * CAP), 0, LEAVES_DEV), jax.random.fold_in(key_list[4], 1), 0, LEAVES_DEV - 1).astype(jnp.int32)
    near_list = plant(jax.random.randint(key_list[5], (TOTAL_LEAVES, NEAR), 0, 3 * LEAVES_DEV), jax.random.fold_in(key_list[5], 1), 0, (3 * LEAVES_DEV) - 1).astype(jnp.int32)
    m2l_source = plant(jax.random.randint(key_list[6], (N_SLAB * N_GRP, LIST), 0, N_GRP * CAP), jax.random.fold_in(key_list[6], 1), 0, (N_GRP * CAP) - 1).astype(jnp.int32)
    m2l_target = draw_m2l_target(jax.random.fold_in(key_list[9], 71), 0)
    m2l_operator = plant(jax.random.randint(key_list[8], (N_SLAB * N_GRP, LIST), 0, OPS), jax.random.fold_in(key_list[8], 1), 0, OPS - 1).astype(jnp.int32)
    return dict(coords=coords, charges=charges, multipoles=multipoles, operators=operators, send_list=send_list, near_list=near_list, m2l_source=m2l_source, m2l_target=m2l_target, m2l_operator=m2l_operator)


SOFT2 = 0.0625

def near_block(args):
    window, targets, lists = args
    picked = jnp.take(window, lists, axis=1)
    sources = picked.reshape(4, LEAVES_DEV, NEAR * LEAF_PTS)
    tgt = jnp.transpose(targets, (0, 2, 1))
    dx = tgt[0][:, :, None] - sources[0][None]
    dy = tgt[1][:, :, None] - sources[1][None]
    dz = tgt[2][:, :, None] - sources[2][None]
    inverse = 1.0 / jnp.sqrt(dx * dx + dy * dy + dz * dz + SOFT2)
    potential = lax.optimization_barrier(jnp.sum(inverse * sources[3][None], axis=2))
    return potential.T.reshape(-1)

def reference(coords, charges, multipoles, operators, send_list, near_list, m2l_source, m2l_target, m2l_operator):
    blocks_all = N_SLAB * N_GRP
    stacked = jnp.concatenate([coords, charges[None, :]], axis=0)
    blocks = stacked.reshape(4, N_SLAB, N_GRP, LEAVES_DEV, LEAF_PTS)
    padded = jnp.pad(blocks, ((0, 0), (1, 1), (0, 0), (0, 0), (0, 0)))
    window = jnp.concatenate([padded[:, :-2], padded[:, 1:-1], padded[:, 2:]], axis=3)
    window = jnp.transpose(window.reshape(4, blocks_all, 3 * LEAVES_DEV, LEAF_PTS), (1, 0, 2, 3))
    targets = jnp.transpose(blocks.reshape(4, blocks_all, LEAVES_DEV, LEAF_PTS), (1, 0, 2, 3))
    lists = near_list.reshape(blocks_all, LEAVES_DEV, NEAR)
    near_potential = lax.map(near_block, (window, targets, lists)).reshape(-1)
    sends = send_list.reshape(N_SLAB, N_GRP, N_GRP, CAP)
    base = (jnp.arange(N_SLAB, dtype=jnp.int32)[:, None] * N_GRP + jnp.arange(N_GRP, dtype=jnp.int32)[None, :]) * LEAVES_DEV
    global_index = sends + base[:, :, None, None]
    global_index = jnp.transpose(global_index, (0, 2, 1, 3)).reshape(blocks_all, N_GRP * CAP).astype(jnp.int32)

    def far_block(args):
        index_row, source_row, target_row, operator_row = args
        columns = jnp.take(multipoles, jnp.take(index_row, source_row), axis=1)
        matrices = jnp.take(operators, operator_row, axis=0)
        translated = jnp.einsum('ecd,de->ce', matrices, columns, precision=lax.Precision.HIGHEST)
        summed = jax.ops.segment_sum(translated.T, target_row, num_segments=LEAVES_DEV + 1)
        return summed[:LEAVES_DEV].T
    local_exp = lax.map(far_block, (global_index, m2l_source, m2l_target, m2l_operator))
    local_exp = jnp.transpose(local_exp, (1, 0, 2)).reshape(NCOEF, blocks_all * LEAVES_DEV)
    return (local_exp, near_potential)
```

```python
import functools

import jax
import jax.numpy as jnp
from jax import lax
from jax.experimental import pallas as pl
from jax.experimental.pallas import tpu as pltpu
from jax.sharding import PartitionSpec as P

SOFT2 = 0.0625
LANES = 128
VMEM = pl.BlockSpec(memory_space=pltpu.VMEM)
ANY = pl.BlockSpec(memory_space=pl.ANY)
PARAMS = pltpu.CompilerParams(vmem_limit_bytes=48 * 1024 * 1024)
WIDE = pltpu.CompilerParams(vmem_limit_bytes=64 * 1024 * 1024)


def lane_gather(x, idx):
    return jnp.take_along_axis(x, idx, axis=1, mode="promise_in_bounds")


def prep_kernel(coords_hbm, charges_hbm, multipoles_hbm, send_hbm, table_ref, out_ref, coords_ref, charges_ref, multipoles_ref, send_ref, sems):
    pairs = (
        (coords_hbm, coords_ref),
        (charges_hbm, charges_ref),
        (send_hbm, send_ref),
        (multipoles_hbm, multipoles_ref),
    )
    copies = [pltpu.make_async_copy(src, dst, sems.at[i]) for i, (src, dst) in enumerate(pairs)]
    for copy in copies:
        copy.start()
    copies[0].wait()
    copies[1].wait()
    for c in range(4):
        rows = charges_ref[...] if c == 3 else coords_ref[:, c, :]
        cols = rows.T
        for pair in range(4):
            a = cols[32 * pair : 32 * pair + 16, :]
            b = cols[32 * pair + 16 : 32 * pair + 32, :]
            table_ref[16 * c : 16 * c + 16, LANES * pair : LANES * (pair + 1)] = jnp.concatenate([a, b], axis=1)
    copies[2].wait()
    copies[3].wait()
    ncoef, leaves = multipoles_ref.shape
    for sb in range(send_ref.shape[1] // LANES):
        send = send_ref[:, LANES * sb : LANES * (sb + 1)]
        lane = send & (LANES - 1)
        group = send >> 7
        idx = jnp.broadcast_to(lane, (ncoef, LANES))
        picked = jnp.zeros((ncoef, LANES), jnp.float32)
        for g in range(leaves // LANES):
            got = lane_gather(multipoles_ref[:, LANES * g : LANES * (g + 1)], idx)
            picked = jnp.where(group == g, got, picked)
        out_ref[LANES * sb : LANES * (sb + 1), :] = picked.T


def count_kernel(source_ref, target_ref, operator_ref, low_ref, high_ref, flag_ref, acc_ref, *, sources, leaves, chunk):
    nrows = acc_ref.shape[1]
    entries = source_ref.shape[1]
    base = pl.program_id(0) * nrows
    half = entries // 2
    for h in range(2):
        for k in range(half // chunk):
            at = pl.ds(h * half + k * chunk, chunk)
            op = operator_ref[:, at]
            code = (op >> 1) * sources + source_ref[:, at] - base
            weight = jnp.where((op & 1) == 1, 4096.0, 1.0)
            a = jnp.where(lax.broadcasted_iota(jnp.int32, (nrows, chunk), 0) == code, weight, 0.0).astype(jnp.bfloat16)
            b = jnp.where(
                lax.broadcasted_iota(jnp.int32, (leaves, chunk), 0) == target_ref[:, at], 1.0, 0.0
            ).astype(jnp.bfloat16)
            part = lax.dot_general(a, b, (((1,), (1,)), ((), ())), preferred_element_type=jnp.float32)
            if k == 0:
                acc_ref[h] = part
            else:
                acc_ref[h] += part
    first, second = acc_ref[0], acc_ref[1]
    odd_first = jnp.floor(first * (1.0 / 4096.0))
    odd_second = jnp.floor(second * (1.0 / 4096.0))
    odd = odd_first + odd_second
    even = (first + second) - 4096.0 * odd
    top = jnp.zeros((), jnp.float32)
    for i, count in enumerate((even, odd)):
        high = 256.0 * jnp.floor(count * (1.0 / 256.0))
        low_ref[i] = (count - high).astype(jnp.bfloat16)
        high_ref[i] = high.astype(jnp.bfloat16)
        top = jnp.maximum(top, jnp.max(high))
    flag_ref[0, 0, 0] = (top > 0.0).astype(jnp.int32)


def split(x):
    hi = x.astype(jnp.bfloat16)
    return hi, (x - hi.astype(jnp.float32)).astype(jnp.bfloat16)


def far_kernel(flag_ref, operators_ref, gathered_hbm, low_ref, high_ref, out_ref, received_ref, table_ref, split_ref, sems, *, ops):
    ncoef, leaves = out_ref.shape
    peers, sources, _ = gathered_hbm.shape
    cap = sources // peers
    start = pl.multiple_of(lax.axis_index("grp") * cap, cap)
    copies = [
        pltpu.make_async_copy(
            gathered_hbm.at[p, pl.ds(start, cap), :], received_ref.at[pl.ds(cap * p, cap), :], sems.at[p]
        )
        for p in range(peers)
    ]
    for copy in copies:
        copy.start()
    for copy in copies:
        copy.wait()
    blocks = sources // LANES
    for k in range(blocks):
        table_ref[k] = lax.dot_general(
            operators_ref[...],
            received_ref[LANES * k : LANES * (k + 1), :],
            (((1,), (1,)), ((), ())),
            precision=lax.Precision.HIGHEST,
            preferred_element_type=jnp.float32,
        )
    split_ref[...] = jnp.zeros_like(split_ref)
    for op in range(ops):
        for k in range(blocks):
            lane = ((op % 2) * (ops // 2) + op // 2) * sources + LANES * k
            hi, lo = split(table_ref[k, pl.ds(op, ncoef, stride=ops), :])
            split_ref[:ncoef, lane : lane + LANES] = hi
            split_ref[LANES : LANES + ncoef, lane : lane + LANES] = lo

    def product(counts_ref):
        both = jnp.dot(split_ref[...], counts_ref[...], preferred_element_type=jnp.float32)
        return both[:ncoef, :] + both[LANES : LANES + ncoef, :]

    out_ref[...] = product(low_ref)
    flagged = flag_ref[0, 0, 0]
    for i in range(1, flag_ref.shape[0]):
        flagged = flagged | flag_ref[i, 0, 0]

    @pl.when(flagged > 0)
    def _():
        out_ref[...] += product(high_ref)


def near_kernel(gathered_hbm, own_ref, list_ref, out_ref, left_ref, right_ref, picked_ref, place_ref, pot_ref, sems):
    pts = 16
    slabs = gathered_hbm.shape[0]
    me = lax.axis_index("slab")
    sides = ((left_ref, me > 0, jnp.maximum(me - 1, 0)), (right_ref, me < slabs - 1, jnp.minimum(me + 1, slabs - 1)))
    copies = [pltpu.make_async_copy(gathered_hbm.at[at], ref, sems.at[i]) for i, (ref, _, at) in enumerate(sides)]
    for copy in copies:
        copy.start()
    near, leaves = list_ref.shape
    groups = leaves // LANES
    lane = lax.broadcasted_iota(jnp.int32, (near, LANES), 1)
    for g in range(groups):
        idx = 8 * (lane & 15) + 2 * g + (lane >> 6)
        part = (lane & 63) >> 4
        row = jnp.zeros((near, LANES), jnp.int32)
        for s in range(groups):
            row = jnp.where(part == s, lane_gather(list_ref[:, LANES * s : LANES * (s + 1)], idx), row)
        place_ref[g] = ((row >> 9) << 9) + ((row & 7) << 6) + ((row >> 3) & 63)
    for copy, (ref, inside, _) in zip(copies, sides):
        copy.wait()

        @pl.when(jnp.logical_not(inside))
        def _(ref=ref):
            ref[...] = jnp.zeros_like(ref)

    windows = (left_ref, own_ref, right_ref)
    rows = 4 * pts

    def step(i, carry):
        g = i // near
        n = i % near
        place = jnp.broadcast_to(place_ref[g, pl.ds(n, 1), :], (8, LANES))
        idx = place & (LANES - 1)
        group = place >> 7
        picked = [jnp.zeros((8, LANES), jnp.float32) for _ in range(rows // 8)]
        for s in range(3 * groups):
            here = group == s
            for r in range(rows // 8):
                source = windows[s // groups][8 * r : 8 * r + 8, LANES * (s % groups) : LANES * (s % groups + 1)]
                picked[r] = jnp.where(here, lane_gather(source, idx), picked[r])
        for r in range(rows // 8):
            picked_ref[8 * r : 8 * r + 8, :] = picked[r]
        at = pl.ds(pl.multiple_of(g * LANES, LANES), LANES)
        tx, ty, tz = (own_ref[pts * c : pts * (c + 1), at] for c in range(3))
        acc = jnp.where(n == 0, 0.0, pot_ref[g])
        for p in range(pts):
            sx, sy, sz, q = (picked_ref[pts * c + p : pts * c + p + 1, :] for c in range(4))
            dx, dy, dz = tx - sx, ty - sy, tz - sz
            acc += q * lax.rsqrt(dx * dx + dy * dy + (dz * dz + SOFT2))
        pot_ref[g] = acc
        return carry

    lax.fori_loop(0, groups * near, step, 0)
    half = LANES // 2
    pieces = []
    for g in range(groups):
        pot = pot_ref[g]
        pieces += [pot[:, :half], pot[:, half:]]
    out_ref[...] = jnp.concatenate(pieces, axis=0).T


def shards(
    coords,
    charges,
    multipoles,
    operators,
    send_list,
    near_list,
    m2l_source,
    m2l_target,
    m2l_operator,
):
    ncoef, leaves = multipoles.shape
    npoints = charges.shape[0]
    near = near_list.shape[1]
    entries = m2l_source.shape[1]
    ops = operators.shape[0]
    sources = send_list.shape[1]
    f32 = jnp.float32

    tiles = npoints // LANES
    coords3 = jnp.transpose(coords.reshape(3, tiles, LANES), (1, 0, 2))
    table, outgoing = pl.pallas_call(
        prep_kernel,
        name="prep",
        out_shape=(
            jax.ShapeDtypeStruct((64, leaves), f32),
            jax.ShapeDtypeStruct((sources, ncoef), f32),
        ),
        in_specs=[ANY] * 4,
        out_specs=(VMEM, VMEM),
        scratch_shapes=[
            pltpu.VMEM((tiles, 3, LANES), f32),
            pltpu.VMEM((tiles, LANES), f32),
            pltpu.VMEM((ncoef, leaves), f32),
            pltpu.VMEM((1, sources), jnp.int32),
            pltpu.SemaphoreType.DMA((4,)),
        ],
        compiler_params=WIDE,
    )(coords3, charges.reshape(tiles, LANES), multipoles, send_list)
    gathered = lax.all_gather(outgoing, "grp")
    window = lax.all_gather(table, "slab")

    nrows = ops // 2 * sources
    block = min(nrows, 512)
    low, high, flag = pl.pallas_call(
        functools.partial(count_kernel, sources=sources, leaves=leaves, chunk=512),
        name="counts",
        grid=(nrows // block,),
        out_shape=(
            jax.ShapeDtypeStruct((2, nrows, leaves), jnp.bfloat16),
            jax.ShapeDtypeStruct((2, nrows, leaves), jnp.bfloat16),
            jax.ShapeDtypeStruct((nrows // block, 1, 1), jnp.int32),
        ),
        in_specs=[pl.BlockSpec((1, entries), lambda i: (0, 0))] * 3,
        out_specs=(
            pl.BlockSpec((2, block, leaves), lambda i: (0, i, 0)),
            pl.BlockSpec((2, block, leaves), lambda i: (0, i, 0)),
            pl.BlockSpec((1, 1, 1), lambda i: (i, 0, 0), memory_space=pltpu.SMEM),
        ),
        scratch_shapes=[pltpu.VMEM((2, block, leaves), f32)],
        compiler_params=PARAMS,
    )(m2l_source, m2l_target, m2l_operator)

    local_exp = pl.pallas_call(
        functools.partial(far_kernel, ops=ops),
        name="far",
        out_shape=jax.ShapeDtypeStruct((ncoef, leaves), f32),
        in_specs=[pl.BlockSpec(memory_space=pltpu.SMEM), VMEM, ANY, VMEM, VMEM],
        out_specs=VMEM,
        scratch_shapes=[
            pltpu.VMEM((sources, ncoef), f32),
            pltpu.VMEM((sources // LANES, ncoef * ops, LANES), f32),
            pltpu.VMEM((2 * LANES, ops * sources), jnp.bfloat16),
            pltpu.SemaphoreType.DMA((gathered.shape[0],)),
        ],
        compiler_params=PARAMS,
    )(flag, jnp.transpose(operators, (1, 0, 2)).reshape(ncoef * ops, ncoef), gathered, low.reshape(ops * sources, leaves), high.reshape(ops * sources, leaves))

    near_potential = pl.pallas_call(
        near_kernel,
        name="near",
        out_shape=jax.ShapeDtypeStruct((tiles, LANES), f32),
        in_specs=[ANY, VMEM, VMEM],
        out_specs=VMEM,
        scratch_shapes=[
            pltpu.VMEM((64, leaves), f32),
            pltpu.VMEM((64, leaves), f32),
            pltpu.VMEM((64, LANES), f32),
            pltpu.VMEM((leaves // LANES, near, LANES), jnp.int32),
            pltpu.VMEM((leaves // LANES, 16, LANES), f32),
            pltpu.SemaphoreType.DMA((2,)),
        ],
        compiler_params=PARAMS,
    )(window, table, near_list.T)
    return (local_exp, near_potential.reshape(npoints))


def solution(mesh):
    both = ("slab", "grp")
    return jax.shard_map(
        shards,
        mesh=mesh,
        in_specs=(
            P(None, both),
            P(both),
            P(None, both),
            P(),
            P(both, None),
            P(both, None),
            P(both, None),
            P(both, None),
            P(both, None),
        ),
        out_specs=(P(None, both), P(both)),
        check_vma=False,
    )
```

```python
import functools

import jax
import jax.numpy as jnp
from jax import lax
from jax.experimental import pallas as pl
from jax.experimental.pallas import tpu as pltpu
from jax.sharding import PartitionSpec as P

SOFT2 = 0.0625
LANES = 128
PTS = 16
VMEM = pl.BlockSpec(memory_space=pltpu.VMEM)
ANY = pl.BlockSpec(memory_space=pl.ANY)
PARAMS = pltpu.CompilerParams(vmem_limit_bytes=48 * 1024 * 1024)
WIDE = pltpu.CompilerParams(vmem_limit_bytes=64 * 1024 * 1024)
NT = (((1,), (1,)), ((), ()))


def lane_gather(x, idx):
    return jnp.take_along_axis(x, idx, axis=1, mode="promise_in_bounds")


def split(x):
    hi = x.astype(jnp.bfloat16)
    return hi, (x - hi.astype(jnp.float32)).astype(jnp.bfloat16)


def pad_lanes(x):
    return jnp.concatenate([x, jnp.zeros((x.shape[0], LANES - x.shape[1]), x.dtype)], axis=1)


def prep_kernel(
    coords_hbm, charges_hbm, multipoles_hbm, send_hbm, table_ref, out_ref,
    coords_ref, charges_ref, multipoles_ref, send_ref, sems,
):
    pairs = (
        (coords_hbm, coords_ref),
        (charges_hbm, charges_ref),
        (send_hbm, send_ref),
        (multipoles_hbm, multipoles_ref),
    )
    copies = [pltpu.make_async_copy(src, dst, sems.at[i]) for i, (src, dst) in enumerate(pairs)]
    for copy in copies:
        copy.start()
    copies[0].wait()
    copies[1].wait()
    for c in range(4):
        rows = charges_ref[...] if c == 3 else coords_ref[:, c, :]
        cols = rows.T
        for pair in range(4):
            a = cols[32 * pair : 32 * pair + 16, :]
            b = cols[32 * pair + 16 : 32 * pair + 32, :]
            table_ref[16 * c : 16 * c + 16, LANES * pair : LANES * (pair + 1)] = jnp.concatenate([a, b], axis=1)
    copies[2].wait()
    copies[3].wait()
    ncoef, leaves = multipoles_ref.shape
    for sb in range(send_ref.shape[1] // LANES):
        send = send_ref[:, LANES * sb : LANES * (sb + 1)]
        lane = send & (LANES - 1)
        group = send >> 7
        idx = jnp.broadcast_to(lane, (ncoef, LANES))
        picked = jnp.zeros((ncoef, LANES), jnp.float32)
        for g in range(leaves // LANES):
            got = lane_gather(multipoles_ref[:, LANES * g : LANES * (g + 1)], idx)
            picked = jnp.where(group == g, got, picked)
        out_ref[LANES * sb : LANES * (sb + 1), :] = picked.T


def counts_kernel(
    source_ref, target_ref, operator_ref, operators_ref, low_ref, high_ref, flag_ref, parts_ref,
    acc_ref, wide_ref, *, sources, leaves, chunk, ops,
):
    nrows = acc_ref.shape[1]
    entries = source_ref.shape[1]
    base = pl.program_id(0) * nrows
    half = entries // 2
    for h in range(2):
        for k in range(half // chunk):
            at = pl.ds(h * half + k * chunk, chunk)
            op = operator_ref[:, at]
            code = (op >> 1) * sources + source_ref[:, at] - base
            weight = jnp.where((op & 1) == 1, 4096.0, 1.0)
            a = jnp.where(lax.broadcasted_iota(jnp.int32, (nrows, chunk), 0) == code, weight, 0.0).astype(jnp.bfloat16)
            b = jnp.where(
                lax.broadcasted_iota(jnp.int32, (leaves, chunk), 0) == target_ref[:, at], 1.0, 0.0
            ).astype(jnp.bfloat16)
            part = lax.dot_general(a, b, NT, preferred_element_type=jnp.float32)
            if k == 0:
                acc_ref[h] = part
            else:
                acc_ref[h] += part
    first, second = acc_ref[0], acc_ref[1]
    odd_first = jnp.floor(first * (1.0 / 4096.0))
    odd_second = jnp.floor(second * (1.0 / 4096.0))
    odd = odd_first + odd_second
    even = (first + second) - 4096.0 * odd
    top = jnp.zeros((), jnp.float32)
    for i, count in enumerate((even, odd)):
        high = 256.0 * jnp.floor(count * (1.0 / 256.0))
        low_ref[i] = (count - high).astype(jnp.bfloat16)
        high_ref[i] = high.astype(jnp.bfloat16)
        top = jnp.maximum(top, jnp.max(high))
    flag_ref[0, 0, 0] = (top > 0.0).astype(jnp.int32)

    @pl.when(pl.program_id(0) == 0)
    def _():
        ncoef = operators_ref.shape[1]
        wide_ref[...] = pad_lanes(operators_ref[...])
        for op in range(ops):
            row = ((op % 2) * (ops // 2) + op // 2) * LANES
            matrix = wide_ref[pl.ds(op, ncoef, stride=ops), :]
            matrix = jnp.concatenate([matrix, jnp.zeros((LANES - ncoef, LANES), jnp.float32)], axis=0)
            hi, lo = split(matrix)
            parts_ref[row : row + LANES, :LANES] = hi
            parts_ref[row : row + LANES, LANES:] = lo


def far_kernel(flag_ref, parts_ref, received_ref, low_ref, high_ref, out_ref, split_ref, *, ops):
    ncoef, leaves = out_ref.shape
    sources = received_ref.shape[0]
    hi, lo = split(pad_lanes(received_ref[...]))
    table = lax.dot_general(
        parts_ref[...], jnp.concatenate([hi, hi], axis=1), NT, preferred_element_type=jnp.float32
    ) + lax.dot_general(parts_ref[:, :LANES], lo, NT, preferred_element_type=jnp.float32)
    for k in range(ops):
        hi, lo = split(table[LANES * k : LANES * (k + 1), :])
        split_ref[:LANES, sources * k : sources * (k + 1)] = hi
        split_ref[LANES:, sources * k : sources * (k + 1)] = lo

    def product(counts_ref):
        both = jnp.dot(split_ref[...], counts_ref[...], preferred_element_type=jnp.float32)
        return both[:ncoef, :] + both[LANES : LANES + ncoef, :]

    out_ref[...] = product(low_ref)
    flagged = flag_ref[0, 0, 0]
    for i in range(1, flag_ref.shape[0]):
        flagged = flagged | flag_ref[i, 0, 0]

    @pl.when(flagged > 0)
    def _():
        out_ref[...] += product(high_ref)


def near_kernel(second_ref, own_ref, first_ref, list_ref, out_ref, picked_ref, place_ref, pot_ref):
    near, leaves = list_ref.shape
    groups = leaves // LANES
    even = lax.axis_index("slab") % 2 == 0
    lane = lax.broadcasted_iota(jnp.int32, (near, LANES), 1)
    for g in range(groups):
        idx = 8 * (lane & 15) + 2 * g + (lane >> 6)
        part = (lane & 63) >> 4
        row = jnp.zeros((near, LANES), jnp.int32)
        for s in range(groups):
            row = jnp.where(part == s, lane_gather(list_ref[:, LANES * s : LANES * (s + 1)], idx), row)
        block = row >> 9
        block = jnp.where(even, 2 - block, block)
        place_ref[g] = (block << 9) + ((row & 7) << 6) + ((row >> 3) & 63)
    windows = (first_ref, own_ref, second_ref)
    rows = 4 * PTS

    def step(g, carry):
        at = pl.ds(pl.multiple_of(g * LANES, LANES), LANES)
        tx, ty, tz = (own_ref[PTS * c : PTS * (c + 1), at] for c in range(3))
        acc = jnp.zeros((PTS, LANES), jnp.float32)
        for n in range(near):
            place = jnp.broadcast_to(place_ref[g, n : n + 1, :], (8, LANES))
            idx = place & (LANES - 1)
            group = place >> 7
            picked = [jnp.zeros((8, LANES), jnp.float32) for _ in range(rows // 8)]
            for s in range(3 * groups):
                here = group == s
                for r in range(rows // 8):
                    source = windows[s // groups][8 * r : 8 * r + 8, LANES * (s % groups) : LANES * (s % groups + 1)]
                    picked[r] = jnp.where(here, lane_gather(source, idx), picked[r])
            for r in range(rows // 8):
                picked_ref[n, 8 * r : 8 * r + 8, :] = picked[r]
            for p in range(PTS):
                sx, sy, sz, q = (picked_ref[n, PTS * c + p : PTS * c + p + 1, :] for c in range(4))
                dx, dy, dz = tx - sx, ty - sy, tz - sz
                acc += q * lax.rsqrt(dx * dx + dy * dy + (dz * dz + SOFT2))
        pot_ref[g] = acc
        return carry

    lax.fori_loop(0, groups, step, 0)
    half = LANES // 2
    pieces = []
    for g in range(groups):
        pot = pot_ref[g]
        pieces += [pot[:, :half], pot[:, half:]]
    out_ref[...] = jnp.concatenate(pieces, axis=0).T


def shards(
    coords,
    charges,
    multipoles,
    operators,
    send_list,
    near_list,
    m2l_source,
    m2l_target,
    m2l_operator,
):
    ncoef, leaves = multipoles.shape
    npoints = charges.shape[0]
    near = near_list.shape[1]
    entries = m2l_source.shape[1]
    ops = operators.shape[0]
    sources = send_list.shape[1]
    peers = lax.axis_size("grp")
    f32, bf16 = jnp.float32, jnp.bfloat16

    tiles = npoints // LANES
    coords3 = jnp.transpose(coords.reshape(3, tiles, LANES), (1, 0, 2))
    table, outgoing = pl.pallas_call(
        prep_kernel,
        name="prep",
        out_shape=(
            jax.ShapeDtypeStruct((4 * PTS, leaves), f32),
            jax.ShapeDtypeStruct((sources, ncoef), f32),
        ),
        in_specs=[ANY] * 4,
        out_specs=(VMEM, VMEM),
        scratch_shapes=[
            pltpu.VMEM((tiles, 3, LANES), f32),
            pltpu.VMEM((tiles, LANES), f32),
            pltpu.VMEM((ncoef, leaves), f32),
            pltpu.VMEM((1, sources), jnp.int32),
            pltpu.SemaphoreType.DMA((4,)),
        ],
        compiler_params=WIDE,
    )(coords3, charges.reshape(tiles, LANES), multipoles, send_list)
    received = lax.all_to_all(
        outgoing.reshape(peers, sources // peers, ncoef), "grp", split_axis=0, concat_axis=0, tiled=True
    ).reshape(sources, ncoef)
    slabs = lax.axis_size("slab")

    def exchange(start):
        ties = [(i, i + 1) for i in range(start, slabs - 1, 2)]
        return lax.ppermute(table, "slab", ties + [(b, a) for a, b in ties])

    first = exchange(0)
    second = exchange(1)

    nrows = ops // 2 * sources
    block = min(nrows, 512)
    low, high, flag, parts = pl.pallas_call(
        functools.partial(counts_kernel, sources=sources, leaves=leaves, chunk=512, ops=ops),
        name="counts",
        grid=(nrows // block,),
        out_shape=(
            jax.ShapeDtypeStruct((2, nrows, leaves), bf16),
            jax.ShapeDtypeStruct((2, nrows, leaves), bf16),
            jax.ShapeDtypeStruct((nrows // block, 1, 1), jnp.int32),
            jax.ShapeDtypeStruct((ops * LANES, 2 * LANES), bf16),
        ),
        in_specs=[pl.BlockSpec((1, entries), lambda i: (0, 0))] * 3
        + [pl.BlockSpec((ncoef * ops, ncoef), lambda i: (0, 0))],
        out_specs=(
            pl.BlockSpec((2, block, leaves), lambda i: (0, i, 0)),
            pl.BlockSpec((2, block, leaves), lambda i: (0, i, 0)),
            pl.BlockSpec((1, 1, 1), lambda i: (i, 0, 0), memory_space=pltpu.SMEM),
            pl.BlockSpec((ops * LANES, 2 * LANES), lambda i: (0, 0)),
        ),
        scratch_shapes=[pltpu.VMEM((2, block, leaves), f32), pltpu.VMEM((ncoef * ops, LANES), f32)],
        compiler_params=PARAMS,
    )(m2l_source, m2l_target, m2l_operator, jnp.transpose(operators, (1, 0, 2)).reshape(ncoef * ops, ncoef))

    local_exp = pl.pallas_call(
        functools.partial(far_kernel, ops=ops),
        name="far",
        out_shape=jax.ShapeDtypeStruct((ncoef, leaves), f32),
        in_specs=[pl.BlockSpec(memory_space=pltpu.SMEM)] + [VMEM] * 4,
        out_specs=VMEM,
        scratch_shapes=[pltpu.VMEM((2 * LANES, ops * sources), bf16)],
        compiler_params=PARAMS,
    )(flag, parts, received, low.reshape(ops * sources, leaves), high.reshape(ops * sources, leaves))

    near_potential = pl.pallas_call(
        near_kernel,
        name="near",
        out_shape=jax.ShapeDtypeStruct((tiles, LANES), f32),
        in_specs=[VMEM] * 4,
        out_specs=VMEM,
        scratch_shapes=[
            pltpu.VMEM((near, 4 * PTS, LANES), f32),
            pltpu.VMEM((leaves // LANES, near, LANES), jnp.int32),
            pltpu.VMEM((leaves // LANES, PTS, LANES), f32),
        ],
        compiler_params=PARAMS,
    )(second, table, first, near_list.T)
    return (local_exp, near_potential.reshape(npoints))


def solution(mesh):
    both = ("slab", "grp")
    return jax.shard_map(
        shards,
        mesh=mesh,
        in_specs=(
            P(None, both),
            P(both),
            P(None, both),
            P(),
            P(both, None),
            P(both, None),
            P(both, None),
            P(both, None),
            P(both, None),
        ),
        out_specs=(P(None, both), P(both)),
        check_vma=False,
    )
```

```python
import functools

import jax
import jax.numpy as jnp
from jax import lax
from jax.experimental import pallas as pl
from jax.experimental.pallas import tpu as pltpu
from jax.sharding import PartitionSpec as P

SOFT2 = 0.0625
LANES = 128
PTS = 16
SCALE = 2.0**20
MARK = jnp.bfloat16
VMEM = pl.BlockSpec(memory_space=pltpu.VMEM)
ANY = pl.BlockSpec(memory_space=pl.ANY)
PARAMS = pltpu.CompilerParams(vmem_limit_bytes=24 * 1024 * 1024)
NT = (((1,), (1,)), ((), ()))


def lane_gather(x, idx):
    return jnp.take_along_axis(x, idx, axis=1, mode="promise_in_bounds")


def split(x):
    hi = x.astype(jnp.bfloat16)
    return hi, (x - hi.astype(jnp.float32)).astype(jnp.bfloat16)


def pad_lanes(x):
    return jnp.concatenate([x, jnp.zeros((x.shape[0], LANES - x.shape[1]), x.dtype)], axis=1)


def prep_kernel(coords_hbm, charges_hbm, multipoles_hbm, send_hbm, *refs, others):
    sources, refs = refs[:others], refs[others:]
    (table_ref, table_hbm, out_ref, *targets), refs = refs[: others + 3], refs[others + 3 :]
    coords_ref, charges_ref, multipoles_ref, send_ref, sems = refs
    pairs = (
        (coords_hbm, coords_ref),
        (charges_hbm, charges_ref),
        (send_hbm, send_ref),
        (multipoles_hbm, multipoles_ref),
        *zip(sources, targets),
    )
    copies = [pltpu.make_async_copy(src, dst, sems.at[i]) for i, (src, dst) in enumerate(pairs)]
    for copy in copies:
        copy.start()
    copies[0].wait()
    copies[1].wait()
    for c in range(4):
        rows = charges_ref[...] if c == 3 else coords_ref[:, c, :]
        cols = rows.T
        for pair in range(4):
            a = cols[32 * pair : 32 * pair + 16, :]
            b = cols[32 * pair + 16 : 32 * pair + 32, :]
            table_ref[16 * c : 16 * c + 16, LANES * pair : LANES * (pair + 1)] = jnp.concatenate([a, b], axis=1)
    whole = pltpu.make_async_copy(table_ref, table_hbm, sems.at[len(copies)])
    whole.start()
    copies[2].wait()
    copies[3].wait()
    ncoef, leaves = multipoles_ref.shape
    for sb in range(send_ref.shape[1] // LANES):
        send = send_ref[:, LANES * sb : LANES * (sb + 1)]
        lane = send & (LANES - 1)
        group = send >> 7
        idx = jnp.broadcast_to(lane, (ncoef, LANES))
        picked = jnp.zeros((ncoef, LANES), jnp.float32)
        for g in range(leaves // LANES):
            got = lane_gather(multipoles_ref[:, LANES * g : LANES * (g + 1)], idx)
            picked = jnp.where(group == g, got, picked)
        out_ref[LANES * sb : LANES * (sb + 1), :] = picked.T
    for copy in copies[4:]:
        copy.wait()
    whole.wait()


def decode(acc):
    odd = jnp.floor(acc * (1.0 / 8192.0))
    return acc - 8192.0 * odd, odd + 2048.0


def near_kernel(
    second_ref, own_ref, first_ref, list_ref, source_ref, target_ref, operator_ref, operators_ref,
    near_ref, low_ref, acc_ref, peak_ref, parts_ref,
    packed_ref, picked_ref, place_ref, pot_ref, wide_ref, a_ref, b_ref, *, ops, sources,
):
    near, leaves = list_ref.shape
    ncoef = operators_ref.shape[1]
    nrows = acc_ref.shape[0]
    block, chunk = a_ref.shape
    groups = leaves // LANES
    each = ops // groups
    f32, bf16 = jnp.float32, jnp.bfloat16
    even = lax.axis_index("slab") % 2 == 0
    lane = lax.broadcasted_iota(jnp.int32, (near, LANES), 1)
    for g in range(groups):
        idx = 8 * (lane & 15) + 2 * g + (lane >> 6)
        part = (lane & 63) >> 4
        row = jnp.zeros((near, LANES), jnp.int32)
        for s in range(groups):
            row = jnp.where(part == s, lane_gather(list_ref[:, LANES * s : LANES * (s + 1)], idx), row)
        side = row >> 9
        side = jnp.where(even, 2 - side, side)
        place_ref[g] = (side << 9) + ((row & 7) << 6) + ((row >> 3) & 63)
    wide_ref[...] = pad_lanes(operators_ref[...])
    acc_ref[...] = jnp.full(acc_ref.shape, -(2.0**24), f32)
    iota = lax.broadcasted_iota(jnp.int32, (max(block, leaves), LANES), 0).astype(jnp.int16).reshape(-1, 16, LANES)
    zero = jnp.zeros((1, 16, LANES), bf16)
    one = jnp.ones((1, 16, LANES), bf16)

    def spread(row, dtype):
        return jnp.broadcast_to(row, (16, LANES)).astype(dtype)[None]

    def columns(ref, g, c):
        return ref[:, pl.ds(pl.multiple_of(g * chunk + c * LANES, LANES), LANES)]

    def mark_codes(g, k):
        for c in range(chunk // LANES):
            op = columns(operator_ref, g, c)
            code = spread((op >> 1) * sources + columns(source_ref, g, c) - block * k, jnp.int16)
            weight = spread(jnp.where((op & 1) == 1, 8192.0, 1.0), bf16)
            marks = jnp.where(iota[: block // 16] == code, weight, zero).reshape(block, LANES)
            a_ref[:, LANES * c : LANES * (c + 1)] = marks.astype(MARK)

    def mark_leaves(g, h):
        size = leaves // 2
        for c in range(chunk // LANES):
            leaf = spread(columns(target_ref, g, c) - size * h, jnp.int16)
            marks = jnp.where(iota[: size // 16] == leaf, one, zero).reshape(size, LANES)
            b_ref[size * h : size * (h + 1), LANES * c : LANES * (c + 1)] = marks.astype(MARK)

    def count(k, h):
        to = (slice(block * k, block * (k + 1)), slice(leaves // 2 * h, leaves // 2 * (h + 1)))
        acc_ref[to] += lax.dot_general(a_ref[...], b_ref[to[1], :], NT, preferred_element_type=f32)

    def cut(g):
        for j in range(each):
            place = each * g + j
            op = 2 * lax.rem(place, ops // 2) + lax.div(place, ops // 2)
            matrix = wide_ref[pl.ds(op, ncoef, stride=ops), :]
            matrix = jnp.concatenate([matrix, jnp.zeros((LANES - ncoef, LANES), f32)], axis=0)
            hi, lo = split(matrix)
            parts_ref[pl.ds(pl.multiple_of(place * LANES, LANES), LANES), :] = jnp.concatenate([hi, lo], axis=1)

    for g in range(groups):
        cut(g)
    for k, ref in enumerate((first_ref, own_ref, second_ref)):
        x, y, z = (
            jnp.clip(jnp.floor(ref[PTS * c : PTS * (c + 1), :] * SCALE + 0.5), -SCALE, SCALE - 1.0).astype(jnp.int32)
            for c in range(3)
        )
        packed_ref[:PTS, leaves * k : leaves * (k + 1)] = (x << 11) | ((y >> 10) & 2047)
        packed_ref[PTS:, leaves * k : leaves * (k + 1)] = (z << 11) | (y & 1023)

    def gather(place):
        idx = place & (LANES - 1)
        group = place >> 7
        words = [jnp.zeros((8, LANES), jnp.int32) for _ in range(2 * PTS // 8)]
        charge = [jnp.zeros((8, LANES), f32) for _ in range(PTS // 8)]
        for s in range(3 * groups):
            here = group == s
            window = (first_ref, own_ref, second_ref)[s // groups]
            at = slice(LANES * (s % groups), LANES * (s % groups + 1))
            for r in range(2 * PTS // 8):
                got = lane_gather(packed_ref[8 * r : 8 * r + 8, LANES * s : LANES * (s + 1)], idx)
                words[r] = jnp.where(here, got, words[r])
            for r in range(PTS // 8):
                got = lane_gather(window[3 * PTS + 8 * r : 3 * PTS + 8 * r + 8, at], idx)
                charge[r] = jnp.where(here, got, charge[r])
        return words, charge

    def step(g, carry):
        for k in range(1, nrows // block):
            mark_codes(g, k)
            for h in range(2):
                mark_leaves(g, h)
                count(k, h)
        mark_codes(g, 0)
        at = pl.ds(pl.multiple_of(g * LANES, LANES), LANES)
        tx, ty, tz = (own_ref[PTS * c : PTS * (c + 1), at] * SCALE for c in range(3))
        square = tx * tx + ty * ty + (tz * tz + SOFT2 * SCALE * SCALE)
        tx, ty, tz = -2.0 * tx, -2.0 * ty, -2.0 * tz
        acc = jnp.zeros((PTS, LANES), f32)
        for n in range(near):
            if n % (near // 2) == 0:
                mark_leaves(g, n // (near // 2))
                count(0, n // (near // 2))
            words, charge = gather(jnp.broadcast_to(place_ref[g, n : n + 1, :], (8, LANES)))
            for r in range(PTS // 8):
                first, second = words[r], words[PTS // 8 + r]
                x = (first >> 11).astype(f32)
                y = (((first << 21) >> 11) | (second & 1023)).astype(f32)
                z = (second >> 11).astype(f32)
                for k, row in enumerate((x, y, z, charge[r], x * x + y * y + z * z)):
                    picked_ref[n, PTS * k + 8 * r : PTS * k + 8 * r + 8, :] = row
            for p in range(PTS):
                sx, sy, sz, q, far = (picked_ref[n, PTS * c + p : PTS * c + p + 1, :] for c in range(5))
                acc += q * lax.rsqrt((square + far) + tx * sx + (ty * sy + tz * sz))
        pot_ref[g] = acc * SCALE
        return carry

    lax.fori_loop(0, groups, step, 0)
    half = LANES // 2
    pieces = []
    for g in range(groups):
        pot = pot_ref[g]
        pieces += [pot[:, :half], pot[:, half:]]
    near_ref[...] = jnp.concatenate(pieces, axis=0).T
    count_even, count_odd = decode(acc_ref[...])
    low_ref[:nrows, :] = count_even.astype(bf16)
    low_ref[nrows:, :] = count_odd.astype(bf16)
    peak_ref[...] = jnp.max(jnp.maximum(count_even, count_odd).reshape(-1, 8, leaves), axis=0)


def far_kernel(peak_ref, parts_ref, received_ref, low_ref, acc_ref, out_ref, split_ref, *, ops):
    ncoef, leaves = out_ref.shape
    sources = received_ref.shape[0]
    nrows = acc_ref.shape[0]
    hi, lo = split(pad_lanes(received_ref[...]))
    table = lax.dot_general(
        parts_ref[...], jnp.concatenate([hi, hi], axis=1), NT, preferred_element_type=jnp.float32
    ) + lax.dot_general(parts_ref[:, :LANES], lo, NT, preferred_element_type=jnp.float32)
    for k in range(ops):
        hi, lo = split(table[LANES * k : LANES * (k + 1), :])
        split_ref[:LANES, sources * k : sources * (k + 1)] = hi
        split_ref[LANES:, sources * k : sources * (k + 1)] = lo
    both = jnp.dot(split_ref[...], low_ref[...], preferred_element_type=jnp.float32)
    out_ref[...] = both[:ncoef, :] + both[LANES : LANES + ncoef, :]

    @pl.when(jnp.max(peak_ref[...]) > 256.0)
    def _():
        for i, counts in enumerate(decode(acc_ref[...])):
            at = slice(nrows * i, nrows * (i + 1))
            missing = (counts - low_ref[at, :].astype(jnp.float32)).astype(jnp.bfloat16)
            both = jnp.dot(split_ref[:, at], missing, preferred_element_type=jnp.float32)
            out_ref[...] += both[:ncoef, :] + both[LANES : LANES + ncoef, :]


def shards(
    coords,
    charges,
    multipoles,
    operators,
    send_list,
    near_list,
    m2l_source,
    m2l_target,
    m2l_operator,
):
    ncoef, leaves = multipoles.shape
    npoints = charges.shape[0]
    near = near_list.shape[1]
    entries = m2l_source.shape[1]
    ops = operators.shape[0]
    sources = send_list.shape[1]
    peers = lax.axis_size("grp")
    f32, bf16 = jnp.float32, jnp.bfloat16

    tiles = npoints // LANES
    points = (jnp.transpose(coords.reshape(3, tiles, LANES), (1, 0, 2)), charges.reshape(tiles, LANES))
    others = (
        near_list.T,
        m2l_source,
        m2l_target,
        m2l_operator,
        jnp.transpose(operators, (1, 0, 2)).reshape(ncoef * ops, ncoef),
    )
    table, sent, outgoing, near_list, m2l_source, m2l_target, m2l_operator, operators = pl.pallas_call(
        functools.partial(prep_kernel, others=len(others)),
        name="prep",
        out_shape=(
            pltpu.VMEM((4 * PTS, leaves), f32),
            pltpu.HBM((4 * PTS, leaves), f32),
            pltpu.VMEM((sources, ncoef), f32),
            *(pltpu.VMEM(x.shape, x.dtype) for x in others),
        ),
        in_specs=[ANY] * (4 + len(others)),
        out_specs=(VMEM, ANY, VMEM) + (VMEM,) * len(others),
        scratch_shapes=[
            pltpu.VMEM((tiles, 3, LANES), f32),
            pltpu.VMEM((tiles, LANES), f32),
            pltpu.VMEM((ncoef, leaves), f32),
            pltpu.VMEM((1, sources), jnp.int32),
            pltpu.SemaphoreType.DMA((5 + len(others),)),
        ],
        compiler_params=PARAMS,
    )(*(pltpu.with_memory_space_constraint(x, pltpu.HBM) for x in (*points, multipoles, send_list, *others)))
    received = lax.all_to_all(
        outgoing.reshape(peers, sources // peers, ncoef), "grp", split_axis=0, concat_axis=0, tiled=True
    ).reshape(sources, ncoef)
    slabs = lax.axis_size("slab")

    def exchange(start):
        ties = [(i, i + 1) for i in range(start, slabs - 1, 2)]
        return lax.ppermute(sent, "slab", ties + [(b, a) for a, b in ties])

    first = exchange(0)
    second = exchange(1)

    nrows = ops // 2 * sources
    block = min(nrows, 512)
    groups = leaves // LANES
    chunk = entries // groups
    near_potential, low, acc, peak, parts = pl.pallas_call(
        functools.partial(near_kernel, ops=ops, sources=sources),
        name="near_counts",
        out_shape=(
            jax.ShapeDtypeStruct((tiles, LANES), f32),
            pltpu.VMEM((2 * nrows, leaves), bf16),
            pltpu.VMEM((nrows, leaves), f32),
            pltpu.VMEM((8, leaves), f32),
            pltpu.VMEM((ops * LANES, 2 * LANES), bf16),
        ),
        in_specs=[VMEM] * 8,
        out_specs=(VMEM,) * 5,
        scratch_shapes=[
            pltpu.VMEM((2 * PTS, 3 * leaves), jnp.int32),
            pltpu.VMEM((near, 5 * PTS, LANES), f32),
            pltpu.VMEM((groups, near, LANES), jnp.int32),
            pltpu.VMEM((groups, PTS, LANES), f32),
            pltpu.VMEM((ncoef * ops, LANES), f32),
            pltpu.VMEM((block, chunk), MARK),
            pltpu.VMEM((leaves, chunk), MARK),
        ],
        compiler_params=PARAMS,
    )(second, table, first, near_list, m2l_source, m2l_target, m2l_operator, operators)

    local_exp = pl.pallas_call(
        functools.partial(far_kernel, ops=ops),
        name="far",
        out_shape=jax.ShapeDtypeStruct((ncoef, leaves), f32),
        in_specs=[VMEM] * 5,
        out_specs=VMEM,
        scratch_shapes=[pltpu.VMEM((2 * LANES, ops * sources), bf16)],
        compiler_params=PARAMS,
    )(peak, parts, received, low, acc)
    return (local_exp, near_potential.reshape(npoints))


def solution(mesh):
    both = ("slab", "grp")
    return jax.shard_map(
        shards,
        mesh=mesh,
        in_specs=(
            P(None, both),
            P(both),
            P(None, both),
            P(),
            P(both, None),
            P(both, None),
            P(both, None),
            P(both, None),
            P(both, None),
        ),
        out_specs=(P(None, both), P(both)),
        check_vma=False,
    )
```

```python
import functools

import jax
import jax.numpy as jnp
from jax import lax
from jax.experimental import pallas as pl
from jax.experimental.pallas import tpu as pltpu
from jax.sharding import PartitionSpec as P

SOFT2 = 0.0625
LANES = 128
PTS = 16
SCALE = 2.0**20
VMEM = pl.BlockSpec(memory_space=pltpu.VMEM)
ANY = pl.BlockSpec(memory_space=pl.ANY)
PARAMS = pltpu.CompilerParams(vmem_limit_bytes=48 * 1024 * 1024)
NT = (((1,), (1,)), ((), ()))


def lane_gather(x, idx):
    return jnp.take_along_axis(x, idx, axis=1, mode="promise_in_bounds")


def split(x):
    hi = x.astype(jnp.bfloat16)
    return hi, (x - hi.astype(jnp.float32)).astype(jnp.bfloat16)


def pad_lanes(x):
    return jnp.concatenate([x, jnp.zeros((x.shape[0], LANES - x.shape[1]), x.dtype)], axis=1)


def prep_kernel(coords_hbm, charges_hbm, multipoles_hbm, send_hbm, *refs, others):
    sources, refs = refs[:others], refs[others:]
    (table_ref, out_ref, *targets), refs = refs[: others + 2], refs[others + 2 :]
    coords_ref, charges_ref, multipoles_ref, send_ref, sems = refs
    pairs = (
        (coords_hbm, coords_ref),
        (charges_hbm, charges_ref),
        (send_hbm, send_ref),
        (multipoles_hbm, multipoles_ref),
        *zip(sources, targets),
    )
    copies = [pltpu.make_async_copy(src, dst, sems.at[i]) for i, (src, dst) in enumerate(pairs)]
    for copy in copies:
        copy.start()
    copies[0].wait()
    copies[1].wait()
    for c in range(4):
        rows = charges_ref[...] if c == 3 else coords_ref[:, c, :]
        cols = rows.T
        for pair in range(4):
            a = cols[32 * pair : 32 * pair + 16, :]
            b = cols[32 * pair + 16 : 32 * pair + 32, :]
            table_ref[16 * c : 16 * c + 16, LANES * pair : LANES * (pair + 1)] = jnp.concatenate([a, b], axis=1)
    copies[2].wait()
    copies[3].wait()
    ncoef, leaves = multipoles_ref.shape
    for sb in range(send_ref.shape[1] // LANES):
        send = send_ref[:, LANES * sb : LANES * (sb + 1)]
        lane = send & (LANES - 1)
        group = send >> 7
        idx = jnp.broadcast_to(lane, (ncoef, LANES))
        picked = jnp.zeros((ncoef, LANES), jnp.float32)
        for g in range(leaves // LANES):
            got = lane_gather(multipoles_ref[:, LANES * g : LANES * (g + 1)], idx)
            picked = jnp.where(group == g, got, picked)
        out_ref[LANES * sb : LANES * (sb + 1), :] = picked.T
    for copy in copies[4:]:
        copy.wait()


def cut_kernel(list_ref, operators_ref, place_ref, parts_ref, wide_ref, *, ops):
    near, leaves = list_ref.shape
    ncoef = operators_ref.shape[1]
    groups = leaves // LANES
    even = lax.axis_index("slab") % 2 == 0
    lane = lax.broadcasted_iota(jnp.int32, (near, LANES), 1)
    for g in range(groups):
        idx = 8 * (lane & 15) + 2 * g + (lane >> 6)
        part = (lane & 63) >> 4
        row = jnp.zeros((near, LANES), jnp.int32)
        for s in range(groups):
            row = jnp.where(part == s, lane_gather(list_ref[:, LANES * s : LANES * (s + 1)], idx), row)
        side = row >> 9
        side = jnp.where(even, 2 - side, side)
        place_ref[g] = (side << 9) + ((row & 7) << 6) + ((row >> 3) & 63)
    wide_ref[...] = pad_lanes(operators_ref[...])
    for op in range(ops):
        matrix = wide_ref[pl.ds(op, ncoef, stride=ops), :]
        matrix = jnp.concatenate([matrix, jnp.zeros((LANES - ncoef, LANES), jnp.float32)], axis=0)
        hi, lo = split(matrix)
        parts_ref[LANES * spot(op, ops) : LANES * (spot(op, ops) + 1), :] = jnp.concatenate([hi, lo], axis=1)


def spot(op, ops):
    return (op % 4) * (ops // 4) + op // 4


def near_kernel(
    second_ref, own_ref, first_ref, place_ref, source_ref, target_ref, operator_ref,
    near_ref, low_ref, rest_ref, inexact_ref,
    packed_ref, picked_ref, pot_ref, acc_ref, pair_ref, a_ref, b_ref, *, ops, sources,
):
    groups, near, _ = place_ref.shape
    leaves = own_ref.shape[1]
    block, chunk = a_ref.shape
    codes = acc_ref.shape[1]
    f32, bf16 = jnp.float32, jnp.bfloat16
    iota = lax.broadcasted_iota(jnp.int32, (max(block, leaves), LANES), 0).astype(jnp.int16).reshape(-1, 16, LANES)
    zero = jnp.zeros((1, 16, LANES), bf16)
    one = jnp.ones((1, 16, LANES), bf16)

    def spread(row, dtype):
        return jnp.broadcast_to(row, (16, LANES)).astype(dtype)[None]

    def columns(ref, g, c):
        return ref[:, pl.ds(pl.multiple_of(g * chunk + c * LANES, LANES), LANES)]

    def mark_leaves(g):
        for c in range(chunk // LANES):
            leaf = spread(columns(target_ref, g, c), jnp.int16)
            marks = jnp.where(iota[: leaves // 16] == leaf, one, zero).reshape(leaves, LANES)
            b_ref[:, LANES * c : LANES * (c + 1)] = marks

    def mark_codes(g, first, size, shift, weigh):
        for c in range(chunk // LANES):
            op = columns(operator_ref, g, c)
            code = spread((op >> shift) * sources + columns(source_ref, g, c) - first, jnp.int16)
            marks = jnp.where(iota[: size // 16] == code, spread(weigh(op), bf16), zero).reshape(size, LANES)
            a_ref[:size, LANES * c : LANES * (c + 1)] = marks

    def products(size):
        return lax.dot_general(b_ref[...], a_ref[:size, :], NT, preferred_element_type=f32)

    def digit_weight(op):
        last = op & 3
        return jnp.where(last == 0, 1.0, jnp.where(last == 1, 64.0, jnp.where(last == 2, 4096.0, 2.0**18)))

    def count(g):
        mark_leaves(g)
        for first in range(0, codes, block):
            size = min(block, codes - first)
            mark_codes(g, first, size, 2, digit_weight)
            acc_ref[:, first : first + size] += products(size)

    acc_ref[...] = jnp.zeros_like(acc_ref)
    for k, ref in enumerate((first_ref, own_ref, second_ref)):
        x, y, z = (
            jnp.clip(jnp.floor(ref[PTS * c : PTS * (c + 1), :] * SCALE + 0.5), -SCALE, SCALE - 1.0).astype(jnp.int32)
            for c in range(3)
        )
        packed_ref[:PTS, leaves * k : leaves * (k + 1)] = (x << 11) | ((y >> 10) & 2047)
        packed_ref[PTS:, leaves * k : leaves * (k + 1)] = (z << 11) | (y & 1023)

    def gather(place):
        idx = place & (LANES - 1)
        group = place >> 7
        words = [jnp.zeros((8, LANES), jnp.int32) for _ in range(2 * PTS // 8)]
        charge = [jnp.zeros((8, LANES), f32) for _ in range(PTS // 8)]
        for s in range(3 * groups):
            here = group == s
            window = (first_ref, own_ref, second_ref)[s // groups]
            at = slice(LANES * (s % groups), LANES * (s % groups + 1))
            for r in range(2 * PTS // 8):
                got = lane_gather(packed_ref[8 * r : 8 * r + 8, LANES * s : LANES * (s + 1)], idx)
                words[r] = jnp.where(here, got, words[r])
            for r in range(PTS // 8):
                got = lane_gather(window[3 * PTS + 8 * r : 3 * PTS + 8 * r + 8, at], idx)
                charge[r] = jnp.where(here, got, charge[r])
        return words, charge

    def step(g, carry):
        count(g)
        at = pl.ds(pl.multiple_of(g * LANES, LANES), LANES)
        tx, ty, tz = (own_ref[PTS * c : PTS * (c + 1), at] * SCALE for c in range(3))
        square = tx * tx + ty * ty + (tz * tz + SOFT2 * SCALE * SCALE)
        tx, ty, tz = -2.0 * tx, -2.0 * ty, -2.0 * tz
        acc = jnp.zeros((PTS, LANES), f32)
        for n in range(near):
            words, charge = gather(jnp.broadcast_to(place_ref[g, n : n + 1, :], (8, LANES)))
            for r in range(PTS // 8):
                first, second = words[r], words[PTS // 8 + r]
                x = (first >> 11).astype(f32)
                y = (((first << 21) >> 11) | (second & 1023)).astype(f32)
                z = (second >> 11).astype(f32)
                for k, row in enumerate((x, y, z, charge[r], x * x + y * y + z * z)):
                    picked_ref[n, PTS * k + 8 * r : PTS * k + 8 * r + 8, :] = row
            for p in range(PTS):
                sx, sy, sz, q, far = (picked_ref[n, PTS * c + p : PTS * c + p + 1, :] for c in range(5))
                acc += q * lax.rsqrt((square + far) + tx * sx + (ty * sy + tz * sz))
        pot_ref[g] = acc * SCALE
        return carry

    lax.fori_loop(0, groups, step, 0)
    half = LANES // 2
    pieces = []
    for g in range(groups):
        pot = pot_ref[g]
        pieces += [pot[:, :half], pot[:, half:]]
    near_ref[...] = jnp.concatenate(pieces, axis=0).T

    value = acc_ref[...]
    total = jnp.zeros_like(value)
    left = value
    for digit in range(4):
        above = jnp.floor(left * (1.0 / 64.0))
        here = left - 64.0 * above
        low_ref[:, codes * digit : codes * (digit + 1)] = here.astype(bf16)
        total += here
        left = above
    total = jnp.where(value < 2.0**24, total, -(2.0**30))
    used = jnp.sum(jnp.where(target_ref[...] < leaves, 1.0, 0.0))
    carried = jnp.sum(total) != used
    inexact_ref[...] = jnp.zeros_like(inexact_ref)

    @pl.when(carried)
    def _():
        pairs = ops // 2 * sources
        for first in range(0, pairs, block):
            size = min(block, pairs - first)
            pair_ref[:, :size] = jnp.full((leaves, size), -(2.0**24), f32)

            def more(g, carry):
                mark_leaves(g)
                mark_codes(g, first, size, 1, lambda op: jnp.where((op & 1) == 1, 8192.0, 1.0))
                pair_ref[:, :size] += products(size)
                return carry

            lax.fori_loop(0, groups, more, 0)
            for lane in range(first, first + size, LANES):
                value = pair_ref[:, lane - first : lane - first + LANES]
                odd = jnp.floor(value * (1.0 / 8192.0))
                for parity, count in enumerate((value - 8192.0 * odd, odd + 2048.0)):
                    to = spot(2 * (lane // sources) + parity, ops) * sources + lane % sources
                    kept = count.astype(bf16)
                    low_ref[:, to : to + LANES] = kept
                    rest_ref[:, to : to + LANES] = (count - kept.astype(f32)).astype(bf16)
        inexact_ref[...] = jnp.ones_like(inexact_ref)


def far_kernel(inexact_ref, parts_ref, received_ref, low_ref, rest_ref, out_ref, split_ref, *, ops):
    ncoef, leaves = out_ref.shape
    sources = received_ref.shape[0]
    hi, lo = split(pad_lanes(received_ref[...]))
    table = lax.dot_general(
        parts_ref[...], jnp.concatenate([hi, hi], axis=1), NT, preferred_element_type=jnp.float32
    ) + lax.dot_general(parts_ref[:, :LANES], lo, NT, preferred_element_type=jnp.float32)
    for k in range(ops):
        hi, lo = split(table[LANES * k : LANES * (k + 1), :])
        split_ref[:LANES, sources * k : sources * (k + 1)] = hi
        split_ref[LANES:, sources * k : sources * (k + 1)] = lo

    def product(counts):
        both = lax.dot_general(split_ref[...], counts, NT, preferred_element_type=jnp.float32)
        return both[:ncoef, :] + both[LANES : LANES + ncoef, :]

    out_ref[...] = product(low_ref[...])

    @pl.when(jnp.max(inexact_ref[...]) > 0.0)
    def _():
        out_ref[...] += product(rest_ref[...])


def shards(
    coords,
    charges,
    multipoles,
    operators,
    send_list,
    near_list,
    m2l_source,
    m2l_target,
    m2l_operator,
):
    ncoef, leaves = multipoles.shape
    npoints = charges.shape[0]
    near = near_list.shape[1]
    entries = m2l_source.shape[1]
    ops = operators.shape[0]
    sources = send_list.shape[1]
    peers = lax.axis_size("grp")
    f32, bf16 = jnp.float32, jnp.bfloat16

    tiles = npoints // LANES
    points = (jnp.transpose(coords.reshape(3, tiles, LANES), (1, 0, 2)), charges.reshape(tiles, LANES))
    others = (
        near_list.T,
        m2l_source,
        m2l_target,
        m2l_operator,
        jnp.transpose(operators, (1, 0, 2)).reshape(ncoef * ops, ncoef),
    )
    table, outgoing, near_list, m2l_source, m2l_target, m2l_operator, operators = pl.pallas_call(
        functools.partial(prep_kernel, others=len(others)),
        name="prep",
        out_shape=(
            pltpu.VMEM((4 * PTS, leaves), f32),
            pltpu.VMEM((sources, ncoef), f32),
            *(pltpu.VMEM(x.shape, x.dtype) for x in others),
        ),
        in_specs=[ANY] * (4 + len(others)),
        out_specs=(VMEM,) * (2 + len(others)),
        scratch_shapes=[
            pltpu.VMEM((tiles, 3, LANES), f32),
            pltpu.VMEM((tiles, LANES), f32),
            pltpu.VMEM((ncoef, leaves), f32),
            pltpu.VMEM((1, sources), jnp.int32),
            pltpu.SemaphoreType.DMA((4 + len(others),)),
        ],
        compiler_params=PARAMS,
    )(*(pltpu.with_memory_space_constraint(x, pltpu.HBM) for x in (*points, multipoles, send_list, *others)))
    received = lax.all_to_all(
        outgoing.reshape(peers, sources // peers, ncoef), "grp", split_axis=0, concat_axis=0, tiled=True
    ).reshape(sources, ncoef)
    slabs = lax.axis_size("slab")

    def exchange(start):
        ties = [(i, i + 1) for i in range(start, slabs - 1, 2)]
        return lax.ppermute(table, "slab", ties + [(b, a) for a, b in ties])

    first = exchange(0)
    second = exchange(1)

    codes = ops // 4 * sources
    block = min(2 * codes, 512)
    groups = leaves // LANES
    chunk = entries // groups
    places, parts = pl.pallas_call(
        functools.partial(cut_kernel, ops=ops),
        name="cut",
        out_shape=(
            jax.ShapeDtypeStruct((groups, near, LANES), jnp.int32),
            jax.ShapeDtypeStruct((ops * LANES, 2 * LANES), bf16),
        ),
        in_specs=[VMEM] * 2,
        out_specs=(VMEM,) * 2,
        scratch_shapes=[pltpu.VMEM((ncoef * ops, LANES), f32)],
        compiler_params=PARAMS,
    )(near_list, operators)
    near_potential, low, rest, inexact = pl.pallas_call(
        functools.partial(near_kernel, ops=ops, sources=sources),
        name="near_counts",
        out_shape=(
            jax.ShapeDtypeStruct((tiles, LANES), f32),
            jax.ShapeDtypeStruct((leaves, ops * sources), bf16),
            jax.ShapeDtypeStruct((leaves, ops * sources), bf16),
            jax.ShapeDtypeStruct((8, LANES), f32),
        ),
        in_specs=[VMEM] * 7,
        out_specs=(VMEM,) * 4,
        scratch_shapes=[
            pltpu.VMEM((2 * PTS, 3 * leaves), jnp.int32),
            pltpu.VMEM((near, 5 * PTS, LANES), f32),
            pltpu.VMEM((groups, PTS, LANES), f32),
            pltpu.VMEM((leaves, codes), f32),
            pltpu.VMEM((leaves, block), f32),
            pltpu.VMEM((block, chunk), bf16),
            pltpu.VMEM((leaves, chunk), bf16),
        ],
        compiler_params=PARAMS,
    )(second, table, first, places, m2l_source, m2l_target, m2l_operator)

    local_exp = pl.pallas_call(
        functools.partial(far_kernel, ops=ops),
        name="far",
        out_shape=jax.ShapeDtypeStruct((ncoef, leaves), f32),
        in_specs=[VMEM] * 5,
        out_specs=VMEM,
        scratch_shapes=[pltpu.VMEM((2 * LANES, ops * sources), bf16)],
        compiler_params=PARAMS,
    )(inexact, parts, received, low, rest)
    return (local_exp, near_potential.reshape(npoints))


def solution(mesh):
    both = ("slab", "grp")
    return jax.shard_map(
        shards,
        mesh=mesh,
        in_specs=(
            P(None, both),
            P(both),
            P(None, both),
            P(),
            P(both, None),
            P(both, None),
            P(both, None),
            P(both, None),
            P(both, None),
        ),
        out_specs=(P(None, both), P(both)),
        check_vma=False,
    )
```

```python
import functools

import jax
import jax.numpy as jnp
from jax import lax
from jax.experimental import pallas as pl
from jax.experimental.pallas import tpu as pltpu
from jax.sharding import PartitionSpec as P

SOFT2 = 0.0625
LANES = 128
PTS = 16
SCALE = 2.0**20
VMEM = pl.BlockSpec(memory_space=pltpu.VMEM)
ANY = pl.BlockSpec(memory_space=pl.ANY)
PARAMS = pltpu.CompilerParams(vmem_limit_bytes=48 * 1024 * 1024)
NT = (((1,), (1,)), ((), ()))


def lane_gather(x, idx):
    return jnp.take_along_axis(x, idx, axis=1, mode="promise_in_bounds")


def split(x):
    hi = x.astype(jnp.bfloat16)
    return hi, (x - hi.astype(jnp.float32)).astype(jnp.bfloat16)


def pad_lanes(x):
    return jnp.concatenate([x, jnp.zeros((x.shape[0], LANES - x.shape[1]), x.dtype)], axis=1)


def prep_kernel(coords_hbm, charges_hbm, multipoles_hbm, send_hbm, *refs, others):
    sources, refs = refs[:others], refs[others:]
    (table_ref, out_ref, *targets), refs = refs[: others + 2], refs[others + 2 :]
    coords_ref, charges_ref, multipoles_ref, send_ref, sems = refs
    pairs = (
        (coords_hbm, coords_ref),
        (charges_hbm, charges_ref),
        (send_hbm, send_ref),
        (multipoles_hbm, multipoles_ref),
        *zip(sources, targets),
    )
    copies = [pltpu.make_async_copy(src, dst, sems.at[i]) for i, (src, dst) in enumerate(pairs)]
    for copy in copies:
        copy.start()
    copies[0].wait()
    copies[1].wait()
    for c in range(4):
        rows = charges_ref[...] if c == 3 else coords_ref[:, c, :]
        cols = rows.T
        for pair in range(4):
            a = cols[32 * pair : 32 * pair + 16, :]
            b = cols[32 * pair + 16 : 32 * pair + 32, :]
            table_ref[16 * c : 16 * c + 16, LANES * pair : LANES * (pair + 1)] = jnp.concatenate([a, b], axis=1)
    copies[2].wait()
    copies[3].wait()
    ncoef, leaves = multipoles_ref.shape
    for sb in range(send_ref.shape[1] // LANES):
        send = send_ref[:, LANES * sb : LANES * (sb + 1)]
        lane = send & (LANES - 1)
        group = send >> 7
        idx = jnp.broadcast_to(lane, (ncoef, LANES))
        picked = jnp.zeros((ncoef, LANES), jnp.float32)
        for g in range(leaves // LANES):
            got = lane_gather(multipoles_ref[:, LANES * g : LANES * (g + 1)], idx)
            picked = jnp.where(group == g, got, picked)
        out_ref[LANES * sb : LANES * (sb + 1), :] = picked.T
    for copy in copies[4:]:
        copy.wait()


def cut_kernel(list_ref, operators_ref, place_ref, parts_ref, wide_ref, *, ops):
    near, leaves = list_ref.shape
    ncoef = operators_ref.shape[1]
    groups = leaves // LANES
    even = lax.axis_index("slab") % 2 == 0
    lane = lax.broadcasted_iota(jnp.int32, (near, LANES), 1)
    for g in range(groups):
        idx = 8 * (lane & 15) + 2 * g + (lane >> 6)
        part = (lane & 63) >> 4
        row = jnp.zeros((near, LANES), jnp.int32)
        for s in range(groups):
            row = jnp.where(part == s, lane_gather(list_ref[:, LANES * s : LANES * (s + 1)], idx), row)
        side = row >> 9
        side = jnp.where(even, 2 - side, side)
        place_ref[g] = (side << 9) + ((row & 7) << 6) + ((row >> 3) & 63)
    wide_ref[...] = pad_lanes(operators_ref[...])
    for op in range(ops):
        matrix = wide_ref[pl.ds(op, ncoef, stride=ops), :]
        matrix = jnp.concatenate([matrix, jnp.zeros((LANES - ncoef, LANES), jnp.float32)], axis=0)
        hi, lo = split(matrix)
        parts_ref[LANES * spot(op, ops) : LANES * (spot(op, ops) + 1), :] = jnp.concatenate([hi, lo], axis=1)


def spot(op, ops):
    return (op % 4) * (ops // 4) + op // 4


def near_kernel(
    second_ref, own_ref, first_ref, place_ref, source_ref, target_ref, operator_ref,
    near_ref, low_ref, rest_ref, inexact_ref,
    packed_ref, picked_ref, pot_ref, acc_ref, pair_ref, a_ref, b_ref, *, ops, sources,
):
    groups, near, _ = place_ref.shape
    leaves = own_ref.shape[1]
    _, codes, chunk = a_ref.shape
    block = pair_ref.shape[1]
    f32, bf16 = jnp.float32, jnp.bfloat16
    iota = lax.broadcasted_iota(jnp.int32, (max(block, leaves), LANES), 0).astype(jnp.int16).reshape(-1, 16, LANES)
    zero = jnp.zeros((1, 16, LANES), bf16)
    one = jnp.ones((1, 16, LANES), bf16)

    def spread(row, dtype):
        return jnp.broadcast_to(row, (16, LANES)).astype(dtype)[None]

    def columns(ref, g, c):
        return ref[:, pl.ds(pl.multiple_of(g * chunk + c * LANES, LANES), LANES)]

    def mark_leaves(g, c, ref):
        leaf = spread(columns(target_ref, g, c), jnp.int16)
        marks = jnp.where(iota[: leaves // 16] == leaf, one, zero).reshape(leaves, LANES)
        ref[:, LANES * c : LANES * (c + 1)] = marks

    def mark_codes(g, c, ref, first, shift, weigh):
        size = ref.shape[0]
        op = columns(operator_ref, g, c)
        code = spread((op >> shift) * sources + columns(source_ref, g, c) - first, jnp.int16)
        marks = jnp.where(iota[: size // 16] == code, spread(weigh(op), bf16), zero).reshape(size, LANES)
        ref[:, LANES * c : LANES * (c + 1)] = marks

    def products(leaf_ref, code_ref):
        return lax.dot_general(leaf_ref[...], code_ref[...], NT, preferred_element_type=f32)

    def digit_weight(op):
        last = op & 3
        return jnp.where(last == 0, 1.0, jnp.where(last == 1, 64.0, jnp.where(last == 2, 4096.0, 2.0**18)))

    def marks(g, side):
        for c in range(chunk // LANES):
            mark_leaves(g, c, b_ref.at[side])
            for first in range(0, codes, block):
                mark_codes(g, c, a_ref.at[side, first : first + block], first, 2, digit_weight)
            yield

    def count(side):
        for first in range(0, codes, block):
            acc_ref[:, first : first + block] += products(b_ref.at[side], a_ref.at[side, first : first + block])

    acc_ref[...] = jnp.zeros_like(acc_ref)
    for k, ref in enumerate((first_ref, own_ref, second_ref)):
        x, y, z = (
            jnp.clip(jnp.floor(ref[PTS * c : PTS * (c + 1), :] * SCALE + 0.5), -SCALE, SCALE - 1.0).astype(jnp.int32)
            for c in range(3)
        )
        packed_ref[:PTS, leaves * k : leaves * (k + 1)] = (x << 11) | ((y >> 10) & 2047)
        packed_ref[PTS:, leaves * k : leaves * (k + 1)] = (z << 11) | (y & 1023)

    def gather(g, n):
        place = jnp.broadcast_to(place_ref[g, n : n + 1, :], (8, LANES))
        idx = place & (LANES - 1)
        group = place >> 7
        words = [jnp.zeros((8, LANES), jnp.int32) for _ in range(2 * PTS // 8)]
        charge = [jnp.zeros((8, LANES), f32) for _ in range(PTS // 8)]
        for s in range(3 * groups):
            here = group == s
            window = (first_ref, own_ref, second_ref)[s // groups]
            at = slice(LANES * (s % groups), LANES * (s % groups + 1))
            for r in range(2 * PTS // 8):
                got = lane_gather(packed_ref[8 * r : 8 * r + 8, LANES * s : LANES * (s + 1)], idx)
                words[r] = jnp.where(here, got, words[r])
            for r in range(PTS // 8):
                got = lane_gather(window[3 * PTS + 8 * r : 3 * PTS + 8 * r + 8, at], idx)
                charge[r] = jnp.where(here, got, charge[r])
            yield
        for r in range(PTS // 8):
            first, second = words[r], words[PTS // 8 + r]
            x = (first >> 11).astype(f32)
            y = (((first << 21) >> 11) | (second & 1023)).astype(f32)
            z = (second >> 11).astype(f32)
            for k, row in enumerate((x, y, z, charge[r], x * x + y * y + z * z)):
                picked_ref[n, PTS * k + 8 * r : PTS * k + 8 * r + 8, :] = row

    def quarter(g, side):
        later = lax.rem(g + 1, groups)
        count(side)
        marking = marks(later, 1 - side)
        at = pl.ds(pl.multiple_of(g * LANES, LANES), LANES)
        tx, ty, tz = (own_ref[PTS * c : PTS * (c + 1), at] * SCALE for c in range(3))
        square = tx * tx + ty * ty + (tz * tz + SOFT2 * SCALE * SCALE)
        tx, ty, tz = -2.0 * tx, -2.0 * ty, -2.0 * tz
        sums = [jnp.zeros((PTS, LANES), f32) for _ in range(2)]
        for n in range(near):
            coming = gather(g, n + 1) if n + 1 < near else gather(later, 0)
            for p in range(PTS):
                sx, sy, sz, q, far = (picked_ref[n, PTS * c + p : PTS * c + p + 1, :] for c in range(5))
                sums[p % 2] += q * lax.rsqrt((square + far) + tx * sx + (ty * sy + tz * sz))
                next(coming, None)
            next(marking, None)
        for _ in marking:
            pass
        pot_ref[g] = (sums[0] + sums[1]) * SCALE

    for _ in gather(0, 0):
        pass
    for _ in marks(0, 0):
        pass

    def step(i, carry):
        quarter(2 * i, 0)
        quarter(2 * i + 1, 1)
        return carry

    lax.fori_loop(0, groups // 2, step, 0)
    half = LANES // 2
    pieces = []
    for g in range(groups):
        pot = pot_ref[g]
        pieces += [pot[:, :half], pot[:, half:]]
    near_ref[...] = jnp.concatenate(pieces, axis=0).T

    value = acc_ref[...]
    total = jnp.zeros_like(value)
    left = value
    for digit in range(4):
        above = jnp.floor(left * (1.0 / 64.0))
        here = left - 64.0 * above
        low_ref[:, codes * digit : codes * (digit + 1)] = here.astype(bf16)
        total += here
        left = above
    total = jnp.where(value < 2.0**24, total, -(2.0**30))
    used = jnp.sum(jnp.where(target_ref[...] < leaves, 1.0, 0.0))
    carried = jnp.sum(total) != used
    inexact_ref[...] = jnp.zeros_like(inexact_ref)

    @pl.when(carried)
    def _():
        pairs = ops // 2 * sources
        size = pair_ref.shape[1]
        for first in range(0, pairs, size):
            pair_ref[...] = jnp.full(pair_ref.shape, -(2.0**24), f32)

            def more(g, carry):
                for c in range(chunk // LANES):
                    mark_leaves(g, c, b_ref.at[0])
                    mark_codes(g, c, a_ref.at[0, :size], first, 1, lambda op: jnp.where((op & 1) == 1, 8192.0, 1.0))
                pair_ref[...] += products(b_ref.at[0], a_ref.at[0, :size])
                return carry

            lax.fori_loop(0, groups, more, 0)
            for lane in range(first, first + size, LANES):
                value = pair_ref[:, lane - first : lane - first + LANES]
                odd = jnp.floor(value * (1.0 / 8192.0))
                for parity, count in enumerate((value - 8192.0 * odd, odd + 2048.0)):
                    to = spot(2 * (lane // sources) + parity, ops) * sources + lane % sources
                    kept = count.astype(bf16)
                    low_ref[:, to : to + LANES] = kept
                    rest_ref[:, to : to + LANES] = (count - kept.astype(f32)).astype(bf16)
        inexact_ref[...] = jnp.ones_like(inexact_ref)


def far_kernel(inexact_ref, parts_ref, received_ref, low_ref, rest_ref, out_ref, split_ref, *, ops):
    ncoef, leaves = out_ref.shape
    sources = received_ref.shape[0]
    hi, lo = split(pad_lanes(received_ref[...]))
    table = lax.dot_general(
        parts_ref[...], jnp.concatenate([hi, hi], axis=1), NT, preferred_element_type=jnp.float32
    ) + lax.dot_general(parts_ref[:, :LANES], lo, NT, preferred_element_type=jnp.float32)
    for k in range(ops):
        hi, lo = split(table[LANES * k : LANES * (k + 1), :])
        split_ref[:LANES, sources * k : sources * (k + 1)] = hi
        split_ref[LANES:, sources * k : sources * (k + 1)] = lo

    def product(counts):
        both = lax.dot_general(split_ref[...], counts, NT, preferred_element_type=jnp.float32)
        return both[:ncoef, :] + both[LANES : LANES + ncoef, :]

    out_ref[...] = product(low_ref[...])

    @pl.when(jnp.max(inexact_ref[...]) > 0.0)
    def _():
        out_ref[...] += product(rest_ref[...])


def shards(
    coords,
    charges,
    multipoles,
    operators,
    send_list,
    near_list,
    m2l_source,
    m2l_target,
    m2l_operator,
):
    ncoef, leaves = multipoles.shape
    npoints = charges.shape[0]
    near = near_list.shape[1]
    entries = m2l_source.shape[1]
    ops = operators.shape[0]
    sources = send_list.shape[1]
    peers = lax.axis_size("grp")
    f32, bf16 = jnp.float32, jnp.bfloat16

    tiles = npoints // LANES
    points = (jnp.transpose(coords.reshape(3, tiles, LANES), (1, 0, 2)), charges.reshape(tiles, LANES))
    others = (
        near_list.T,
        m2l_source,
        m2l_target,
        m2l_operator,
        jnp.transpose(operators, (1, 0, 2)).reshape(ncoef * ops, ncoef),
    )
    table, outgoing, near_list, m2l_source, m2l_target, m2l_operator, operators = pl.pallas_call(
        functools.partial(prep_kernel, others=len(others)),
        name="prep",
        out_shape=(
            pltpu.VMEM((4 * PTS, leaves), f32),
            pltpu.VMEM((sources, ncoef), f32),
            *(pltpu.VMEM(x.shape, x.dtype) for x in others),
        ),
        in_specs=[ANY] * (4 + len(others)),
        out_specs=(VMEM,) * (2 + len(others)),
        scratch_shapes=[
            pltpu.VMEM((tiles, 3, LANES), f32),
            pltpu.VMEM((tiles, LANES), f32),
            pltpu.VMEM((ncoef, leaves), f32),
            pltpu.VMEM((1, sources), jnp.int32),
            pltpu.SemaphoreType.DMA((4 + len(others),)),
        ],
        compiler_params=PARAMS,
    )(*(pltpu.with_memory_space_constraint(x, pltpu.HBM) for x in (*points, multipoles, send_list, *others)))
    received = lax.all_to_all(
        outgoing.reshape(peers, sources // peers, ncoef), "grp", split_axis=0, concat_axis=0, tiled=True
    ).reshape(sources, ncoef)
    slabs = lax.axis_size("slab")

    def exchange(start):
        ties = [(i, i + 1) for i in range(start, slabs - 1, 2)]
        return lax.ppermute(table, "slab", ties + [(b, a) for a, b in ties])

    first = exchange(0)
    second = exchange(1)

    codes = ops // 4 * sources
    block = min(codes, 512)
    groups = leaves // LANES
    chunk = entries // groups
    places, parts = pl.pallas_call(
        functools.partial(cut_kernel, ops=ops),
        name="cut",
        out_shape=(
            jax.ShapeDtypeStruct((groups, near, LANES), jnp.int32),
            jax.ShapeDtypeStruct((ops * LANES, 2 * LANES), bf16),
        ),
        in_specs=[VMEM] * 2,
        out_specs=(VMEM,) * 2,
        scratch_shapes=[pltpu.VMEM((ncoef * ops, LANES), f32)],
        compiler_params=PARAMS,
    )(near_list, operators)
    near_potential, low, rest, inexact = pl.pallas_call(
        functools.partial(near_kernel, ops=ops, sources=sources),
        name="near_counts",
        out_shape=(
            jax.ShapeDtypeStruct((tiles, LANES), f32),
            jax.ShapeDtypeStruct((leaves, ops * sources), bf16),
            jax.ShapeDtypeStruct((leaves, ops * sources), bf16),
            jax.ShapeDtypeStruct((8, LANES), f32),
        ),
        in_specs=[VMEM] * 7,
        out_specs=(VMEM,) * 4,
        scratch_shapes=[
            pltpu.VMEM((2 * PTS, 3 * leaves), jnp.int32),
            pltpu.VMEM((near, 5 * PTS, LANES), f32),
            pltpu.VMEM((groups, PTS, LANES), f32),
            pltpu.VMEM((leaves, codes), f32),
            pltpu.VMEM((leaves, block), f32),
            pltpu.VMEM((2, codes, chunk), bf16),
            pltpu.VMEM((2, leaves, chunk), bf16),
        ],
        compiler_params=pltpu.CompilerParams(vmem_limit_bytes=(46 + sources // 64) * 1024 * 1024),
    )(second, table, first, places, m2l_source, m2l_target, m2l_operator)

    local_exp = pl.pallas_call(
        functools.partial(far_kernel, ops=ops),
        name="far",
        out_shape=jax.ShapeDtypeStruct((ncoef, leaves), f32),
        in_specs=[VMEM] * 5,
        out_specs=VMEM,
        scratch_shapes=[pltpu.VMEM((2 * LANES, ops * sources), bf16)],
        compiler_params=PARAMS,
    )(inexact, parts, received, low, rest)
    return (local_exp, near_potential.reshape(npoints))


def solution(mesh):
    both = ("slab", "grp")
    return jax.shard_map(
        shards,
        mesh=mesh,
        in_specs=(
            P(None, both),
            P(both),
            P(None, both),
            P(),
            P(both, None),
            P(both, None),
            P(both, None),
            P(both, None),
            P(both, None),
        ),
        out_specs=(P(None, both), P(both)),
        check_vma=False,
    )
```

```python
import functools

import jax
import jax.numpy as jnp
from jax import lax
from jax.experimental import pallas as pl
from jax.experimental.pallas import tpu as pltpu
from jax.sharding import PartitionSpec as P

SOFT2 = 0.0625
LANES = 128
PTS = 16
SCALE = 2.0**20
VMEM = pl.BlockSpec(memory_space=pltpu.VMEM)
ANY = pl.BlockSpec(memory_space=pl.ANY)
PARAMS = pltpu.CompilerParams(vmem_limit_bytes=48 * 1024 * 1024)
NT = (((1,), (1,)), ((), ()))


def lane_gather(x, idx):
    return jnp.take_along_axis(x, idx, axis=1, mode="promise_in_bounds")


def split(x):
    hi = x.astype(jnp.bfloat16)
    return hi, (x - hi.astype(jnp.float32)).astype(jnp.bfloat16)


def pad_lanes(x):
    return jnp.concatenate([x, jnp.zeros((x.shape[0], LANES - x.shape[1]), x.dtype)], axis=1)


def prep_kernel(coords_hbm, charges_hbm, multipoles_hbm, send_hbm, *refs, others):
    sources, refs = refs[:others], refs[others:]
    (table_ref, out_ref, *targets), refs = refs[: others + 2], refs[others + 2 :]
    coords_ref, charges_ref, multipoles_ref, send_ref, sems = refs
    pairs = (
        (coords_hbm, coords_ref),
        (charges_hbm, charges_ref),
        (send_hbm, send_ref),
        (multipoles_hbm, multipoles_ref),
        *zip(sources, targets),
    )
    copies = [pltpu.make_async_copy(src, dst, sems.at[i]) for i, (src, dst) in enumerate(pairs)]
    for copy in copies:
        copy.start()
    copies[0].wait()
    copies[1].wait()
    for c in range(4):
        rows = charges_ref[...] if c == 3 else coords_ref[:, c, :]
        cols = rows.T
        for pair in range(4):
            a = cols[32 * pair : 32 * pair + 16, :]
            b = cols[32 * pair + 16 : 32 * pair + 32, :]
            table_ref[16 * c : 16 * c + 16, LANES * pair : LANES * (pair + 1)] = jnp.concatenate([a, b], axis=1)
    copies[2].wait()
    copies[3].wait()
    ncoef, leaves = multipoles_ref.shape
    for sb in range(send_ref.shape[1] // LANES):
        send = send_ref[:, LANES * sb : LANES * (sb + 1)]
        lane = send & (LANES - 1)
        group = send >> 7
        idx = jnp.broadcast_to(lane, (ncoef, LANES))
        picked = jnp.zeros((ncoef, LANES), jnp.float32)
        for g in range(leaves // LANES):
            got = lane_gather(multipoles_ref[:, LANES * g : LANES * (g + 1)], idx)
            picked = jnp.where(group == g, got, picked)
        out_ref[LANES * sb : LANES * (sb + 1), :] = picked.T
    for copy in copies[4:]:
        copy.wait()


def cut_kernel(list_ref, operators_ref, place_ref, parts_ref, wide_ref, *, ops):
    near, leaves = list_ref.shape
    ncoef = operators_ref.shape[1]
    groups = leaves // LANES
    even = lax.axis_index("slab") % 2 == 0
    lane = lax.broadcasted_iota(jnp.int32, (near, LANES), 1)
    for g in range(groups):
        idx = 8 * (lane & 15) + 2 * g + (lane >> 6)
        part = (lane & 63) >> 4
        row = jnp.zeros((near, LANES), jnp.int32)
        for s in range(groups):
            row = jnp.where(part == s, lane_gather(list_ref[:, LANES * s : LANES * (s + 1)], idx), row)
        side = row >> 9
        side = jnp.where(even, 2 - side, side)
        place_ref[near * g : near * (g + 1), :] = (side << 9) + ((row & 7) << 6) + ((row >> 3) & 63)
    wide_ref[...] = pad_lanes(operators_ref[...])
    for op in range(ops):
        matrix = wide_ref[pl.ds(op, ncoef, stride=ops), :]
        matrix = jnp.concatenate([matrix, jnp.zeros((LANES - ncoef, LANES), jnp.float32)], axis=0)
        hi, lo = split(matrix)
        parts_ref[LANES * spot(op, ops) : LANES * (spot(op, ops) + 1), :] = jnp.concatenate([hi, lo], axis=1)


def spot(op, ops):
    return (op % 4) * (ops // 4) + op // 4


def near_kernel(
    second_ref, own_ref, first_ref, place_ref, source_ref, target_ref, operator_ref,
    near_ref, low_ref, rest_ref, inexact_ref,
    packed_ref, picked_ref, target_points_ref, pot_ref, acc_ref, pair_ref, a_ref, b_ref, *, ops, sources,
):
    leaves = own_ref.shape[1]
    groups = leaves // LANES
    near = place_ref.shape[0] // groups
    codes, chunk = a_ref.shape
    block = pair_ref.shape[1]
    f32, bf16 = jnp.float32, jnp.bfloat16
    iota = lax.broadcasted_iota(jnp.int32, (max(block, leaves), LANES), 0).astype(jnp.int16).reshape(-1, 16, LANES)
    zero = jnp.zeros((1, 16, LANES), bf16)
    one = jnp.ones((1, 16, LANES), bf16)

    def spread(row, dtype):
        return jnp.broadcast_to(row, (16, LANES)).astype(dtype)[None]

    def columns(ref, g, c):
        return ref[:, pl.ds(pl.multiple_of((g * (chunk // LANES) + c) * LANES, LANES), LANES)]

    def mark_leaves(g, c, ref):
        leaf = spread(columns(target_ref, g, c), jnp.int16)
        marks = jnp.where(iota[: leaves // 16] == leaf, one, zero).reshape(leaves, LANES)
        ref[:, LANES * c : LANES * (c + 1)] = marks

    def mark_codes(g, c, ref, first, shift, weigh):
        size = ref.shape[0]
        op = columns(operator_ref, g, c)
        code = spread((op >> shift) * sources + columns(source_ref, g, c) - first, jnp.int16)
        marks = jnp.where(iota[: size // 16] == code, spread(weigh(op), bf16), zero).reshape(size, LANES)
        ref[:, LANES * c : LANES * (c + 1)] = marks

    def products(leaf_ref, code_ref):
        return lax.dot_general(leaf_ref[...], code_ref[...], NT, preferred_element_type=f32)

    def digit_weight(op):
        last = op & 3
        return jnp.where(last == 0, 1.0, jnp.where(last == 1, 64.0, jnp.where(last == 2, 4096.0, 2.0**18)))

    def count():
        for first in range(0, codes, block):
            acc_ref[:, first : first + block] += products(b_ref, a_ref.at[first : first + block])

    acc_ref[...] = jnp.zeros_like(acc_ref)
    for k, ref in enumerate((first_ref, own_ref, second_ref)):
        x, y, z = (
            jnp.clip(jnp.floor(ref[PTS * c : PTS * (c + 1), :] * SCALE + 0.5), -SCALE, SCALE - 1.0).astype(jnp.int32)
            for c in range(3)
        )
        packed_ref[:PTS, leaves * k : leaves * (k + 1)] = (x << 11) | ((y >> 10) & 2047)
        packed_ref[PTS:, leaves * k : leaves * (k + 1)] = (z << 11) | (y & 1023)

    for g in range(groups):
        at = slice(LANES * g, LANES * (g + 1))
        tx, ty, tz = (own_ref[PTS * c : PTS * (c + 1), at] * SCALE for c in range(3))
        square = tx * tx + ty * ty + (tz * tz + SOFT2 * SCALE * SCALE)
        for k, rows in enumerate((-2.0 * tx, -2.0 * ty, -2.0 * tz, square)):
            target_points_ref[g, PTS * k : PTS * (k + 1), :] = rows
    pot_ref[...] = jnp.zeros_like(pot_ref)
    steps = groups * near

    def gather(step, side):
        place = jnp.broadcast_to(place_ref[pl.ds(step, 1), :], (8, LANES))
        idx = place & (LANES - 1)
        group = place >> 7
        words = [jnp.zeros((8, LANES), jnp.int32) for _ in range(2 * PTS // 8)]
        charge = [jnp.zeros((8, LANES), f32) for _ in range(PTS // 8)]
        for s in range(3 * groups):
            here = group == s
            window = (first_ref, own_ref, second_ref)[s // groups]
            at = slice(LANES * (s % groups), LANES * (s % groups + 1))
            for r in range(2 * PTS // 8):
                got = lane_gather(packed_ref[8 * r : 8 * r + 8, LANES * s : LANES * (s + 1)], idx)
                words[r] = jnp.where(here, got, words[r])
            for r in range(PTS // 8):
                got = lane_gather(window[3 * PTS + 8 * r : 3 * PTS + 8 * r + 8, at], idx)
                charge[r] = jnp.where(here, got, charge[r])
            yield
        for r in range(PTS // 8):
            first, second = words[r], words[PTS // 8 + r]
            x = (first >> 11).astype(f32)
            y = (((first << 21) >> 11) | (second & 1023)).astype(f32)
            z = (second >> 11).astype(f32)
            for k, row in enumerate((x, y, z, charge[r], x * x + y * y + z * z)):
                picked_ref[side, PTS * k + 8 * r : PTS * k + 8 * r + 8, :] = row

    def pairs(step, side):
        g = lax.div(step, near)
        tx, ty, tz, square = (target_points_ref[g, PTS * k : PTS * (k + 1), :] for k in range(4))
        coming = gather(lax.rem(step + 1, steps), 1 - side)
        sums = [jnp.zeros((PTS, LANES), f32) for _ in range(2)]
        for p in range(PTS):
            sx, sy, sz, q, far = (picked_ref[side, PTS * c + p : PTS * c + p + 1, :] for c in range(5))
            sums[p % 2] += q * lax.rsqrt((square + far) + tx * sx + (ty * sy + tz * sz))
            next(coming, None)
        pot_ref[g] += sums[0] + sums[1]

    def mark(part):
        for c in range(chunk // LANES):
            mark_leaves(part, c, b_ref)
            for first in range(0, codes, block):
                mark_codes(part, c, a_ref.at[first : first + block], first, 2, digit_weight)

    passes = steps // 2
    for _ in gather(0, 0):
        pass
    mark(0)

    def step(i, carry):
        count()
        pairs(2 * i, 0)
        pairs(2 * i + 1, 1)
        mark(lax.rem(i + 1, passes))
        return carry

    lax.fori_loop(0, passes, step, 0)
    half = LANES // 2
    pieces = []
    for g in range(groups):
        pot = pot_ref[g] * SCALE
        pieces += [pot[:, :half], pot[:, half:]]
    near_ref[...] = jnp.concatenate(pieces, axis=0).T

    value = acc_ref[...]
    total = jnp.zeros_like(value)
    left = value
    for digit in range(4):
        above = jnp.floor(left * (1.0 / 64.0))
        here = left - 64.0 * above
        low_ref[:, codes * digit : codes * (digit + 1)] = here.astype(bf16)
        total += here
        left = above
    total = jnp.where(value < 2.0**24, total, -(2.0**30))
    used = jnp.sum(jnp.where(target_ref[...] < leaves, 1.0, 0.0))
    carried = jnp.sum(total) != used
    inexact_ref[...] = jnp.zeros_like(inexact_ref)

    @pl.when(carried)
    def _():
        pairs = ops // 2 * sources
        size = pair_ref.shape[1]
        for first in range(0, pairs, size):
            pair_ref[...] = jnp.full(pair_ref.shape, -(2.0**24), f32)

            def more(part, carry):
                for c in range(chunk // LANES):
                    mark_leaves(part, c, b_ref)
                    mark_codes(part, c, a_ref.at[:size], first, 1, lambda op: jnp.where((op & 1) == 1, 8192.0, 1.0))
                pair_ref[...] += products(b_ref, a_ref.at[:size])
                return carry

            lax.fori_loop(0, passes, more, 0)
            for lane in range(first, first + size, LANES):
                value = pair_ref[:, lane - first : lane - first + LANES]
                odd = jnp.floor(value * (1.0 / 8192.0))
                for parity, count in enumerate((value - 8192.0 * odd, odd + 2048.0)):
                    to = spot(2 * (lane // sources) + parity, ops) * sources + lane % sources
                    kept = count.astype(bf16)
                    low_ref[:, to : to + LANES] = kept
                    rest_ref[:, to : to + LANES] = (count - kept.astype(f32)).astype(bf16)
        inexact_ref[...] = jnp.ones_like(inexact_ref)


def far_kernel(inexact_ref, parts_ref, received_ref, low_ref, rest_ref, out_ref, split_ref, *, ops):
    ncoef, leaves = out_ref.shape
    sources = received_ref.shape[0]
    hi, lo = split(pad_lanes(received_ref[...]))
    table = lax.dot_general(
        parts_ref[...], jnp.concatenate([hi, hi], axis=1), NT, preferred_element_type=jnp.float32
    ) + lax.dot_general(parts_ref[:, :LANES], lo, NT, preferred_element_type=jnp.float32)
    for k in range(ops):
        hi, lo = split(table[LANES * k : LANES * (k + 1), :])
        split_ref[:LANES, sources * k : sources * (k + 1)] = hi
        split_ref[LANES:, sources * k : sources * (k + 1)] = lo

    def product(counts):
        both = lax.dot_general(split_ref[...], counts, NT, preferred_element_type=jnp.float32)
        return both[:ncoef, :] + both[LANES : LANES + ncoef, :]

    out_ref[...] = product(low_ref[...])

    @pl.when(jnp.max(inexact_ref[...]) > 0.0)
    def _():
        out_ref[...] += product(rest_ref[...])


def shards(
    coords,
    charges,
    multipoles,
    operators,
    send_list,
    near_list,
    m2l_source,
    m2l_target,
    m2l_operator,
):
    ncoef, leaves = multipoles.shape
    npoints = charges.shape[0]
    near = near_list.shape[1]
    entries = m2l_source.shape[1]
    ops = operators.shape[0]
    sources = send_list.shape[1]
    peers = lax.axis_size("grp")
    f32, bf16 = jnp.float32, jnp.bfloat16

    tiles = npoints // LANES
    points = (jnp.transpose(coords.reshape(3, tiles, LANES), (1, 0, 2)), charges.reshape(tiles, LANES))
    others = (
        near_list.T,
        m2l_source,
        m2l_target,
        m2l_operator,
        jnp.transpose(operators, (1, 0, 2)).reshape(ncoef * ops, ncoef),
    )
    table, outgoing, near_list, m2l_source, m2l_target, m2l_operator, operators = pl.pallas_call(
        functools.partial(prep_kernel, others=len(others)),
        name="prep",
        out_shape=(
            pltpu.VMEM((4 * PTS, leaves), f32),
            pltpu.VMEM((sources, ncoef), f32),
            *(pltpu.VMEM(x.shape, x.dtype) for x in others),
        ),
        in_specs=[ANY] * (4 + len(others)),
        out_specs=(VMEM,) * (2 + len(others)),
        scratch_shapes=[
            pltpu.VMEM((tiles, 3, LANES), f32),
            pltpu.VMEM((tiles, LANES), f32),
            pltpu.VMEM((ncoef, leaves), f32),
            pltpu.VMEM((1, sources), jnp.int32),
            pltpu.SemaphoreType.DMA((4 + len(others),)),
        ],
        compiler_params=PARAMS,
    )(*(pltpu.with_memory_space_constraint(x, pltpu.HBM) for x in (*points, multipoles, send_list, *others)))
    received = lax.all_to_all(
        outgoing.reshape(peers, sources // peers, ncoef), "grp", split_axis=0, concat_axis=0, tiled=True
    ).reshape(sources, ncoef)
    slabs = lax.axis_size("slab")

    def exchange(start):
        ties = [(i, i + 1) for i in range(start, slabs - 1, 2)]
        return lax.ppermute(table, "slab", ties + [(b, a) for a, b in ties])

    first = exchange(0)
    second = exchange(1)

    codes = ops // 4 * sources
    block = min(codes, 512)
    groups = leaves // LANES
    chunk = entries // (groups * near // 2)
    places, parts = pl.pallas_call(
        functools.partial(cut_kernel, ops=ops),
        name="cut",
        out_shape=(
            jax.ShapeDtypeStruct((groups * near, LANES), jnp.int32),
            jax.ShapeDtypeStruct((ops * LANES, 2 * LANES), bf16),
        ),
        in_specs=[VMEM] * 2,
        out_specs=(VMEM,) * 2,
        scratch_shapes=[pltpu.VMEM((ncoef * ops, LANES), f32)],
        compiler_params=PARAMS,
    )(near_list, operators)
    near_potential, low, rest, inexact = pl.pallas_call(
        functools.partial(near_kernel, ops=ops, sources=sources),
        name="near_counts",
        out_shape=(
            jax.ShapeDtypeStruct((tiles, LANES), f32),
            jax.ShapeDtypeStruct((leaves, ops * sources), bf16),
            jax.ShapeDtypeStruct((leaves, ops * sources), bf16),
            jax.ShapeDtypeStruct((8, LANES), f32),
        ),
        in_specs=[VMEM] * 7,
        out_specs=(VMEM,) * 4,
        scratch_shapes=[
            pltpu.VMEM((2 * PTS, 3 * leaves), jnp.int32),
            pltpu.VMEM((2, 5 * PTS, LANES), f32),
            pltpu.VMEM((groups, 4 * PTS, LANES), f32),
            pltpu.VMEM((groups, PTS, LANES), f32),
            pltpu.VMEM((leaves, codes), f32),
            pltpu.VMEM((leaves, block), f32),
            pltpu.VMEM((codes, chunk), bf16),
            pltpu.VMEM((leaves, chunk), bf16),
        ],
        compiler_params=pltpu.CompilerParams(vmem_limit_bytes=(46 + sources // 64) * 1024 * 1024),
    )(second, table, first, places, m2l_source, m2l_target, m2l_operator)

    local_exp = pl.pallas_call(
        functools.partial(far_kernel, ops=ops),
        name="far",
        out_shape=jax.ShapeDtypeStruct((ncoef, leaves), f32),
        in_specs=[VMEM] * 5,
        out_specs=VMEM,
        scratch_shapes=[pltpu.VMEM((2 * LANES, ops * sources), bf16)],
        compiler_params=PARAMS,
    )(inexact, parts, received, low, rest)
    return (local_exp, near_potential.reshape(npoints))


def solution(mesh):
    both = ("slab", "grp")
    return jax.shard_map(
        shards,
        mesh=mesh,
        in_specs=(
            P(None, both),
            P(both),
            P(None, both),
            P(),
            P(both, None),
            P(both, None),
            P(both, None),
            P(both, None),
            P(both, None),
        ),
        out_specs=(P(None, both), P(both)),
        check_vma=False,
    )
```

```python
import functools

import jax
import jax.numpy as jnp
from jax import lax
from jax.experimental import pallas as pl
from jax.experimental.pallas import tpu as pltpu
from jax.sharding import PartitionSpec as P

SOFT2 = 0.0625
LANES = 128
PTS = 16
SCALE = 2.0**20
VMEM = pl.BlockSpec(memory_space=pltpu.VMEM)
ANY = pl.BlockSpec(memory_space=pl.ANY)
PARAMS = pltpu.CompilerParams(vmem_limit_bytes=48 * 1024 * 1024)
NT = (((1,), (1,)), ((), ()))


def lane_gather(x, idx):
    return jnp.take_along_axis(x, idx, axis=1, mode="promise_in_bounds")


def split(x):
    hi = x.astype(jnp.bfloat16)
    return hi, (x - hi.astype(jnp.float32)).astype(jnp.bfloat16)


def pad_lanes(x):
    return jnp.concatenate([x, jnp.zeros((x.shape[0], LANES - x.shape[1]), x.dtype)], axis=1)


def prep_kernel(coords_hbm, charges_hbm, multipoles_hbm, send_hbm, *refs, others):
    sources, refs = refs[:others], refs[others:]
    (table_ref, out_ref, *targets), refs = refs[: others + 2], refs[others + 2 :]
    coords_ref, charges_ref, multipoles_ref, send_ref, sems = refs
    pairs = (
        (coords_hbm, coords_ref),
        (charges_hbm, charges_ref),
        (send_hbm, send_ref),
        (multipoles_hbm, multipoles_ref),
        *zip(sources, targets),
    )
    copies = [pltpu.make_async_copy(src, dst, sems.at[i]) for i, (src, dst) in enumerate(pairs)]
    for copy in copies:
        copy.start()
    copies[0].wait()
    copies[1].wait()
    for c in range(4):
        rows = charges_ref[...] if c == 3 else coords_ref[:, c, :]
        cols = rows.T
        for pair in range(4):
            a = cols[32 * pair : 32 * pair + 16, :]
            b = cols[32 * pair + 16 : 32 * pair + 32, :]
            table_ref[16 * c : 16 * c + 16, LANES * pair : LANES * (pair + 1)] = jnp.concatenate([a, b], axis=1)
    copies[2].wait()
    copies[3].wait()
    ncoef, leaves = multipoles_ref.shape
    for sb in range(send_ref.shape[1] // LANES):
        send = send_ref[:, LANES * sb : LANES * (sb + 1)]
        lane = send & (LANES - 1)
        group = send >> 7
        idx = jnp.broadcast_to(lane, (ncoef, LANES))
        picked = jnp.zeros((ncoef, LANES), jnp.float32)
        for g in range(leaves // LANES):
            got = lane_gather(multipoles_ref[:, LANES * g : LANES * (g + 1)], idx)
            picked = jnp.where(group == g, got, picked)
        out_ref[LANES * sb : LANES * (sb + 1), :] = picked.T
    for copy in copies[4:]:
        copy.wait()


def cut_kernel(list_ref, operators_ref, place_ref, parts_ref, wide_ref, *, ops):
    near, leaves = list_ref.shape
    ncoef = operators_ref.shape[1]
    groups = leaves // LANES
    even = lax.axis_index("slab") % 2 == 0
    lane = lax.broadcasted_iota(jnp.int32, (near, LANES), 1)
    for g in range(groups):
        idx = 8 * (lane & 15) + 2 * g + (lane >> 6)
        part = (lane & 63) >> 4
        row = jnp.zeros((near, LANES), jnp.int32)
        for s in range(groups):
            row = jnp.where(part == s, lane_gather(list_ref[:, LANES * s : LANES * (s + 1)], idx), row)
        side = row >> 9
        side = jnp.where(even, 2 - side, side)
        place_ref[g] = (side << 9) + ((row & 7) << 6) + ((row >> 3) & 63)
    wide_ref[...] = pad_lanes(operators_ref[...])
    for op in range(ops):
        matrix = wide_ref[pl.ds(op, ncoef, stride=ops), :]
        matrix = jnp.concatenate([matrix, jnp.zeros((LANES - ncoef, LANES), jnp.float32)], axis=0)
        hi, lo = split(matrix)
        parts_ref[LANES * spot(op, ops) : LANES * (spot(op, ops) + 1), :] = jnp.concatenate([hi, lo], axis=1)


def spot(op, ops):
    return (op % 4) * (ops // 4) + op // 4


def near_kernel(
    third_ref, own_ref, second_ref, first_ref, place_ref, source_ref, target_ref, operator_ref,
    near_ref, low_ref, rest_ref, inexact_ref,
    words_ref, charge_ref, spread_ref, pot_ref, acc_ref, pair_ref, a_ref, b_ref, *, ops, sources,
):
    groups, near, _ = place_ref.shape
    leaves = own_ref.shape[1]
    block, chunk = a_ref.shape
    codes = acc_ref.shape[1]
    f32, bf16 = jnp.float32, jnp.bfloat16
    iota = lax.broadcasted_iota(jnp.int32, (max(block, leaves), LANES), 0).astype(jnp.int16).reshape(-1, 16, LANES)
    zero = jnp.zeros((1, 16, LANES), bf16)
    one = jnp.ones((1, 16, LANES), bf16)

    def spread(row, dtype):
        return jnp.broadcast_to(row, (16, LANES)).astype(dtype)[None]

    def columns(ref, g, c):
        return ref[:, pl.ds(pl.multiple_of(g * chunk + c * LANES, LANES), LANES)]

    def mark_leaves(g):
        for c in range(chunk // LANES):
            leaf = spread(columns(target_ref, g, c), jnp.int16)
            marks = jnp.where(iota[: leaves // 16] == leaf, one, zero).reshape(leaves, LANES)
            b_ref[:, LANES * c : LANES * (c + 1)] = marks

    def mark_codes(g, first, size, shift, weigh):
        for c in range(chunk // LANES):
            op = columns(operator_ref, g, c)
            code = spread((op >> shift) * sources + columns(source_ref, g, c) - first, jnp.int16)
            marks = jnp.where(iota[: size // 16] == code, spread(weigh(op), bf16), zero).reshape(size, LANES)
            a_ref[:size, LANES * c : LANES * (c + 1)] = marks

    def products(size):
        return lax.dot_general(b_ref[...], a_ref[:size, :], NT, preferred_element_type=f32)

    def digit_weight(op):
        last = op & 3
        return jnp.where(last == 0, 1.0, jnp.where(last == 1, 64.0, jnp.where(last == 2, 4096.0, 2.0**18)))

    def count(g):
        mark_leaves(g)
        for first in range(0, codes, block):
            size = min(block, codes - first)
            mark_codes(g, first, size, 2, digit_weight)
            acc_ref[:, first : first + size] += products(size)

    acc_ref[...] = jnp.zeros_like(acc_ref)
    early = lax.axis_index("slab") < 2
    for k in range(3):
        for c in range(groups):
            at = slice(LANES * c, LANES * (c + 1))
            if k == 0:
                block4 = jnp.where(early, first_ref[:, at], third_ref[:, at])
            else:
                block4 = (own_ref, second_ref)[k - 1][:, at]
            x, y, z = (
                jnp.clip(
                    jnp.floor(block4[PTS * i : PTS * (i + 1), :] * SCALE + 0.5), -SCALE, SCALE - 1.0
                ).astype(jnp.int32)
                for i in range(3)
            )
            for w, word in enumerate(((x << 11) | ((y >> 10) & 2047), (z << 11) | (y & 1023))):
                for j in range(PTS):
                    words_ref[w, j, groups * k + c] = jnp.broadcast_to(word[j : j + 1, :], (near, LANES))
            for j in range(PTS):
                charge_ref[j, groups * k + c] = jnp.broadcast_to(
                    block4[3 * PTS + j : 3 * PTS + j + 1, :], (near, LANES)
                )
    for g in range(groups):
        at = slice(LANES * g, LANES * (g + 1))
        tx, ty, tz = (own_ref[PTS * c : PTS * (c + 1), at] * SCALE for c in range(3))
        square = tx * tx + ty * ty + (tz * tz + SOFT2 * SCALE * SCALE)
        for k, rows in enumerate((-2.0 * tx, -2.0 * ty, -2.0 * tz, square)):
            for p in range(PTS):
                spread_ref[g, p, k] = jnp.broadcast_to(rows[p : p + 1, :], (near, LANES))

    def gather(place, j, found):
        idx = place & (LANES - 1)
        group = place >> 7
        points = [[jnp.zeros((near, LANES), t) for t in (jnp.int32, jnp.int32, f32)] for _ in range(2)]
        for s in range(3 * groups):
            here = group == s
            for i, point in enumerate(points):
                for w, ref in enumerate((words_ref.at[0], words_ref.at[1], charge_ref)):
                    point[w] = jnp.where(here, lane_gather(ref[j + i, s], idx), point[w])
            yield
        for first, second, charge in points:
            x = (first >> 11).astype(f32)
            y = (((first << 21) >> 11) | (second & 1023)).astype(f32)
            z = (second >> 11).astype(f32)
            found.append((x, y, z, x * x + y * y + z * z, charge))

    def step(g, carry):
        count(g)
        place = place_ref[g]
        sums = [jnp.zeros((near, LANES), f32) for _ in range(PTS)]
        found = []
        for _ in gather(place, 0, found):
            pass
        for j in range(0, PTS, 2):
            now, found = found, []
            coming = gather(place, j + 2, found) if j + 2 < PTS else iter(())
            for p in range(PTS):
                tx, ty, tz, square = (spread_ref[g, p, k] for k in range(4))
                for x, y, z, far, charge in now:
                    sums[p] += charge * lax.rsqrt((square + far) + tx * x + (ty * y + tz * z))
                next(coming, None)
        for p in range(PTS):
            pot_ref[g, p : p + 1, :] = jnp.sum(sums[p], axis=0, keepdims=True) * SCALE
        return carry

    lax.fori_loop(0, groups, step, 0)
    half = LANES // 2
    pieces = []
    for g in range(groups):
        pot = pot_ref[g]
        pieces += [pot[:, :half], pot[:, half:]]
    near_ref[...] = jnp.concatenate(pieces, axis=0).T

    value = acc_ref[...]
    total = jnp.zeros_like(value)
    left = value
    for digit in range(4):
        above = jnp.floor(left * (1.0 / 64.0))
        here = left - 64.0 * above
        low_ref[:, codes * digit : codes * (digit + 1)] = here.astype(bf16)
        total += here
        left = above
    total = jnp.where(value < 2.0**24, total, -(2.0**30))
    used = jnp.sum(jnp.where(target_ref[...] < leaves, 1.0, 0.0))
    carried = jnp.sum(total) != used
    inexact_ref[...] = jnp.zeros_like(inexact_ref)

    @pl.when(carried)
    def _():
        pairs = ops // 2 * sources
        for first in range(0, pairs, block):
            size = min(block, pairs - first)
            pair_ref[:, :size] = jnp.full((leaves, size), -(2.0**24), f32)

            def more(g, carry):
                mark_leaves(g)
                mark_codes(g, first, size, 1, lambda op: jnp.where((op & 1) == 1, 8192.0, 1.0))
                pair_ref[:, :size] += products(size)
                return carry

            lax.fori_loop(0, groups, more, 0)
            for lane in range(first, first + size, LANES):
                value = pair_ref[:, lane - first : lane - first + LANES]
                odd = jnp.floor(value * (1.0 / 8192.0))
                for parity, count in enumerate((value - 8192.0 * odd, odd + 2048.0)):
                    to = spot(2 * (lane // sources) + parity, ops) * sources + lane % sources
                    kept = count.astype(bf16)
                    low_ref[:, to : to + LANES] = kept
                    rest_ref[:, to : to + LANES] = (count - kept.astype(f32)).astype(bf16)
        inexact_ref[...] = jnp.ones_like(inexact_ref)


def far_kernel(inexact_ref, parts_ref, received_ref, low_ref, rest_ref, out_ref, split_ref, *, ops):
    ncoef, leaves = out_ref.shape
    sources = received_ref.shape[0]
    hi, lo = split(pad_lanes(received_ref[...]))
    table = lax.dot_general(
        parts_ref[...], jnp.concatenate([hi, hi], axis=1), NT, preferred_element_type=jnp.float32
    ) + lax.dot_general(parts_ref[:, :LANES], lo, NT, preferred_element_type=jnp.float32)
    for k in range(ops):
        hi, lo = split(table[LANES * k : LANES * (k + 1), :])
        split_ref[:LANES, sources * k : sources * (k + 1)] = hi
        split_ref[LANES:, sources * k : sources * (k + 1)] = lo

    def product(counts):
        both = lax.dot_general(split_ref[...], counts, NT, preferred_element_type=jnp.float32)
        return both[:ncoef, :] + both[LANES : LANES + ncoef, :]

    out_ref[...] = product(low_ref[...])

    @pl.when(jnp.max(inexact_ref[...]) > 0.0)
    def _():
        out_ref[...] += product(rest_ref[...])


def shards(
    coords,
    charges,
    multipoles,
    operators,
    send_list,
    near_list,
    m2l_source,
    m2l_target,
    m2l_operator,
):
    ncoef, leaves = multipoles.shape
    npoints = charges.shape[0]
    near = near_list.shape[1]
    entries = m2l_source.shape[1]
    ops = operators.shape[0]
    sources = send_list.shape[1]
    peers = lax.axis_size("grp")
    f32, bf16 = jnp.float32, jnp.bfloat16

    tiles = npoints // LANES
    points = (jnp.transpose(coords.reshape(3, tiles, LANES), (1, 0, 2)), charges.reshape(tiles, LANES))
    others = (
        near_list.T,
        m2l_source,
        m2l_target,
        m2l_operator,
        jnp.transpose(operators, (1, 0, 2)).reshape(ncoef * ops, ncoef),
    )
    table, outgoing, near_list, m2l_source, m2l_target, m2l_operator, operators = pl.pallas_call(
        functools.partial(prep_kernel, others=len(others)),
        name="prep",
        out_shape=(
            pltpu.VMEM((4 * PTS, leaves), f32),
            pltpu.VMEM((sources, ncoef), f32),
            *(pltpu.VMEM(x.shape, x.dtype) for x in others),
        ),
        in_specs=[ANY] * (4 + len(others)),
        out_specs=(VMEM,) * (2 + len(others)),
        scratch_shapes=[
            pltpu.VMEM((tiles, 3, LANES), f32),
            pltpu.VMEM((tiles, LANES), f32),
            pltpu.VMEM((ncoef, leaves), f32),
            pltpu.VMEM((1, sources), jnp.int32),
            pltpu.SemaphoreType.DMA((4 + len(others),)),
        ],
        compiler_params=PARAMS,
    )(*(pltpu.with_memory_space_constraint(x, pltpu.HBM) for x in (*points, multipoles, send_list, *others)))
    received = lax.all_to_all(
        outgoing.reshape(peers, sources // peers, ncoef), "grp", split_axis=0, concat_axis=0, tiled=True
    ).reshape(sources, ncoef)
    slabs = lax.axis_size("slab")

    def exchange(ties):
        return lax.ppermute(table, "slab", ties + [(b, a) for a, b in ties])

    first = exchange([(0, 1)])
    second = exchange([(i, i + 1) for i in range(1, slabs - 1, 2)])
    third = exchange([(i, i + 1) for i in range(2, slabs - 1, 2)])

    codes = ops // 4 * sources
    block = min(2 * codes, 512)
    groups = leaves // LANES
    chunk = entries // groups
    places, parts = pl.pallas_call(
        functools.partial(cut_kernel, ops=ops),
        name="cut",
        out_shape=(
            jax.ShapeDtypeStruct((groups, near, LANES), jnp.int32),
            jax.ShapeDtypeStruct((ops * LANES, 2 * LANES), bf16),
        ),
        in_specs=[VMEM] * 2,
        out_specs=(VMEM,) * 2,
        scratch_shapes=[pltpu.VMEM((ncoef * ops, LANES), f32)],
        compiler_params=PARAMS,
    )(near_list, operators)
    near_potential, low, rest, inexact = pl.pallas_call(
        functools.partial(near_kernel, ops=ops, sources=sources),
        name="near_counts",
        out_shape=(
            jax.ShapeDtypeStruct((tiles, LANES), f32),
            jax.ShapeDtypeStruct((leaves, ops * sources), bf16),
            jax.ShapeDtypeStruct((leaves, ops * sources), bf16),
            jax.ShapeDtypeStruct((8, LANES), f32),
        ),
        in_specs=[VMEM] * 8,
        out_specs=(VMEM,) * 4,
        scratch_shapes=[
            pltpu.VMEM((2, PTS, 3 * groups, near, LANES), jnp.int32),
            pltpu.VMEM((PTS, 3 * groups, near, LANES), f32),
            pltpu.VMEM((groups, PTS, 4, near, LANES), f32),
            pltpu.VMEM((groups, PTS, LANES), f32),
            pltpu.VMEM((leaves, codes), f32),
            pltpu.VMEM((leaves, block), f32),
            pltpu.VMEM((block, chunk), bf16),
            pltpu.VMEM((leaves, chunk), bf16),
        ],
        compiler_params=PARAMS,
    )(third, table, second, first, places, m2l_source, m2l_target, m2l_operator)

    local_exp = pl.pallas_call(
        functools.partial(far_kernel, ops=ops),
        name="far",
        out_shape=jax.ShapeDtypeStruct((ncoef, leaves), f32),
        in_specs=[VMEM] * 5,
        out_specs=VMEM,
        scratch_shapes=[pltpu.VMEM((2 * LANES, ops * sources), bf16)],
        compiler_params=PARAMS,
    )(inexact, parts, received, low, rest)
    return (local_exp, near_potential.reshape(npoints))


def solution(mesh):
    both = ("slab", "grp")
    return jax.shard_map(
        shards,
        mesh=mesh,
        in_specs=(
            P(None, both),
            P(both),
            P(None, both),
            P(),
            P(both, None),
            P(both, None),
            P(both, None),
            P(both, None),
            P(both, None),
        ),
        out_specs=(P(None, both), P(both)),
        check_vma=False,
    )
```

```python
import functools

import jax
import jax.numpy as jnp
from jax import lax
from jax.experimental import pallas as pl
from jax.experimental.pallas import tpu as pltpu
from jax.sharding import PartitionSpec as P

SOFT2 = 0.0625
LANES = 128
PTS = 16
UNITS = 2.0**20
SCALE = 2.0**31
VMEM = pl.BlockSpec(memory_space=pltpu.VMEM)
ANY = pl.BlockSpec(memory_space=pl.ANY)
PARAMS = pltpu.CompilerParams(vmem_limit_bytes=48 * 1024 * 1024)
NT = (((1,), (1,)), ((), ()))


def lane_gather(x, idx):
    return jnp.take_along_axis(x, idx, axis=1, mode="promise_in_bounds")


def split(x):
    hi = x.astype(jnp.bfloat16)
    return hi, (x - hi.astype(jnp.float32)).astype(jnp.bfloat16)


def pad_lanes(x):
    return jnp.concatenate([x, jnp.zeros((x.shape[0], LANES - x.shape[1]), x.dtype)], axis=1)


def prep_kernel(coords_hbm, charges_hbm, multipoles_hbm, send_hbm, *refs, others):
    sources, refs = refs[:others], refs[others:]
    (table_ref, out_ref, *targets), refs = refs[: others + 2], refs[others + 2 :]
    coords_ref, charges_ref, multipoles_ref, send_ref, sems = refs
    pairs = (
        (coords_hbm, coords_ref),
        (charges_hbm, charges_ref),
        (send_hbm, send_ref),
        (multipoles_hbm, multipoles_ref),
        *zip(sources, targets),
    )
    copies = [pltpu.make_async_copy(src, dst, sems.at[i]) for i, (src, dst) in enumerate(pairs)]
    for copy in copies:
        copy.start()
    copies[0].wait()
    copies[1].wait()
    for c in range(4):
        rows = charges_ref[...] if c == 3 else coords_ref[:, c, :]
        cols = rows.T
        for pair in range(4):
            a = cols[32 * pair : 32 * pair + 16, :]
            b = cols[32 * pair + 16 : 32 * pair + 32, :]
            table_ref[16 * c : 16 * c + 16, LANES * pair : LANES * (pair + 1)] = jnp.concatenate([a, b], axis=1)
    copies[2].wait()
    copies[3].wait()
    ncoef, leaves = multipoles_ref.shape
    for sb in range(send_ref.shape[1] // LANES):
        send = send_ref[:, LANES * sb : LANES * (sb + 1)]
        lane = send & (LANES - 1)
        group = send >> 7
        idx = jnp.broadcast_to(lane, (ncoef, LANES))
        picked = jnp.zeros((ncoef, LANES), jnp.float32)
        for g in range(leaves // LANES):
            got = lane_gather(multipoles_ref[:, LANES * g : LANES * (g + 1)], idx)
            picked = jnp.where(group == g, got, picked)
        out_ref[LANES * sb : LANES * (sb + 1), :] = picked.T
    for copy in copies[4:]:
        copy.wait()


def cut_kernel(list_ref, operators_ref, place_ref, parts_ref, wide_ref, *, ops):
    near, leaves = list_ref.shape
    ncoef = operators_ref.shape[1]
    groups = leaves // LANES
    even = lax.axis_index("slab") % 2 == 0
    lane = lax.broadcasted_iota(jnp.int32, (near, LANES), 1)
    for g in range(groups):
        idx = 8 * (lane & 15) + 2 * g + (lane >> 6)
        part = (lane & 63) >> 4
        row = jnp.zeros((near, LANES), jnp.int32)
        for s in range(groups):
            row = jnp.where(part == s, lane_gather(list_ref[:, LANES * s : LANES * (s + 1)], idx), row)
        side = row >> 9
        side = jnp.where(even, 2 - side, side)
        place_ref[g] = (side << 9) + ((row & 7) << 6) + ((row >> 3) & 63)
    wide_ref[...] = pad_lanes(operators_ref[...])
    for op in range(ops):
        matrix = wide_ref[pl.ds(op, ncoef, stride=ops), :]
        matrix = jnp.concatenate([matrix, jnp.zeros((LANES - ncoef, LANES), jnp.float32)], axis=0)
        hi, lo = split(matrix)
        parts_ref[LANES * spot(op, ops) : LANES * (spot(op, ops) + 1), :] = jnp.concatenate([hi, lo], axis=1)


def spot(op, ops):
    return (op % 4) * (ops // 4) + op // 4


class Marks:
    def __init__(self, rows, chunk):
        self.iota = lax.broadcasted_iota(jnp.int32, (rows, LANES), 0).astype(jnp.int16).reshape(-1, 16, LANES)
        self.chunk = chunk

    def columns(self, ref, part, c):
        return ref[:, pl.ds(pl.multiple_of(part * self.chunk + c * LANES, LANES), LANES)]

    def put(self, ref, c, code, weight):
        size = ref.shape[0]
        code, weight = (
            jnp.broadcast_to(x, (16, LANES)).astype(t)[None] for x, t in ((code, jnp.int16), (weight, jnp.bfloat16))
        )
        marks = jnp.where(self.iota[: size // 16] == code, weight, jnp.zeros((1, 16, LANES), jnp.bfloat16))
        ref[:, LANES * c : LANES * (c + 1)] = marks.reshape(size, LANES)


def near_kernel(
    second_ref, own_ref, first_ref, place_ref, source_ref, target_ref, operator_ref,
    near_ref, low_ref, peak_ref,
    packed_ref, charge_ref, picked_ref, pot_ref, acc_ref, a_ref, b_ref, *, sources,
):
    groups, near, _ = place_ref.shape
    leaves = own_ref.shape[1]
    half, codes = acc_ref.shape
    block, chunk = a_ref.shape
    f32 = jnp.float32
    marks = Marks(max(block, half), chunk)

    def count(g):
        for c in range(chunk // LANES):
            leaf = marks.columns(target_ref, g, c)
            upper = leaf >= half
            leaf = jnp.where(leaf < leaves, jnp.where(upper, leaf - half, leaf), -1)
            marks.put(b_ref, c, leaf, jnp.where(upper, 4096.0, 1.0))
        for first in range(0, codes, block):
            for c in range(chunk // LANES):
                op = marks.columns(operator_ref, g, c)
                code = (op >> 2) * sources + marks.columns(source_ref, g, c) - first
                last = op & 3
                weight = jnp.where(last == 0, 1.0, jnp.where(last == 1, 8.0, jnp.where(last == 2, 64.0, 512.0)))
                marks.put(a_ref, c, code, weight)
            acc_ref[:, first : first + block] += lax.dot_general(b_ref[...], a_ref[...], NT, preferred_element_type=f32)

    acc_ref[...] = jnp.zeros_like(acc_ref)
    me = lax.axis_index("slab")
    last = lax.axis_size("slab") - 1
    from_right = me % 2 == 0
    ends = (jnp.logical_and(from_right, me == last), False, jnp.where(from_right, me == 0, me == last))
    for k, (ref, end) in enumerate(zip((first_ref, own_ref, second_ref), ends)):
        x, y, z = (
            jnp.clip(jnp.floor(ref[PTS * c : PTS * (c + 1), :] * UNITS), -UNITS, UNITS - 1.0).astype(jnp.int32)
            for c in range(3)
        )
        at = slice(leaves * k, leaves * (k + 1))
        packed_ref[:PTS, at] = (x << 11) | ((y >> 10) & 2047)
        packed_ref[PTS:, at] = (z << 11) | ((y & 1023) << 1)
        charge_ref[:, at] = jnp.where(end, 0.0, ref[3 * PTS :, :])

    def gather(place):
        idx = place & (LANES - 1)
        group = place >> 7
        refs = [packed_ref.at[8 * r : 8 * r + 8] for r in range(2 * PTS // 8)]
        refs += [charge_ref.at[8 * r : 8 * r + 8] for r in range(PTS // 8)]
        found = [lane_gather(ref[:, :LANES], idx) for ref in refs]
        for s in range(1, 3 * groups):
            here = group == s
            for r, ref in enumerate(refs):
                found[r] = jnp.where(here, lane_gather(ref[:, LANES * s : LANES * (s + 1)], idx), found[r])
        return found

    def step(g, carry):
        count(g)
        at = pl.ds(pl.multiple_of(g * LANES, LANES), LANES)
        tx, ty, tz = (own_ref[PTS * c : PTS * (c + 1), at] * SCALE for c in range(3))
        square = tx * tx + ty * ty + (tz * tz + SOFT2 * SCALE * SCALE)
        tx, ty, tz = -2.0 * tx, -2.0 * ty, -2.0 * tz
        acc = jnp.zeros((PTS, LANES), f32)
        for n in range(near):
            found = gather(jnp.broadcast_to(place_ref[g, n : n + 1, :], (8, LANES)))
            for r in range(PTS // 8):
                first, second, charge = found[r :: PTS // 8]
                x = first.astype(f32)
                y = ((first << 21) | ((second & 2047) << 10)).astype(f32)
                z = second.astype(f32)
                for k, row in enumerate((x, y, z, charge, x * x + y * y + z * z)):
                    picked_ref[n, PTS * k + 8 * r : PTS * k + 8 * r + 8, :] = row
            for p in range(PTS):
                sx, sy, sz, q, far = (picked_ref[n, PTS * c + p : PTS * c + p + 1, :] for c in range(5))
                acc += q * lax.rsqrt((square + far) + tx * sx + (ty * sy + tz * sz))
        pot_ref[g] = acc * SCALE
        return carry

    lax.fori_loop(0, groups, step, 0)
    width = LANES // 2
    pieces = []
    for g in range(groups):
        pot = pot_ref[g]
        pieces += [pot[:, :width], pot[:, width:]]
    near_ref[...] = jnp.concatenate(pieces, axis=0).T

    value = acc_ref[...]
    peak_ref[...] = jnp.max(value.reshape(-1, 8, codes), axis=0)
    value = value.astype(jnp.int32)
    for digit in range(8):
        h, d = digit // 4, digit % 4
        here = (value >> (3 * digit)) & 7
        low_ref[half * h : half * (h + 1), codes * d : codes * (d + 1)] = here.astype(f32).astype(jnp.bfloat16)


def far_kernel(
    parts_ref, received_ref, low_ref, peak_ref, source_ref, target_ref, operator_ref,
    out_ref, split_ref, pair_ref, a_ref, b_ref, *, ops,
):
    ncoef, leaves = out_ref.shape
    sources = received_ref.shape[0]
    f32 = jnp.float32
    hi, lo = split(pad_lanes(received_ref[...]))
    table = lax.dot_general(
        parts_ref[...], jnp.concatenate([hi, hi], axis=1), NT, preferred_element_type=f32
    ) + lax.dot_general(parts_ref[:, :LANES], lo, NT, preferred_element_type=f32)
    ones = jnp.where(lax.broadcasted_iota(jnp.int32, (LANES, sources), 0) == LANES - 1, 1.0, 0.0)
    for k in range(ops):
        hi, lo = split(table[LANES * k : LANES * (k + 1), :] + ones)
        split_ref[:LANES, sources * k : sources * (k + 1)] = hi
        split_ref[LANES:, sources * k : sources * (k + 1)] = lo
    both = lax.dot_general(split_ref[...], low_ref[...], NT, preferred_element_type=f32)
    out_ref[...] = both[:ncoef, :] + both[LANES : LANES + ncoef, :]

    used = jnp.sum(jnp.where(target_ref[...] < leaves, 1.0, 0.0))
    total = jnp.sum(both[LANES - 1 : LANES, :])
    carried = jnp.logical_or(total != used, jnp.max(peak_ref[...]) >= 2.0**24)

    @pl.when(carried)
    def _():
        size, chunk = a_ref.shape
        marks = Marks(max(size, leaves), chunk)
        out_ref[...] = jnp.zeros_like(out_ref)
        for first in range(0, ops // 2 * sources, size):
            pair_ref[...] = jnp.full(pair_ref.shape, -(2.0**24), f32)

            def more(part, carry):
                for c in range(chunk // LANES):
                    op = marks.columns(operator_ref, part, c)
                    code = (op >> 1) * sources + marks.columns(source_ref, part, c) - first
                    marks.put(a_ref, c, code, jnp.where((op & 1) == 1, 8192.0, 1.0))
                    marks.put(b_ref, c, marks.columns(target_ref, part, c), jnp.ones((1, LANES), f32))
                pair_ref[...] += lax.dot_general(b_ref[...], a_ref[...], NT, preferred_element_type=f32)
                return carry

            lax.fori_loop(0, target_ref.shape[1] // chunk, more, 0)
            for lane in range(first, first + size, LANES):
                value = pair_ref[:, lane - first : lane - first + LANES]
                odd = jnp.floor(value * (1.0 / 8192.0))
                for parity, count in enumerate((value - 8192.0 * odd, odd + 2048.0)):
                    at = spot(2 * (lane // sources) + parity, ops) * sources + lane % sources
                    rows = split_ref[:, at : at + LANES].astype(f32)
                    rows = rows[:ncoef, :] + rows[LANES : LANES + ncoef, :]
                    out_ref[...] += lax.dot_general(
                        rows, count, NT, precision=lax.Precision.HIGHEST, preferred_element_type=f32
                    )


def shards(
    coords,
    charges,
    multipoles,
    operators,
    send_list,
    near_list,
    m2l_source,
    m2l_target,
    m2l_operator,
):
    ncoef, leaves = multipoles.shape
    npoints = charges.shape[0]
    near = near_list.shape[1]
    entries = m2l_source.shape[1]
    ops = operators.shape[0]
    sources = send_list.shape[1]
    peers = lax.axis_size("grp")
    f32, bf16 = jnp.float32, jnp.bfloat16

    tiles = npoints // LANES
    points = (jnp.transpose(coords.reshape(3, tiles, LANES), (1, 0, 2)), charges.reshape(tiles, LANES))
    others = (
        near_list.T,
        m2l_source,
        m2l_target,
        m2l_operator,
        jnp.transpose(operators, (1, 0, 2)).reshape(ncoef * ops, ncoef),
    )
    table, outgoing, near_list, m2l_source, m2l_target, m2l_operator, operators = pl.pallas_call(
        functools.partial(prep_kernel, others=len(others)),
        name="prep",
        out_shape=(
            pltpu.VMEM((4 * PTS, leaves), f32),
            pltpu.VMEM((sources, ncoef), f32),
            *(pltpu.VMEM(x.shape, x.dtype) for x in others),
        ),
        in_specs=[ANY] * (4 + len(others)),
        out_specs=(VMEM,) * (2 + len(others)),
        scratch_shapes=[
            pltpu.VMEM((tiles, 3, LANES), f32),
            pltpu.VMEM((tiles, LANES), f32),
            pltpu.VMEM((ncoef, leaves), f32),
            pltpu.VMEM((1, sources), jnp.int32),
            pltpu.SemaphoreType.DMA((4 + len(others),)),
        ],
        compiler_params=PARAMS,
    )(*(pltpu.with_memory_space_constraint(x, pltpu.HBM) for x in (*points, multipoles, send_list, *others)))
    received = lax.all_to_all(
        outgoing.reshape(peers, sources // peers, ncoef), "grp", split_axis=0, concat_axis=0, tiled=True
    ).reshape(sources, ncoef)
    slabs = lax.axis_size("slab")

    def exchange(start):
        partner = list(range(slabs))
        for i in range(start, slabs - 1, 2):
            partner[i], partner[i + 1] = i + 1, i
        return lax.ppermute(table, "slab", list(enumerate(partner)))

    first = exchange(0)
    second = exchange(1)

    codes = ops // 4 * sources
    block = min(codes, 512)
    groups = leaves // LANES
    chunk = entries // groups
    places, parts = pl.pallas_call(
        functools.partial(cut_kernel, ops=ops),
        name="cut",
        out_shape=(
            jax.ShapeDtypeStruct((groups, near, LANES), jnp.int32),
            jax.ShapeDtypeStruct((ops * LANES, 2 * LANES), bf16),
        ),
        in_specs=[VMEM] * 2,
        out_specs=(VMEM,) * 2,
        scratch_shapes=[pltpu.VMEM((ncoef * ops, LANES), f32)],
        compiler_params=PARAMS,
    )(near_list, operators)
    near_potential, low, peak = pl.pallas_call(
        functools.partial(near_kernel, sources=sources),
        name="near_counts",
        out_shape=(
            jax.ShapeDtypeStruct((tiles, LANES), f32),
            jax.ShapeDtypeStruct((leaves, ops * sources), bf16),
            jax.ShapeDtypeStruct((8, codes), f32),
        ),
        in_specs=[VMEM] * 7,
        out_specs=(VMEM,) * 3,
        scratch_shapes=[
            pltpu.VMEM((2 * PTS, 3 * leaves), jnp.int32),
            pltpu.VMEM((PTS, 3 * leaves), f32),
            pltpu.VMEM((near, 5 * PTS, LANES), f32),
            pltpu.VMEM((groups, PTS, LANES), f32),
            pltpu.VMEM((leaves // 2, codes), f32),
            pltpu.VMEM((block, chunk), bf16),
            pltpu.VMEM((leaves // 2, chunk), bf16),
        ],
        compiler_params=PARAMS,
    )(second, table, first, places, m2l_source, m2l_target, m2l_operator)

    local_exp = pl.pallas_call(
        functools.partial(far_kernel, ops=ops),
        name="far",
        out_shape=jax.ShapeDtypeStruct((ncoef, leaves), f32),
        in_specs=[VMEM] * 7,
        out_specs=VMEM,
        scratch_shapes=[
            pltpu.VMEM((2 * LANES, ops * sources), bf16),
            pltpu.VMEM((leaves, 512), f32),
            pltpu.VMEM((512, 512), bf16),
            pltpu.VMEM((leaves, 512), bf16),
        ],
        compiler_params=PARAMS,
    )(parts, received, low, peak, m2l_source, m2l_target, m2l_operator)
    return (local_exp, near_potential.reshape(npoints))


def solution(mesh):
    both = ("slab", "grp")
    return jax.shard_map(
        shards,
        mesh=mesh,
        in_specs=(
            P(None, both),
            P(both),
            P(None, both),
            P(),
            P(both, None),
            P(both, None),
            P(both, None),
            P(both, None),
            P(both, None),
        ),
        out_specs=(P(None, both), P(both)),
        check_vma=False,
    )
```

```python
import functools

import jax
import jax.numpy as jnp
from jax import lax
from jax.experimental import pallas as pl
from jax.experimental.pallas import tpu as pltpu
from jax.sharding import PartitionSpec as P

SOFT2 = 0.0625
LANES = 128
PTS = 16
UNITS = 2.0**20
SCALE = 2.0**31
VMEM = pl.BlockSpec(memory_space=pltpu.VMEM)
ANY = pl.BlockSpec(memory_space=pl.ANY)
PARAMS = pltpu.CompilerParams(vmem_limit_bytes=48 * 1024 * 1024)
NT = (((1,), (1,)), ((), ()))


def lane_gather(x, idx):
    return jnp.take_along_axis(x, idx, axis=1, mode="promise_in_bounds")


def split(x):
    hi = x.astype(jnp.bfloat16)
    return hi, (x - hi.astype(jnp.float32)).astype(jnp.bfloat16)


def pad_lanes(x):
    return jnp.concatenate([x, jnp.zeros((x.shape[0], LANES - x.shape[1]), x.dtype)], axis=1)


def prep_kernel(coords_hbm, charges_hbm, multipoles_hbm, send_hbm, *refs, others):
    sources, refs = refs[:others], refs[others:]
    (table_ref, out_ref, *targets), refs = refs[: others + 2], refs[others + 2 :]
    coords_ref, charges_ref, multipoles_ref, send_ref, sems = refs
    pairs = (
        (coords_hbm, coords_ref),
        (charges_hbm, charges_ref),
        (send_hbm, send_ref),
        (multipoles_hbm, multipoles_ref),
        *zip(sources, targets),
    )
    copies = [pltpu.make_async_copy(src, dst, sems.at[i]) for i, (src, dst) in enumerate(pairs)]
    for copy in copies:
        copy.start()
    copies[0].wait()
    copies[1].wait()
    for c in range(4):
        rows = charges_ref[...] if c == 3 else coords_ref[:, c, :]
        cols = rows.T
        for pair in range(4):
            a = cols[32 * pair : 32 * pair + 16, :]
            b = cols[32 * pair + 16 : 32 * pair + 32, :]
            table_ref[16 * c : 16 * c + 16, LANES * pair : LANES * (pair + 1)] = jnp.concatenate([a, b], axis=1)
    copies[2].wait()
    copies[3].wait()
    ncoef, leaves = multipoles_ref.shape
    for sb in range(send_ref.shape[1] // LANES):
        send = send_ref[:, LANES * sb : LANES * (sb + 1)]
        lane = send & (LANES - 1)
        group = send >> 7
        idx = jnp.broadcast_to(lane, (ncoef, LANES))
        picked = jnp.zeros((ncoef, LANES), jnp.float32)
        for g in range(leaves // LANES):
            got = lane_gather(multipoles_ref[:, LANES * g : LANES * (g + 1)], idx)
            picked = jnp.where(group == g, got, picked)
        out_ref[LANES * sb : LANES * (sb + 1), :] = picked.T
    for copy in copies[4:]:
        copy.wait()


def cut_kernel(list_ref, operators_ref, place_ref, parts_ref, wide_ref, *, ops):
    near, leaves = list_ref.shape
    ncoef = operators_ref.shape[1]
    groups = leaves // LANES
    even = lax.axis_index("slab") % 2 == 0
    lane = lax.broadcasted_iota(jnp.int32, (near, LANES), 1)
    for g in range(groups):
        idx = 8 * (lane & 15) + 2 * g + (lane >> 6)
        part = (lane & 63) >> 4
        row = jnp.zeros((near, LANES), jnp.int32)
        for s in range(groups):
            row = jnp.where(part == s, lane_gather(list_ref[:, LANES * s : LANES * (s + 1)], idx), row)
        side = row >> 9
        side = jnp.where(even, 2 - side, side)
        place_ref[g] = (side << 9) + ((row & 7) << 6) + ((row >> 3) & 63)
    wide_ref[...] = pad_lanes(operators_ref[...])
    for op in range(ops):
        matrix = wide_ref[pl.ds(op, ncoef, stride=ops), :]
        matrix = jnp.concatenate([matrix, jnp.zeros((LANES - ncoef, LANES), jnp.float32)], axis=0)
        hi, lo = split(matrix)
        parts_ref[LANES * spot(op, ops) : LANES * (spot(op, ops) + 1), :] = jnp.concatenate([hi, lo], axis=1)


def spot(op, ops):
    return (op % 4) * (ops // 4) + op // 4


class Marks:
    def __init__(self, rows, chunk):
        self.iota = lax.broadcasted_iota(jnp.int32, (rows, LANES), 0).astype(jnp.int16).reshape(-1, 16, LANES)
        self.chunk = chunk

    def columns(self, ref, part, c):
        return ref[:, pl.ds(pl.multiple_of(part * self.chunk + c * LANES, LANES), LANES)]

    def put(self, ref, c, code, weight):
        size = ref.shape[0]
        code, weight = (
            jnp.broadcast_to(x, (16, LANES)).astype(t)[None] for x, t in ((code, jnp.int16), (weight, jnp.bfloat16))
        )
        marks = jnp.where(self.iota[: size // 16] == code, weight, jnp.zeros((1, 16, LANES), jnp.bfloat16))
        ref[:, LANES * c : LANES * (c + 1)] = marks.reshape(size, LANES)


def near_kernel(
    second_ref, own_ref, first_ref, place_ref, source_ref, target_ref, operator_ref,
    near_ref, low_ref, peak_ref,
    packed_ref, charge_ref, picked_ref, pot_ref, acc_ref, a_ref, b_ref, *, sources,
):
    groups, near, _ = place_ref.shape
    leaves = own_ref.shape[1]
    half, codes = acc_ref.shape
    block, chunk = a_ref.shape
    f32 = jnp.float32
    marks = Marks(max(block, half), chunk)

    def count(g):
        for c in range(chunk // LANES):
            leaf = marks.columns(target_ref, g, c)
            upper = leaf >= half
            leaf = jnp.where(leaf < leaves, jnp.where(upper, leaf - half, leaf), -1)
            marks.put(b_ref, c, leaf, jnp.where(upper, 4096.0, 1.0))
        for first in range(0, codes, block):
            for c in range(chunk // LANES):
                op = marks.columns(operator_ref, g, c)
                code = (op >> 2) * sources + marks.columns(source_ref, g, c) - first
                last = op & 3
                weight = jnp.where(last == 0, 1.0, jnp.where(last == 1, 8.0, jnp.where(last == 2, 64.0, 512.0)))
                marks.put(a_ref, c, code, weight)
            acc_ref[:, first : first + block] += lax.dot_general(b_ref[...], a_ref[...], NT, preferred_element_type=f32)

    acc_ref[...] = jnp.zeros_like(acc_ref)
    me = lax.axis_index("slab")
    last = lax.axis_size("slab") - 1
    from_right = me % 2 == 0
    ends = (jnp.logical_and(from_right, me == last), False, jnp.where(from_right, me == 0, me == last))
    for k, (ref, end) in enumerate(zip((first_ref, own_ref, second_ref), ends)):
        x, y, z = (
            jnp.clip(jnp.floor(ref[PTS * c : PTS * (c + 1), :] * UNITS), -UNITS, UNITS - 1.0).astype(jnp.int32)
            for c in range(3)
        )
        at = slice(leaves * k, leaves * (k + 1))
        packed_ref[:PTS, at] = (x << 11) | ((y >> 10) & 2047)
        packed_ref[PTS:, at] = (z << 11) | ((y & 1023) << 1)
        charge_ref[:, at] = jnp.where(end, 0.0, ref[3 * PTS :, :])

    def gather(place):
        idx = place & (LANES - 1)
        group = place >> 7
        refs = [packed_ref.at[8 * r : 8 * r + 8] for r in range(2 * PTS // 8)]
        refs += [charge_ref.at[8 * r : 8 * r + 8] for r in range(PTS // 8)]
        found = [lane_gather(ref[:, :LANES], idx) for ref in refs]
        for s in range(1, 3 * groups):
            here = group == s
            for r, ref in enumerate(refs):
                found[r] = jnp.where(here, lane_gather(ref[:, LANES * s : LANES * (s + 1)], idx), found[r])
        return found

    def step(g, carry):
        count(g)
        at = pl.ds(pl.multiple_of(g * LANES, LANES), LANES)
        tx, ty, tz = (own_ref[PTS * c : PTS * (c + 1), at] * SCALE for c in range(3))
        square = tx * tx + ty * ty + (tz * tz + SOFT2 * SCALE * SCALE)
        tx, ty, tz = -2.0 * tx, -2.0 * ty, -2.0 * tz
        acc = jnp.zeros((PTS, LANES), f32)
        for n in range(near):
            found = gather(jnp.broadcast_to(place_ref[g, n : n + 1, :], (8, LANES)))
            for r in range(PTS // 8):
                first, second, charge = found[r :: PTS // 8]
                x = first.astype(f32)
                y = ((first << 21) | ((second & 2047) << 10)).astype(f32)
                z = second.astype(f32)
                for k, row in enumerate((x, y, z, charge, x * x + y * y + z * z)):
                    picked_ref[n, PTS * k + 8 * r : PTS * k + 8 * r + 8, :] = row
            for p in range(PTS):
                sx, sy, sz, q, far = (picked_ref[n, PTS * c + p : PTS * c + p + 1, :] for c in range(5))
                acc += q * lax.rsqrt((square + far) + tx * sx + (ty * sy + tz * sz))
        pot_ref[g] = acc * SCALE
        return carry

    lax.fori_loop(0, groups, step, 0)
    width = LANES // 2
    pieces = []
    for g in range(groups):
        pot = pot_ref[g]
        pieces += [pot[:, :width], pot[:, width:]]
    near_ref[...] = jnp.concatenate(pieces, axis=0).T

    value = acc_ref[...]
    peak_ref[...] = jnp.max(value.reshape(-1, 8, codes), axis=0)
    value = value.astype(jnp.int32)
    for digit in range(8):
        h, d = digit // 4, digit % 4
        here = (value >> (3 * digit)) & 7
        low_ref[half * h : half * (h + 1), codes * d : codes * (d + 1)] = here.astype(f32).astype(jnp.bfloat16)


def far_kernel(
    parts_ref, received_ref, low_ref, peak_ref, source_ref, target_ref, operator_ref,
    out_ref, split_ref, pair_ref, a_ref, b_ref, *, ops,
):
    ncoef, leaves = out_ref.shape
    sources = received_ref.shape[0]
    f32 = jnp.float32
    hi, lo = split(pad_lanes(received_ref[...]))
    table = lax.dot_general(
        parts_ref[...], jnp.concatenate([hi, hi], axis=1), NT, preferred_element_type=f32
    ) + lax.dot_general(parts_ref[:, :LANES], lo, NT, preferred_element_type=f32)
    ones = jnp.where(lax.broadcasted_iota(jnp.int32, (LANES, sources), 0) == LANES - 1, 1.0, 0.0)
    for k in range(ops):
        hi, lo = split(table[LANES * k : LANES * (k + 1), :] + ones)
        split_ref[:LANES, sources * k : sources * (k + 1)] = hi
        split_ref[LANES:, sources * k : sources * (k + 1)] = lo
    both = lax.dot_general(split_ref[...], low_ref[...], NT, preferred_element_type=f32)
    out_ref[...] = both[:ncoef, :] + both[LANES : LANES + ncoef, :]

    used = jnp.sum(jnp.where(target_ref[...] < leaves, 1.0, 0.0))
    total = jnp.sum(both[LANES - 1 : LANES, :])
    carried = jnp.logical_or(total != used, jnp.max(peak_ref[...]) >= 2.0**24)

    @pl.when(carried)
    def _():
        size, chunk = a_ref.shape
        marks = Marks(max(size, leaves), chunk)
        out_ref[...] = jnp.zeros_like(out_ref)
        for first in range(0, ops // 2 * sources, size):
            pair_ref[...] = jnp.full(pair_ref.shape, -(2.0**24), f32)

            def more(part, carry):
                for c in range(chunk // LANES):
                    op = marks.columns(operator_ref, part, c)
                    code = (op >> 1) * sources + marks.columns(source_ref, part, c) - first
                    marks.put(a_ref, c, code, jnp.where((op & 1) == 1, 8192.0, 1.0))
                    marks.put(b_ref, c, marks.columns(target_ref, part, c), jnp.ones((1, LANES), f32))
                pair_ref[...] += lax.dot_general(b_ref[...], a_ref[...], NT, preferred_element_type=f32)
                return carry

            lax.fori_loop(0, target_ref.shape[1] // chunk, more, 0)
            for lane in range(first, first + size, LANES):
                value = pair_ref[:, lane - first : lane - first + LANES]
                odd = jnp.floor(value * (1.0 / 8192.0))
                for parity, count in enumerate((value - 8192.0 * odd, odd + 2048.0)):
                    at = spot(2 * (lane // sources) + parity, ops) * sources + lane % sources
                    rows = split_ref[:, at : at + LANES].astype(f32)
                    rows = rows[:ncoef, :] + rows[LANES : LANES + ncoef, :]
                    out_ref[...] += lax.dot_general(
                        rows, count, NT, precision=lax.Precision.HIGHEST, preferred_element_type=f32
                    )


def shards(
    coords,
    charges,
    multipoles,
    operators,
    send_list,
    near_list,
    m2l_source,
    m2l_target,
    m2l_operator,
):
    ncoef, leaves = multipoles.shape
    npoints = charges.shape[0]
    near = near_list.shape[1]
    entries = m2l_source.shape[1]
    ops = operators.shape[0]
    sources = send_list.shape[1]
    peers = lax.axis_size("grp")
    f32, bf16 = jnp.float32, jnp.bfloat16

    tiles = npoints // LANES
    points = (jnp.transpose(coords.reshape(3, tiles, LANES), (1, 0, 2)), charges.reshape(tiles, LANES))
    others = (
        near_list.T,
        m2l_source,
        m2l_target,
        m2l_operator,
        jnp.transpose(operators, (1, 0, 2)).reshape(ncoef * ops, ncoef),
    )
    table, outgoing, near_list, m2l_source, m2l_target, m2l_operator, operators = pl.pallas_call(
        functools.partial(prep_kernel, others=len(others)),
        name="prep",
        out_shape=(
            pltpu.VMEM((4 * PTS, leaves), f32),
            pltpu.VMEM((sources, ncoef), f32),
            *(pltpu.VMEM(x.shape, x.dtype) for x in others),
        ),
        in_specs=[ANY] * (4 + len(others)),
        out_specs=(VMEM,) * (2 + len(others)),
        scratch_shapes=[
            pltpu.VMEM((tiles, 3, LANES), f32),
            pltpu.VMEM((tiles, LANES), f32),
            pltpu.VMEM((ncoef, leaves), f32),
            pltpu.VMEM((1, sources), jnp.int32),
            pltpu.SemaphoreType.DMA((4 + len(others),)),
        ],
        compiler_params=PARAMS,
    )(*(pltpu.with_memory_space_constraint(x, pltpu.HBM) for x in (*points, multipoles, send_list, *others)))
    received = lax.all_to_all(
        outgoing.reshape(peers, sources // peers, ncoef), "grp", split_axis=0, concat_axis=0, tiled=True
    ).reshape(sources, ncoef)
    slabs = lax.axis_size("slab")

    def exchange(start):
        partner = list(range(slabs))
        if start == 1 and slabs % 2 == 0:
            partner[0], partner[-1] = slabs - 1, 0
        for i in range(start, slabs - 1, 2):
            partner[i], partner[i + 1] = i + 1, i
        return lax.ppermute(table, "slab", list(enumerate(partner)))

    first = exchange(0)
    second = exchange(1)

    codes = ops // 4 * sources
    block = min(codes, 512)
    groups = leaves // LANES
    chunk = entries // groups
    places, parts = pl.pallas_call(
        functools.partial(cut_kernel, ops=ops),
        name="cut",
        out_shape=(
            jax.ShapeDtypeStruct((groups, near, LANES), jnp.int32),
            jax.ShapeDtypeStruct((ops * LANES, 2 * LANES), bf16),
        ),
        in_specs=[VMEM] * 2,
        out_specs=(VMEM,) * 2,
        scratch_shapes=[pltpu.VMEM((ncoef * ops, LANES), f32)],
        compiler_params=PARAMS,
    )(near_list, operators)
    near_potential, low, peak = pl.pallas_call(
        functools.partial(near_kernel, sources=sources),
        name="near_counts",
        out_shape=(
            jax.ShapeDtypeStruct((tiles, LANES), f32),
            jax.ShapeDtypeStruct((leaves, ops * sources), bf16),
            jax.ShapeDtypeStruct((8, codes), f32),
        ),
        in_specs=[VMEM] * 7,
        out_specs=(VMEM,) * 3,
        scratch_shapes=[
            pltpu.VMEM((2 * PTS, 3 * leaves), jnp.int32),
            pltpu.VMEM((PTS, 3 * leaves), f32),
            pltpu.VMEM((near, 5 * PTS, LANES), f32),
            pltpu.VMEM((groups, PTS, LANES), f32),
            pltpu.VMEM((leaves // 2, codes), f32),
            pltpu.VMEM((block, chunk), bf16),
            pltpu.VMEM((leaves // 2, chunk), bf16),
        ],
        compiler_params=PARAMS,
    )(second, table, first, places, m2l_source, m2l_target, m2l_operator)

    local_exp = pl.pallas_call(
        functools.partial(far_kernel, ops=ops),
        name="far",
        out_shape=jax.ShapeDtypeStruct((ncoef, leaves), f32),
        in_specs=[VMEM] * 7,
        out_specs=VMEM,
        scratch_shapes=[
            pltpu.VMEM((2 * LANES, ops * sources), bf16),
            pltpu.VMEM((leaves, 512), f32),
            pltpu.VMEM((512, 512), bf16),
            pltpu.VMEM((leaves, 512), bf16),
        ],
        compiler_params=PARAMS,
    )(parts, received, low, peak, m2l_source, m2l_target, m2l_operator)
    return (local_exp, near_potential.reshape(npoints))


def solution(mesh):
    both = ("slab", "grp")
    return jax.shard_map(
        shards,
        mesh=mesh,
        in_specs=(
            P(None, both),
            P(both),
            P(None, both),
            P(),
            P(both, None),
            P(both, None),
            P(both, None),
            P(both, None),
            P(both, None),
        ),
        out_specs=(P(None, both), P(both)),
        check_vma=False,
    )
```

```python
import functools

import jax
import jax.numpy as jnp
from jax import lax
from jax.experimental import pallas as pl
from jax.experimental.pallas import tpu as pltpu
from jax.sharding import PartitionSpec as P

SOFT2 = 0.0625
LANES = 128
PTS = 16
UNITS = 2.0**20
SCALE = 2.0**31
VMEM = pl.BlockSpec(memory_space=pltpu.VMEM)
ANY = pl.BlockSpec(memory_space=pl.ANY)
PARAMS = pltpu.CompilerParams(vmem_limit_bytes=48 * 1024 * 1024)
NT = (((1,), (1,)), ((), ()))


def lane_gather(x, idx):
    return jnp.take_along_axis(x, idx, axis=1, mode="promise_in_bounds")


def split(x):
    hi = x.astype(jnp.bfloat16)
    return hi, (x - hi.astype(jnp.float32)).astype(jnp.bfloat16)


def pad_lanes(x):
    return jnp.concatenate([x, jnp.zeros((x.shape[0], LANES - x.shape[1]), x.dtype)], axis=1)


def prep_kernel(coords_hbm, charges_hbm, multipoles_hbm, send_hbm, *refs, others):
    sources, refs = refs[:others], refs[others:]
    (table_ref, out_ref, *targets), refs = refs[: others + 2], refs[others + 2 :]
    coords_ref, charges_ref, multipoles_ref, send_ref, sems = refs
    pairs = (
        (coords_hbm, coords_ref),
        (charges_hbm, charges_ref),
        (send_hbm, send_ref),
        (multipoles_hbm, multipoles_ref),
        *zip(sources, targets),
    )
    copies = [pltpu.make_async_copy(src, dst, sems.at[i]) for i, (src, dst) in enumerate(pairs)]
    for copy in copies:
        copy.start()
    copies[0].wait()
    copies[1].wait()
    for c in range(4):
        rows = charges_ref[...] if c == 3 else coords_ref[:, c, :]
        cols = rows.T
        for pair in range(4):
            a = cols[32 * pair : 32 * pair + 16, :]
            b = cols[32 * pair + 16 : 32 * pair + 32, :]
            table_ref[16 * c : 16 * c + 16, LANES * pair : LANES * (pair + 1)] = jnp.concatenate([a, b], axis=1)
    copies[2].wait()
    copies[3].wait()
    ncoef, leaves = multipoles_ref.shape
    for sb in range(send_ref.shape[1] // LANES):
        send = send_ref[:, LANES * sb : LANES * (sb + 1)]
        lane = send & (LANES - 1)
        group = send >> 7
        idx = jnp.broadcast_to(lane, (ncoef, LANES))
        picked = jnp.zeros((ncoef, LANES), jnp.float32)
        for g in range(leaves // LANES):
            got = lane_gather(multipoles_ref[:, LANES * g : LANES * (g + 1)], idx)
            picked = jnp.where(group == g, got, picked)
        out_ref[LANES * sb : LANES * (sb + 1), :] = picked.T
    for copy in copies[4:]:
        copy.wait()


def cut_kernel(list_ref, operators_ref, place_ref, parts_ref, wide_ref, *, ops):
    near, leaves = list_ref.shape
    ncoef = operators_ref.shape[1]
    groups = leaves // LANES
    even = lax.axis_index("slab") % 2 == 0
    lane = lax.broadcasted_iota(jnp.int32, (near, LANES), 1)
    for g in range(groups):
        idx = 8 * (lane & 15) + 2 * g + (lane >> 6)
        part = (lane & 63) >> 4
        row = jnp.zeros((near, LANES), jnp.int32)
        for s in range(groups):
            row = jnp.where(part == s, lane_gather(list_ref[:, LANES * s : LANES * (s + 1)], idx), row)
        side = row >> 9
        side = jnp.where(even, 2 - side, side)
        place_ref[g] = (side << 9) + ((row & 7) << 6) + ((row >> 3) & 63)
    wide_ref[...] = pad_lanes(operators_ref[...])
    for op in range(ops):
        matrix = wide_ref[pl.ds(op, ncoef, stride=ops), :]
        matrix = jnp.concatenate([matrix, jnp.zeros((LANES - ncoef, LANES), jnp.float32)], axis=0)
        hi, lo = split(matrix)
        parts_ref[LANES * spot(op, ops) : LANES * (spot(op, ops) + 1), :] = jnp.concatenate([hi, lo], axis=1)


def spot(op, ops):
    return (op % 4) * (ops // 4) + op // 4


class Marks:
    def __init__(self, rows, chunk):
        self.iota = lax.broadcasted_iota(jnp.int32, (rows, LANES), 0).astype(jnp.int16).reshape(-1, 16, LANES)
        self.chunk = chunk

    def columns(self, ref, part, c):
        return ref[:, pl.ds(pl.multiple_of(part * self.chunk + c * LANES, LANES), LANES)]

    def put(self, ref, c, code, weight):
        size = ref.shape[0]
        code, weight = (
            jnp.broadcast_to(x, (16, LANES)).astype(t)[None] for x, t in ((code, jnp.int16), (weight, jnp.bfloat16))
        )
        marks = jnp.where(self.iota[: size // 16] == code, weight, jnp.zeros((1, 16, LANES), jnp.bfloat16))
        ref[:, LANES * c : LANES * (c + 1)] = marks.reshape(size, LANES)


def near_kernel(
    second_ref, own_ref, first_ref, place_ref, source_ref, target_ref, operator_ref,
    near_ref, low_ref, peak_ref,
    packed_ref, charge_ref, picked_ref, pot_ref, acc_ref, a_ref, b_ref, *, sources,
):
    groups, near, _ = place_ref.shape
    leaves = own_ref.shape[1]
    half, codes = acc_ref.shape
    block, chunk = a_ref.shape
    f32 = jnp.float32
    marks = Marks(max(block, half), chunk)

    def count(g):
        for c in range(chunk // LANES):
            leaf = marks.columns(target_ref, g, c)
            upper = leaf >= half
            leaf = jnp.where(leaf < leaves, jnp.where(upper, leaf - half, leaf), -1)
            marks.put(b_ref, c, leaf, jnp.where(upper, 4096.0, 1.0))
        for first in range(0, codes, block):
            for c in range(chunk // LANES):
                op = marks.columns(operator_ref, g, c)
                code = (op >> 2) * sources + marks.columns(source_ref, g, c) - first
                last = op & 3
                weight = jnp.where(last == 0, 1.0, jnp.where(last == 1, 8.0, jnp.where(last == 2, 64.0, 512.0)))
                marks.put(a_ref, c, code, weight)
            acc_ref[:, first : first + block] += lax.dot_general(b_ref[...], a_ref[...], NT, preferred_element_type=f32)

    acc_ref[...] = jnp.zeros_like(acc_ref)
    me = lax.axis_index("slab")
    last = lax.axis_size("slab") - 1
    from_right = me % 2 == 0
    ends = (jnp.logical_and(from_right, me == last), False, jnp.where(from_right, me == 0, me == last))
    for k, (ref, end) in enumerate(zip((first_ref, own_ref, second_ref), ends)):
        x, y, z = (
            jnp.clip(jnp.floor(ref[PTS * c : PTS * (c + 1), :] * UNITS), -UNITS, UNITS - 1.0).astype(jnp.int32)
            for c in range(3)
        )
        at = slice(leaves * k, leaves * (k + 1))
        packed_ref[:PTS, at] = (x << 11) | ((y >> 10) & 2047)
        packed_ref[PTS:, at] = (z << 11) | ((y & 1023) << 1)
        charge_ref[:, at] = jnp.where(end, 0.0, ref[3 * PTS :, :])

    def gather(place):
        idx = place & (LANES - 1)
        group = place >> 7
        refs = [packed_ref.at[8 * r : 8 * r + 8] for r in range(2 * PTS // 8)]
        refs += [charge_ref.at[8 * r : 8 * r + 8] for r in range(PTS // 8)]
        found = [lane_gather(ref[:, :LANES], idx) for ref in refs]
        for s in range(1, 3 * groups):
            here = group == s
            for r, ref in enumerate(refs):
                found[r] = jnp.where(here, lane_gather(ref[:, LANES * s : LANES * (s + 1)], idx), found[r])
        return found

    def step(g, carry):
        count(g)
        at = pl.ds(pl.multiple_of(g * LANES, LANES), LANES)
        tx, ty, tz = (own_ref[PTS * c : PTS * (c + 1), at] * SCALE for c in range(3))
        square = tx * tx + ty * ty + (tz * tz + SOFT2 * SCALE * SCALE)
        tx, ty, tz = -2.0 * tx, -2.0 * ty, -2.0 * tz
        acc = jnp.zeros((PTS, LANES), f32)
        for n in range(near):
            found = gather(jnp.broadcast_to(place_ref[g, n : n + 1, :], (8, LANES)))
            for r in range(PTS // 8):
                first, second, charge = found[r :: PTS // 8]
                x = first.astype(f32)
                y = ((first << 21) | ((second & 2047) << 10)).astype(f32)
                z = second.astype(f32)
                for k, row in enumerate((x, y, z, charge, x * x + y * y + z * z)):
                    picked_ref[n, PTS * k + 8 * r : PTS * k + 8 * r + 8, :] = row
            for p in range(PTS):
                sx, sy, sz, q, far = (picked_ref[n, PTS * c + p : PTS * c + p + 1, :] for c in range(5))
                acc += q * lax.rsqrt((square + far) + tx * sx + (ty * sy + tz * sz))
        pot_ref[g] = acc * SCALE
        return carry

    lax.fori_loop(0, groups, step, 0)
    width = LANES // 2
    pieces = []
    for g in range(groups):
        pot = pot_ref[g]
        pieces += [pot[:, :width], pot[:, width:]]
    near_ref[...] = jnp.concatenate(pieces, axis=0).T

    value = acc_ref[...]
    peak_ref[...] = jnp.max(value.reshape(-1, 8, codes), axis=0)
    value = value.astype(jnp.int32)
    for digit in range(8):
        h, d = digit // 4, digit % 4
        here = (value >> (3 * digit)) & 7
        low_ref[half * h : half * (h + 1), codes * d : codes * (d + 1)] = here.astype(f32).astype(jnp.bfloat16)


def far_kernel(
    parts_ref, received_ref, low_ref, peak_ref, source_ref, target_ref, operator_ref,
    out_ref, split_ref, pair_ref, a_ref, b_ref, *, ops,
):
    ncoef, leaves = out_ref.shape
    sources = received_ref.shape[0]
    f32 = jnp.float32
    hi, lo = split(pad_lanes(received_ref[...]))
    table = lax.dot_general(
        parts_ref[...], jnp.concatenate([hi, hi], axis=1), NT, preferred_element_type=f32
    ) + lax.dot_general(parts_ref[:, :LANES], lo, NT, preferred_element_type=f32)
    ones = jnp.where(lax.broadcasted_iota(jnp.int32, (LANES, sources), 0) == LANES - 1, 1.0, 0.0)
    for k in range(ops):
        hi, lo = split(table[LANES * k : LANES * (k + 1), :] + ones)
        split_ref[:LANES, sources * k : sources * (k + 1)] = hi
        split_ref[LANES:, sources * k : sources * (k + 1)] = lo
    both = lax.dot_general(split_ref[...], low_ref[...], NT, preferred_element_type=f32)
    out_ref[...] = both[:ncoef, :] + both[LANES : LANES + ncoef, :]

    used = jnp.sum(jnp.where(target_ref[...] < leaves, 1.0, 0.0))
    total = jnp.sum(both[LANES - 1 : LANES, :])
    carried = jnp.logical_or(total != used, jnp.max(peak_ref[...]) >= 2.0**24)

    @pl.when(carried)
    def _():
        size, chunk = a_ref.shape
        marks = Marks(max(size, leaves), chunk)
        out_ref[...] = jnp.zeros_like(out_ref)
        for first in range(0, ops // 2 * sources, size):
            pair_ref[...] = jnp.full(pair_ref.shape, -(2.0**24), f32)

            def more(part, carry):
                for c in range(chunk // LANES):
                    op = marks.columns(operator_ref, part, c)
                    code = (op >> 1) * sources + marks.columns(source_ref, part, c) - first
                    marks.put(a_ref, c, code, jnp.where((op & 1) == 1, 8192.0, 1.0))
                    marks.put(b_ref, c, marks.columns(target_ref, part, c), jnp.ones((1, LANES), f32))
                pair_ref[...] += lax.dot_general(b_ref[...], a_ref[...], NT, preferred_element_type=f32)
                return carry

            lax.fori_loop(0, target_ref.shape[1] // chunk, more, 0)
            for lane in range(first, first + size, LANES):
                value = pair_ref[:, lane - first : lane - first + LANES]
                odd = jnp.floor(value * (1.0 / 8192.0))
                for parity, count in enumerate((value - 8192.0 * odd, odd + 2048.0)):
                    at = spot(2 * (lane // sources) + parity, ops) * sources + lane % sources
                    rows = split_ref[:, at : at + LANES].astype(f32)
                    rows = rows[:ncoef, :] + rows[LANES : LANES + ncoef, :]
                    out_ref[...] += lax.dot_general(
                        rows, count, NT, precision=lax.Precision.HIGHEST, preferred_element_type=f32
                    )


def shards(
    coords,
    charges,
    multipoles,
    operators,
    send_list,
    near_list,
    m2l_source,
    m2l_target,
    m2l_operator,
):
    ncoef, leaves = multipoles.shape
    npoints = charges.shape[0]
    near = near_list.shape[1]
    entries = m2l_source.shape[1]
    ops = operators.shape[0]
    sources = send_list.shape[1]
    peers = lax.axis_size("grp")
    f32, bf16 = jnp.float32, jnp.bfloat16

    tiles = npoints // LANES
    points = (jnp.transpose(coords.reshape(3, tiles, LANES), (1, 0, 2)), charges.reshape(tiles, LANES))
    others = (
        near_list.T,
        m2l_source,
        m2l_target,
        m2l_operator,
        jnp.transpose(operators, (1, 0, 2)).reshape(ncoef * ops, ncoef),
    )
    table, outgoing, near_list, m2l_source, m2l_target, m2l_operator, operators = pl.pallas_call(
        functools.partial(prep_kernel, others=len(others)),
        name="prep",
        out_shape=(
            pltpu.VMEM((4 * PTS, leaves), f32),
            pltpu.VMEM((sources, ncoef), f32),
            *(pltpu.VMEM(x.shape, x.dtype) for x in others),
        ),
        in_specs=[ANY] * (4 + len(others)),
        out_specs=(VMEM,) * (2 + len(others)),
        scratch_shapes=[
            pltpu.VMEM((tiles, 3, LANES), f32),
            pltpu.VMEM((tiles, LANES), f32),
            pltpu.VMEM((ncoef, leaves), f32),
            pltpu.VMEM((1, sources), jnp.int32),
            pltpu.SemaphoreType.DMA((4 + len(others),)),
        ],
        compiler_params=PARAMS,
    )(*(pltpu.with_memory_space_constraint(x, pltpu.HBM) for x in (*points, multipoles, send_list, *others)))
    received = lax.all_to_all(
        outgoing.reshape(peers, sources // peers, ncoef), "grp", split_axis=0, concat_axis=0, tiled=True
    ).reshape(sources, ncoef)
    slabs = lax.axis_size("slab")

    def exchange(start):
        to = {}
        for slab in range(slabs):
            other = slab + 1 if (slab - start) % 2 == 0 else slab - 1
            for peer in range(peers):
                if 0 <= other < slabs:
                    to[slab * peers + peer] = other * peers + peer
                else:
                    to[slab * peers + peer] = slab * peers + min(peer ^ 1, peers - 1)
        return lax.ppermute(table, ("slab", "grp"), sorted(to.items()))

    first = exchange(0)
    second = exchange(1)

    codes = ops // 4 * sources
    block = min(codes, 512)
    groups = leaves // LANES
    chunk = entries // groups
    places, parts = pl.pallas_call(
        functools.partial(cut_kernel, ops=ops),
        name="cut",
        out_shape=(
            jax.ShapeDtypeStruct((groups, near, LANES), jnp.int32),
            jax.ShapeDtypeStruct((ops * LANES, 2 * LANES), bf16),
        ),
        in_specs=[VMEM] * 2,
        out_specs=(VMEM,) * 2,
        scratch_shapes=[pltpu.VMEM((ncoef * ops, LANES), f32)],
        compiler_params=PARAMS,
    )(near_list, operators)
    near_potential, low, peak = pl.pallas_call(
        functools.partial(near_kernel, sources=sources),
        name="near_counts",
        out_shape=(
            jax.ShapeDtypeStruct((tiles, LANES), f32),
            jax.ShapeDtypeStruct((leaves, ops * sources), bf16),
            jax.ShapeDtypeStruct((8, codes), f32),
        ),
        in_specs=[VMEM] * 7,
        out_specs=(VMEM,) * 3,
        scratch_shapes=[
            pltpu.VMEM((2 * PTS, 3 * leaves), jnp.int32),
            pltpu.VMEM((PTS, 3 * leaves), f32),
            pltpu.VMEM((near, 5 * PTS, LANES), f32),
            pltpu.VMEM((groups, PTS, LANES), f32),
            pltpu.VMEM((leaves // 2, codes), f32),
            pltpu.VMEM((block, chunk), bf16),
            pltpu.VMEM((leaves // 2, chunk), bf16),
        ],
        compiler_params=PARAMS,
    )(second, table, first, places, m2l_source, m2l_target, m2l_operator)

    local_exp = pl.pallas_call(
        functools.partial(far_kernel, ops=ops),
        name="far",
        out_shape=jax.ShapeDtypeStruct((ncoef, leaves), f32),
        in_specs=[VMEM] * 7,
        out_specs=VMEM,
        scratch_shapes=[
            pltpu.VMEM((2 * LANES, ops * sources), bf16),
            pltpu.VMEM((leaves, 512), f32),
            pltpu.VMEM((512, 512), bf16),
            pltpu.VMEM((leaves, 512), bf16),
        ],
        compiler_params=PARAMS,
    )(parts, received, low, peak, m2l_source, m2l_target, m2l_operator)
    return (local_exp, near_potential.reshape(npoints))


def solution(mesh):
    both = ("slab", "grp")
    return jax.shard_map(
        shards,
        mesh=mesh,
        in_specs=(
            P(None, both),
            P(both),
            P(None, both),
            P(),
            P(both, None),
            P(both, None),
            P(both, None),
            P(both, None),
            P(both, None),
        ),
        out_specs=(P(None, both), P(both)),
        check_vma=False,
    )
```

```python
import functools

import jax
import jax.numpy as jnp
from jax import lax
from jax.experimental import pallas as pl
from jax.experimental.pallas import tpu as pltpu
from jax.sharding import PartitionSpec as P

SOFT2 = 0.0625
LANES = 128
PTS = 16
UNITS = 2.0**20
SCALE = 2.0**31
VMEM = pl.BlockSpec(memory_space=pltpu.VMEM)
ANY = pl.BlockSpec(memory_space=pl.ANY)
PARAMS = pltpu.CompilerParams(vmem_limit_bytes=48 * 1024 * 1024)
NT = (((1,), (1,)), ((), ()))


def lane_gather(x, idx):
    return jnp.take_along_axis(x, idx, axis=1, mode="promise_in_bounds")


def split(x):
    hi = x.astype(jnp.bfloat16)
    return hi, (x - hi.astype(jnp.float32)).astype(jnp.bfloat16)


def pad_lanes(x):
    return jnp.concatenate([x, jnp.zeros((x.shape[0], LANES - x.shape[1]), x.dtype)], axis=1)


def prep_kernel(coords_hbm, charges_hbm, multipoles_hbm, send_hbm, *refs, others, cap):
    sources, refs = refs[:others], refs[others:]
    (table_ref, same_ref, other_ref, *targets), refs = refs[: others + 3], refs[others + 3 :]
    coords_ref, charges_ref, multipoles_ref, send_ref, rows_ref, sems = refs
    pairs = (
        (coords_hbm, coords_ref),
        (charges_hbm, charges_ref),
        (send_hbm, send_ref),
        (multipoles_hbm, multipoles_ref),
        *zip(sources, targets),
    )
    copies = [pltpu.make_async_copy(src, dst, sems.at[i]) for i, (src, dst) in enumerate(pairs)]
    for copy in copies:
        copy.start()
    copies[0].wait()
    copies[1].wait()
    for c in range(4):
        rows = charges_ref[...] if c == 3 else coords_ref[:, c, :]
        cols = rows.T
        for pair in range(4):
            a = cols[32 * pair : 32 * pair + 16, :]
            b = cols[32 * pair + 16 : 32 * pair + 32, :]
            table_ref[16 * c : 16 * c + 16, LANES * pair : LANES * (pair + 1)] = jnp.concatenate([a, b], axis=1)
    copies[2].wait()
    copies[3].wait()
    ncoef, leaves = multipoles_ref.shape
    for sb in range(send_ref.shape[1] // LANES):
        send = send_ref[:, LANES * sb : LANES * (sb + 1)]
        lane = send & (LANES - 1)
        group = send >> 7
        idx = jnp.broadcast_to(lane, (ncoef, LANES))
        picked = jnp.zeros((ncoef, LANES), jnp.float32)
        for g in range(leaves // LANES):
            got = lane_gather(multipoles_ref[:, LANES * g : LANES * (g + 1)], idx)
            picked = jnp.where(group == g, got, picked)
        rows_ref[LANES * sb : LANES * (sb + 1), :] = picked.T
    side = lax.axis_index("grp") % 2 if cap else 0
    count = rows_ref.shape[0] // cap if cap else 0
    for k in range(count // 2):
        for ref, peer in ((same_ref, 2 * k + side), (other_ref, 2 * k + 1 - side)):
            ref[cap * k : cap * (k + 1), :] = rows_ref[pl.ds(pl.multiple_of(peer * cap, cap), cap), :]
    if not cap:
        same_ref[...] = rows_ref[: same_ref.shape[0], :]
        other_ref[...] = rows_ref[same_ref.shape[0] :, :]
    for copy in copies[4:]:
        copy.wait()


def join_kernel(out_ref, came_ref, *join_refs, cap):
    chip = lax.axis_index("grp") // 2
    for m, ref in enumerate(join_refs):
        at = pl.ds(pl.multiple_of((chip ^ m) * cap, cap), cap)
        ref[:cap, :] = out_ref[at, :]
        ref[cap:, :] = came_ref[at, :]


def placed(join_refs, rows_ref, cap):
    me = lax.axis_index("grp")
    for m, ref in enumerate(join_refs):
        peer = me ^ (2 * m)
        rows_ref[pl.ds(pl.multiple_of(peer * cap, cap), cap), :] = ref[:cap, :]
        rows_ref[pl.ds(pl.multiple_of((peer ^ 1) * cap, cap), cap), :] = ref[cap:, :]


def cut_kernel(list_ref, operators_ref, place_ref, parts_ref, wide_ref, *, ops):
    near, leaves = list_ref.shape
    ncoef = operators_ref.shape[1]
    groups = leaves // LANES
    even = lax.axis_index("slab") % 2 == 0
    lane = lax.broadcasted_iota(jnp.int32, (near, LANES), 1)
    for g in range(groups):
        idx = 8 * (lane & 15) + 2 * g + (lane >> 6)
        part = (lane & 63) >> 4
        row = jnp.zeros((near, LANES), jnp.int32)
        for s in range(groups):
            row = jnp.where(part == s, lane_gather(list_ref[:, LANES * s : LANES * (s + 1)], idx), row)
        side = row >> 9
        side = jnp.where(even, 2 - side, side)
        place_ref[g] = (side << 9) + ((row & 7) << 6) + ((row >> 3) & 63)
    wide_ref[...] = pad_lanes(operators_ref[...])
    for op in range(ops):
        matrix = wide_ref[pl.ds(op, ncoef, stride=ops), :]
        matrix = jnp.concatenate([matrix, jnp.zeros((LANES - ncoef, LANES), jnp.float32)], axis=0)
        hi, lo = split(matrix)
        parts_ref[LANES * spot(op, ops) : LANES * (spot(op, ops) + 1), :] = jnp.concatenate([hi, lo], axis=1)


def spot(op, ops):
    return (op % 4) * (ops // 4) + op // 4


class Marks:
    def __init__(self, rows, chunk):
        self.iota = lax.broadcasted_iota(jnp.int32, (rows, LANES), 0).astype(jnp.int16).reshape(-1, 16, LANES)
        self.chunk = chunk

    def columns(self, ref, part, c):
        return ref[:, pl.ds(pl.multiple_of(part * self.chunk + c * LANES, LANES), LANES)]

    def put(self, ref, c, code, weight):
        size = ref.shape[0]
        code, weight = (
            jnp.broadcast_to(x, (16, LANES)).astype(t)[None] for x, t in ((code, jnp.int16), (weight, jnp.bfloat16))
        )
        marks = jnp.where(self.iota[: size // 16] == code, weight, jnp.zeros((1, 16, LANES), jnp.bfloat16))
        ref[:, LANES * c : LANES * (c + 1)] = marks.reshape(size, LANES)


def near_kernel(
    second_ref, own_ref, first_ref, place_ref, source_ref, target_ref, operator_ref,
    near_ref, low_ref, peak_ref,
    packed_ref, charge_ref, picked_ref, pot_ref, acc_ref, a_ref, b_ref, *, sources,
):
    groups, near, _ = place_ref.shape
    leaves = own_ref.shape[1]
    half, codes = acc_ref.shape
    block, chunk = a_ref.shape
    f32 = jnp.float32
    marks = Marks(max(block, half), chunk)

    def count(g):
        for c in range(chunk // LANES):
            leaf = marks.columns(target_ref, g, c)
            upper = leaf >= half
            leaf = jnp.where(leaf < leaves, jnp.where(upper, leaf - half, leaf), -1)
            marks.put(b_ref, c, leaf, jnp.where(upper, 4096.0, 1.0))
        for first in range(0, codes, block):
            for c in range(chunk // LANES):
                op = marks.columns(operator_ref, g, c)
                code = (op >> 2) * sources + marks.columns(source_ref, g, c) - first
                last = op & 3
                weight = jnp.where(last == 0, 1.0, jnp.where(last == 1, 8.0, jnp.where(last == 2, 64.0, 512.0)))
                marks.put(a_ref, c, code, weight)
            acc_ref[:, first : first + block] += lax.dot_general(b_ref[...], a_ref[...], NT, preferred_element_type=f32)

    acc_ref[...] = jnp.zeros_like(acc_ref)
    me = lax.axis_index("slab")
    last = lax.axis_size("slab") - 1
    from_right = me % 2 == 0
    ends = (jnp.logical_and(from_right, me == last), False, jnp.where(from_right, me == 0, me == last))
    for k, (ref, end) in enumerate(zip((first_ref, own_ref, second_ref), ends)):
        x, y, z = (
            jnp.clip(jnp.floor(ref[PTS * c : PTS * (c + 1), :] * UNITS), -UNITS, UNITS - 1.0).astype(jnp.int32)
            for c in range(3)
        )
        at = slice(leaves * k, leaves * (k + 1))
        packed_ref[:PTS, at] = (x << 11) | ((y >> 10) & 2047)
        packed_ref[PTS:, at] = (z << 11) | ((y & 1023) << 1)
        charge_ref[:, at] = jnp.where(end, 0.0, ref[3 * PTS :, :])

    def gather(place):
        idx = place & (LANES - 1)
        group = place >> 7
        refs = [packed_ref.at[8 * r : 8 * r + 8] for r in range(2 * PTS // 8)]
        refs += [charge_ref.at[8 * r : 8 * r + 8] for r in range(PTS // 8)]
        found = [lane_gather(ref[:, :LANES], idx) for ref in refs]
        for s in range(1, 3 * groups):
            here = group == s
            for r, ref in enumerate(refs):
                found[r] = jnp.where(here, lane_gather(ref[:, LANES * s : LANES * (s + 1)], idx), found[r])
        return found

    def step(g, carry):
        count(g)
        at = pl.ds(pl.multiple_of(g * LANES, LANES), LANES)
        tx, ty, tz = (own_ref[PTS * c : PTS * (c + 1), at] * SCALE for c in range(3))
        square = tx * tx + ty * ty + (tz * tz + SOFT2 * SCALE * SCALE)
        tx, ty, tz = -2.0 * tx, -2.0 * ty, -2.0 * tz
        acc = jnp.zeros((PTS, LANES), f32)
        for n in range(near):
            found = gather(jnp.broadcast_to(place_ref[g, n : n + 1, :], (8, LANES)))
            for r in range(PTS // 8):
                first, second, charge = found[r :: PTS // 8]
                x = first.astype(f32)
                y = ((first << 21) | ((second & 2047) << 10)).astype(f32)
                z = second.astype(f32)
                for k, row in enumerate((x, y, z, charge, x * x + y * y + z * z)):
                    picked_ref[n, PTS * k + 8 * r : PTS * k + 8 * r + 8, :] = row
            for p in range(PTS):
                sx, sy, sz, q, far = (picked_ref[n, PTS * c + p : PTS * c + p + 1, :] for c in range(5))
                acc += q * lax.rsqrt((square + far) + tx * sx + (ty * sy + tz * sz))
        pot_ref[g] = acc * SCALE
        return carry

    lax.fori_loop(0, groups, step, 0)
    width = LANES // 2
    pieces = []
    for g in range(groups):
        pot = pot_ref[g]
        pieces += [pot[:, :width], pot[:, width:]]
    near_ref[...] = jnp.concatenate(pieces, axis=0).T

    value = acc_ref[...]
    peak_ref[...] = jnp.max(value.reshape(-1, 8, codes), axis=0)
    value = value.astype(jnp.int32)
    for digit in range(8):
        h, d = digit // 4, digit % 4
        here = (value >> (3 * digit)) & 7
        low_ref[half * h : half * (h + 1), codes * d : codes * (d + 1)] = here.astype(f32).astype(jnp.bfloat16)


def far_kernel(
    parts_ref, low_ref, peak_ref, source_ref, target_ref, operator_ref, *refs, ops, cap,
):
    *join_refs, out_ref, received_ref, split_ref, pair_ref, a_ref, b_ref = refs
    if cap:
        placed(join_refs, received_ref, cap)
    else:
        received_ref = join_refs[0]
    ncoef, leaves = out_ref.shape
    sources = received_ref.shape[0]
    f32 = jnp.float32
    hi, lo = split(pad_lanes(received_ref[...]))
    table = lax.dot_general(
        parts_ref[...], jnp.concatenate([hi, hi], axis=1), NT, preferred_element_type=f32
    ) + lax.dot_general(parts_ref[:, :LANES], lo, NT, preferred_element_type=f32)
    ones = jnp.where(lax.broadcasted_iota(jnp.int32, (LANES, sources), 0) == LANES - 1, 1.0, 0.0)
    for k in range(ops):
        hi, lo = split(table[LANES * k : LANES * (k + 1), :] + ones)
        split_ref[:LANES, sources * k : sources * (k + 1)] = hi
        split_ref[LANES:, sources * k : sources * (k + 1)] = lo
    both = lax.dot_general(split_ref[...], low_ref[...], NT, preferred_element_type=f32)
    out_ref[...] = both[:ncoef, :] + both[LANES : LANES + ncoef, :]

    used = jnp.sum(jnp.where(target_ref[...] < leaves, 1.0, 0.0))
    total = jnp.sum(both[LANES - 1 : LANES, :])
    carried = jnp.logical_or(total != used, jnp.max(peak_ref[...]) >= 2.0**24)

    @pl.when(carried)
    def _():
        size, chunk = a_ref.shape
        marks = Marks(max(size, leaves), chunk)
        out_ref[...] = jnp.zeros_like(out_ref)
        for first in range(0, ops // 2 * sources, size):
            pair_ref[...] = jnp.full(pair_ref.shape, -(2.0**24), f32)

            def more(part, carry):
                for c in range(chunk // LANES):
                    op = marks.columns(operator_ref, part, c)
                    code = (op >> 1) * sources + marks.columns(source_ref, part, c) - first
                    marks.put(a_ref, c, code, jnp.where((op & 1) == 1, 8192.0, 1.0))
                    marks.put(b_ref, c, marks.columns(target_ref, part, c), jnp.ones((1, LANES), f32))
                pair_ref[...] += lax.dot_general(b_ref[...], a_ref[...], NT, preferred_element_type=f32)
                return carry

            lax.fori_loop(0, target_ref.shape[1] // chunk, more, 0)
            for lane in range(first, first + size, LANES):
                value = pair_ref[:, lane - first : lane - first + LANES]
                odd = jnp.floor(value * (1.0 / 8192.0))
                for parity, count in enumerate((value - 8192.0 * odd, odd + 2048.0)):
                    at = spot(2 * (lane // sources) + parity, ops) * sources + lane % sources
                    rows = split_ref[:, at : at + LANES].astype(f32)
                    rows = rows[:ncoef, :] + rows[LANES : LANES + ncoef, :]
                    out_ref[...] += lax.dot_general(
                        rows, count, NT, precision=lax.Precision.HIGHEST, preferred_element_type=f32
                    )


def shards(
    coords,
    charges,
    multipoles,
    operators,
    send_list,
    near_list,
    m2l_source,
    m2l_target,
    m2l_operator,
):
    ncoef, leaves = multipoles.shape
    npoints = charges.shape[0]
    near = near_list.shape[1]
    entries = m2l_source.shape[1]
    ops = operators.shape[0]
    sources = send_list.shape[1]
    peers = lax.axis_size("grp")
    f32, bf16 = jnp.float32, jnp.bfloat16

    tiles = npoints // LANES
    cap = sources // peers if peers == 8 else 0
    points = (jnp.transpose(coords.reshape(3, tiles, LANES), (1, 0, 2)), charges.reshape(tiles, LANES))
    others = (
        near_list.T,
        m2l_source,
        m2l_target,
        m2l_operator,
        jnp.transpose(operators, (1, 0, 2)).reshape(ncoef * ops, ncoef),
    )
    table, same, other, near_list, m2l_source, m2l_target, m2l_operator, operators = pl.pallas_call(
        functools.partial(prep_kernel, others=len(others), cap=cap),
        name="prep",
        out_shape=(
            pltpu.VMEM((4 * PTS, leaves), f32),
            pltpu.VMEM((sources // 2, ncoef), f32),
            pltpu.VMEM((sources // 2, ncoef), f32),
            *(pltpu.VMEM(x.shape, x.dtype) for x in others),
        ),
        in_specs=[ANY] * (4 + len(others)),
        out_specs=(VMEM,) * (3 + len(others)),
        scratch_shapes=[
            pltpu.VMEM((tiles, 3, LANES), f32),
            pltpu.VMEM((tiles, LANES), f32),
            pltpu.VMEM((ncoef, leaves), f32),
            pltpu.VMEM((1, sources), jnp.int32),
            pltpu.VMEM((sources, ncoef), f32),
            pltpu.SemaphoreType.DMA((4 + len(others),)),
        ],
        compiler_params=PARAMS,
    )(*(pltpu.with_memory_space_constraint(x, pltpu.HBM) for x in (*points, multipoles, send_list, *others)))
    if cap:
        came = lax.ppermute(other, "grp", [(i, i ^ 1) for i in range(peers)])
        joins = pl.pallas_call(
            functools.partial(join_kernel, cap=cap),
            name="join",
            out_shape=(jax.ShapeDtypeStruct((2 * cap, ncoef), f32),) * (peers // 2),
            in_specs=[VMEM] * 2,
            out_specs=(VMEM,) * (peers // 2),
            compiler_params=PARAMS,
        )(same, came)
        received = [joins[0]] + [
            lax.ppermute(joins[m], "grp", [(i, i ^ (2 * m)) for i in range(peers)]) for m in range(1, peers // 2)
        ]
    else:
        received = [
            lax.all_to_all(
                jnp.concatenate([same, other]).reshape(peers, sources // peers, ncoef), "grp", split_axis=0, concat_axis=0, tiled=True
            ).reshape(sources, ncoef)
        ]
    slabs = lax.axis_size("slab")

    def exchange(start):
        to = {}
        for slab in range(slabs):
            other = slab + 1 if (slab - start) % 2 == 0 else slab - 1
            for peer in range(peers):
                if 0 <= other < slabs:
                    to[slab * peers + peer] = other * peers + peer
                else:
                    to[slab * peers + peer] = slab * peers + min(peer ^ 1, peers - 1)
        return lax.ppermute(table, ("slab", "grp"), sorted(to.items()))

    first = exchange(0)
    second = exchange(1)

    codes = ops // 4 * sources
    block = min(codes, 512)
    groups = leaves // LANES
    chunk = entries // groups
    places, parts = pl.pallas_call(
        functools.partial(cut_kernel, ops=ops),
        name="cut",
        out_shape=(
            jax.ShapeDtypeStruct((groups, near, LANES), jnp.int32),
            jax.ShapeDtypeStruct((ops * LANES, 2 * LANES), bf16),
        ),
        in_specs=[VMEM] * 2,
        out_specs=(VMEM,) * 2,
        scratch_shapes=[pltpu.VMEM((ncoef * ops, LANES), f32)],
        compiler_params=PARAMS,
    )(near_list, operators)
    near_potential, low, peak = pl.pallas_call(
        functools.partial(near_kernel, sources=sources),
        name="near_counts",
        out_shape=(
            jax.ShapeDtypeStruct((tiles, LANES), f32),
            jax.ShapeDtypeStruct((leaves, ops * sources), bf16),
            jax.ShapeDtypeStruct((8, codes), f32),
        ),
        in_specs=[VMEM] * 7,
        out_specs=(VMEM,) * 3,
        scratch_shapes=[
            pltpu.VMEM((2 * PTS, 3 * leaves), jnp.int32),
            pltpu.VMEM((PTS, 3 * leaves), f32),
            pltpu.VMEM((near, 5 * PTS, LANES), f32),
            pltpu.VMEM((groups, PTS, LANES), f32),
            pltpu.VMEM((leaves // 2, codes), f32),
            pltpu.VMEM((block, chunk), bf16),
            pltpu.VMEM((leaves // 2, chunk), bf16),
        ],
        compiler_params=PARAMS,
    )(second, table, first, places, m2l_source, m2l_target, m2l_operator)

    local_exp = pl.pallas_call(
        functools.partial(far_kernel, ops=ops, cap=cap),
        name="far",
        out_shape=jax.ShapeDtypeStruct((ncoef, leaves), f32),
        in_specs=[VMEM] * (6 + len(received)),
        out_specs=VMEM,
        scratch_shapes=[
            pltpu.VMEM((sources, ncoef), f32),
            pltpu.VMEM((2 * LANES, ops * sources), bf16),
            pltpu.VMEM((leaves, 512), f32),
            pltpu.VMEM((512, 512), bf16),
            pltpu.VMEM((leaves, 512), bf16),
        ],
        compiler_params=PARAMS,
    )(parts, low, peak, m2l_source, m2l_target, m2l_operator, *received)
    return (local_exp, near_potential.reshape(npoints))


def solution(mesh):
    both = ("slab", "grp")
    return jax.shard_map(
        shards,
        mesh=mesh,
        in_specs=(
            P(None, both),
            P(both),
            P(None, both),
            P(),
            P(both, None),
            P(both, None),
            P(both, None),
            P(both, None),
            P(both, None),
        ),
        out_specs=(P(None, both), P(both)),
        check_vma=False,
    )
```

```python
import functools

import jax
import jax.numpy as jnp
from jax import lax
from jax.experimental import pallas as pl
from jax.experimental.pallas import tpu as pltpu
from jax.sharding import PartitionSpec as P

SOFT2 = 0.0625
LANES = 128
PTS = 16
UNITS = 2.0**20
SCALE = 2.0**31
VMEM = pl.BlockSpec(memory_space=pltpu.VMEM)
ANY = pl.BlockSpec(memory_space=pl.ANY)
PARAMS = pltpu.CompilerParams(vmem_limit_bytes=48 * 1024 * 1024)
NT = (((1,), (1,)), ((), ()))


def lane_gather(x, idx):
    return jnp.take_along_axis(x, idx, axis=1, mode="promise_in_bounds")


def split(x):
    hi = x.astype(jnp.bfloat16)
    return hi, (x - hi.astype(jnp.float32)).astype(jnp.bfloat16)


def pad_lanes(x):
    return jnp.concatenate([x, jnp.zeros((x.shape[0], LANES - x.shape[1]), x.dtype)], axis=1)


def prep_kernel(coords_hbm, charges_hbm, multipoles_hbm, send_hbm, *refs, others, cap):
    sources, refs = refs[:others], refs[others:]
    (table_ref, same_ref, other_ref, *targets), refs = refs[: others + 3], refs[others + 3 :]
    coords_ref, charges_ref, multipoles_ref, send_ref, rows_ref, sems = refs
    pairs = (
        (coords_hbm, coords_ref),
        (charges_hbm, charges_ref),
        (send_hbm, send_ref),
        (multipoles_hbm, multipoles_ref),
        *zip(sources, targets),
    )
    copies = [pltpu.make_async_copy(src, dst, sems.at[i]) for i, (src, dst) in enumerate(pairs)]
    for copy in copies:
        copy.start()
    copies[0].wait()
    copies[1].wait()
    for c in range(4):
        rows = charges_ref[...] if c == 3 else coords_ref[:, c, :]
        cols = rows.T
        for pair in range(4):
            a = cols[32 * pair : 32 * pair + 16, :]
            b = cols[32 * pair + 16 : 32 * pair + 32, :]
            table_ref[16 * c : 16 * c + 16, LANES * pair : LANES * (pair + 1)] = jnp.concatenate([a, b], axis=1)
    copies[2].wait()
    copies[3].wait()
    ncoef, leaves = multipoles_ref.shape
    for sb in range(send_ref.shape[1] // LANES):
        send = send_ref[:, LANES * sb : LANES * (sb + 1)]
        lane = send & (LANES - 1)
        group = send >> 7
        idx = jnp.broadcast_to(lane, (ncoef, LANES))
        picked = jnp.zeros((ncoef, LANES), jnp.float32)
        for g in range(leaves // LANES):
            got = lane_gather(multipoles_ref[:, LANES * g : LANES * (g + 1)], idx)
            picked = jnp.where(group == g, got, picked)
        rows_ref[LANES * sb : LANES * (sb + 1), :] = picked.T
    side = lax.axis_index("grp") % 2 if cap else 0
    count = rows_ref.shape[0] // cap if cap else 0
    for k in range(count // 2):
        for ref, peer in ((same_ref, 2 * k + side), (other_ref, 2 * k + 1 - side)):
            ref[cap * k : cap * (k + 1), :] = rows_ref[pl.ds(pl.multiple_of(peer * cap, cap), cap), :]
    if not cap:
        same_ref[...] = rows_ref[: same_ref.shape[0], :]
        other_ref[...] = rows_ref[same_ref.shape[0] :, :]
    for copy in copies[4:]:
        copy.wait()


def join_kernel(out_ref, came_ref, peak_ref, *join_refs, cap):
    del peak_ref
    chip = lax.axis_index("grp") // 2
    for m, ref in enumerate(join_refs):
        at = pl.ds(pl.multiple_of((chip ^ m) * cap, cap), cap)
        ref[:cap, :] = out_ref[at, :]
        ref[cap:, :] = came_ref[at, :]


def placed(join_refs, rows_ref, cap):
    me = lax.axis_index("grp")
    for m, ref in enumerate(join_refs):
        peer = me ^ (2 * m)
        rows_ref[pl.ds(pl.multiple_of(peer * cap, cap), cap), :] = ref[:cap, :]
        rows_ref[pl.ds(pl.multiple_of((peer ^ 1) * cap, cap), cap), :] = ref[cap:, :]


def counts_kernel(
    list_ref, operators_ref, source_ref, target_ref, operator_ref, place_ref, parts_ref, low_ref, peak_ref,
    wide_ref, code_ref, weight_ref, acc_ref, a_ref, b_ref, *, ops, sources,
):
    near, leaves = list_ref.shape
    ncoef = operators_ref.shape[1]
    groups = leaves // LANES
    half, codes = acc_ref.shape
    _, block, chunk = a_ref.shape
    f32 = jnp.float32
    even = lax.axis_index("slab") % 2 == 0
    lane = lax.broadcasted_iota(jnp.int32, (near, LANES), 1)
    for g in range(groups):
        idx = 8 * (lane & 15) + 2 * g + (lane >> 6)
        part = (lane & 63) >> 4
        row = jnp.zeros((near, LANES), jnp.int32)
        for s in range(groups):
            row = jnp.where(part == s, lane_gather(list_ref[:, LANES * s : LANES * (s + 1)], idx), row)
        side = row >> 9
        side = jnp.where(even, 2 - side, side)
        place_ref[g] = (side << 9) + ((row & 7) << 6) + ((row >> 3) & 63)

    leaf, op = target_ref[...], operator_ref[...]
    upper = leaf >= half
    code_ref[0] = (op >> 2) * sources + source_ref[...]
    weight_ref[0] = (1 << (3 * (op & 3))).astype(f32)
    code_ref[1] = jnp.where(leaf < leaves, jnp.where(upper, leaf - half, leaf), -1)
    weight_ref[1] = jnp.where(upper, 4096.0, 1.0)
    marks = Marks(max(block, half))
    for part in range(target_ref.shape[0] * LANES // chunk):
        turn = part % 2
        for c in range(chunk // LANES):
            at = slice(part * (chunk // LANES) + c, part * (chunk // LANES) + c + 1)
            marks.put(b_ref.at[turn], c, code_ref[1, at, :], weight_ref[1, at, :])
        for first in range(0, codes, block):
            for c in range(chunk // LANES):
                at = slice(part * (chunk // LANES) + c, part * (chunk // LANES) + c + 1)
                marks.put(a_ref.at[turn], c, code_ref[0, at, :] - first, weight_ref[0, at, :])
            product = lax.dot_general(b_ref[turn], a_ref[turn], NT, preferred_element_type=f32)
            if part == 0:
                acc_ref[:, first : first + block] = product
            else:
                acc_ref[:, first : first + block] += product

    wide_ref[...] = pad_lanes(operators_ref[...])
    for op in range(ops):
        matrix = wide_ref[pl.ds(op, ncoef, stride=ops), :]
        matrix = jnp.concatenate([matrix, jnp.zeros((LANES - ncoef, LANES), f32)], axis=0)
        hi, lo = split(matrix)
        parts_ref[LANES * spot(op, ops) : LANES * (spot(op, ops) + 1), :] = jnp.concatenate([hi, lo], axis=1)

    value = acc_ref[...]
    peak_ref[...] = jnp.max(value.reshape(-1, 8, codes), axis=0)
    value = value.astype(jnp.int32)
    for digit in range(8):
        h, d = digit // 4, digit % 4
        here = (value >> (3 * digit)) & 7
        low_ref[half * h : half * (h + 1), codes * d : codes * (d + 1)] = here.astype(f32).astype(jnp.bfloat16)


def spot(op, ops):
    return (op % 4) * (ops // 4) + op // 4


class Marks:
    def __init__(self, rows):
        self.iota = lax.broadcasted_iota(jnp.int32, (rows, LANES), 0).astype(jnp.int16).reshape(-1, 16, LANES)

    def put(self, ref, c, code, weight):
        size = ref.shape[0]
        code, weight = (
            jnp.broadcast_to(x, (16, LANES)).astype(t)[None] for x, t in ((code, jnp.int16), (weight, jnp.bfloat16))
        )
        marks = jnp.where(self.iota[: size // 16] == code, weight, jnp.zeros((1, 16, LANES), jnp.bfloat16))
        ref[:, LANES * c : LANES * (c + 1)] = marks.reshape(size, LANES)


def near_kernel(
    first_ref, own_ref, second_ref, place_ref, near_ref, packed_ref, charge_ref, picked_ref, pot_ref
):
    groups, near, _ = place_ref.shape
    leaves = own_ref.shape[1]
    f32 = jnp.float32
    me = lax.axis_index("slab")
    last = lax.axis_size("slab") - 1
    from_right = me % 2 == 0
    ends = (jnp.logical_and(from_right, me == last), False, jnp.where(from_right, me == 0, me == last))
    for k, (ref, end) in enumerate(zip((first_ref, own_ref, second_ref), ends)):
        x, y, z = (
            jnp.minimum(jnp.floor(ref[PTS * c : PTS * (c + 1), :] * UNITS), UNITS - 1.0).astype(jnp.int32)
            for c in range(3)
        )
        at = slice(leaves * k, leaves * (k + 1))
        packed_ref[:PTS, at] = (x << 11) | ((y >> 10) & 2047)
        packed_ref[PTS:, at] = (z << 11) | ((y & 1023) << 1)
        charge_ref[:, at] = jnp.where(end, 0.0, ref[3 * PTS :, :])

    def gather(place):
        idx = place & (LANES - 1)
        group = place >> 7
        refs = [packed_ref.at[8 * r : 8 * r + 8] for r in range(2 * PTS // 8)]
        refs += [charge_ref.at[8 * r : 8 * r + 8] for r in range(PTS // 8)]
        found = [lane_gather(ref[:, :LANES], idx) for ref in refs]
        for s in range(1, 3 * groups):
            here = group == s
            for r, ref in enumerate(refs):
                found[r] = jnp.where(here, lane_gather(ref[:, LANES * s : LANES * (s + 1)], idx), found[r])
        return found

    def step(g, carry):
        at = pl.ds(pl.multiple_of(g * LANES, LANES), LANES)
        tx, ty, tz = (own_ref[PTS * c : PTS * (c + 1), at] * SCALE for c in range(3))
        square = tx * tx + ty * ty + (tz * tz + SOFT2 * SCALE * SCALE)
        tx, ty, tz = -2.0 * tx, -2.0 * ty, -2.0 * tz
        acc = jnp.zeros((PTS, LANES), f32)
        for n in range(near):
            found = gather(jnp.broadcast_to(place_ref[g, n : n + 1, :], (8, LANES)))
            for r in range(PTS // 8):
                first, second, charge = found[r :: PTS // 8]
                x = first.astype(f32)
                y = ((first << 21) | ((second & 2047) << 10)).astype(f32)
                z = second.astype(f32)
                for k, row in enumerate((x, y, z, charge, x * x + y * y + z * z)):
                    picked_ref[n, PTS * k + 8 * r : PTS * k + 8 * r + 8, :] = row
            for p in range(PTS):
                sx, sy, sz, q, far = (picked_ref[n, PTS * c + p : PTS * c + p + 1, :] for c in range(5))
                acc += q * lax.rsqrt((square + far) + tx * sx + (ty * sy + tz * sz))
        pot_ref[g] = acc * SCALE
        return carry

    lax.fori_loop(0, groups, step, 0)
    width = LANES // 2
    pieces = []
    for g in range(groups):
        pot = pot_ref[g]
        pieces += [pot[:, :width], pot[:, width:]]
    near_ref[...] = jnp.concatenate(pieces, axis=0).T


def far_kernel(
    parts_ref, low_ref, peak_ref, source_ref, target_ref, operator_ref, *refs, ops, cap,
):
    _, *join_refs, out_ref, received_ref, split_ref, pair_ref, a_ref, b_ref = refs
    if cap:
        placed(join_refs, received_ref, cap)
    else:
        received_ref = join_refs[0]
    ncoef, leaves = out_ref.shape
    sources = received_ref.shape[0]
    f32 = jnp.float32
    hi, lo = split(pad_lanes(received_ref[...]))
    table = lax.dot_general(
        parts_ref[...], jnp.concatenate([hi, hi], axis=1), NT, preferred_element_type=f32
    ) + lax.dot_general(parts_ref[:, :LANES], lo, NT, preferred_element_type=f32)
    ones = jnp.where(lax.broadcasted_iota(jnp.int32, (LANES, sources), 0) == LANES - 1, 1.0, 0.0)
    for k in range(ops):
        hi, lo = split(table[LANES * k : LANES * (k + 1), :] + ones)
        split_ref[:LANES, sources * k : sources * (k + 1)] = hi
        split_ref[LANES:, sources * k : sources * (k + 1)] = lo
    both = lax.dot_general(split_ref[...], low_ref[...], NT, preferred_element_type=f32)
    out_ref[...] = both[:ncoef, :] + both[LANES : LANES + ncoef, :]

    used = jnp.sum(jnp.where(target_ref[...] < leaves, 1.0, 0.0))
    total = jnp.sum(both[LANES - 1 : LANES, :])
    carried = jnp.logical_or(total != used, jnp.max(peak_ref[...]) >= 2.0**24)

    @pl.when(carried)
    def _():
        size, chunk = a_ref.shape
        marks = Marks(max(size, leaves))
        out_ref[...] = jnp.zeros_like(out_ref)
        for first in range(0, ops // 2 * sources, size):
            pair_ref[...] = jnp.full(pair_ref.shape, -(2.0**24), f32)

            def more(part, carry):
                for c in range(chunk // LANES):
                    at = pl.ds(part * (chunk // LANES) + c, 1)
                    op = operator_ref[at, :]
                    code = (op >> 1) * sources + source_ref[at, :] - first
                    marks.put(a_ref, c, code, jnp.where((op & 1) == 1, 8192.0, 1.0))
                    marks.put(b_ref, c, target_ref[at, :], jnp.ones((1, LANES), f32))
                pair_ref[...] += lax.dot_general(b_ref[...], a_ref[...], NT, preferred_element_type=f32)
                return carry

            lax.fori_loop(0, target_ref.shape[0] * LANES // chunk, more, 0)
            for lane in range(first, first + size, LANES):
                value = pair_ref[:, lane - first : lane - first + LANES]
                odd = jnp.floor(value * (1.0 / 8192.0))
                for parity, count in enumerate((value - 8192.0 * odd, odd + 2048.0)):
                    at = spot(2 * (lane // sources) + parity, ops) * sources + lane % sources
                    rows = split_ref[:, at : at + LANES].astype(f32)
                    rows = rows[:ncoef, :] + rows[LANES : LANES + ncoef, :]
                    out_ref[...] += lax.dot_general(
                        rows, count, NT, precision=lax.Precision.HIGHEST, preferred_element_type=f32
                    )


def shards(
    coords,
    charges,
    multipoles,
    operators,
    send_list,
    near_list,
    m2l_source,
    m2l_target,
    m2l_operator,
):
    ncoef, leaves = multipoles.shape
    npoints = charges.shape[0]
    near = near_list.shape[1]
    entries = m2l_source.shape[1]
    ops = operators.shape[0]
    sources = send_list.shape[1]
    peers = lax.axis_size("grp")
    f32, bf16 = jnp.float32, jnp.bfloat16

    tiles = npoints // LANES
    cap = sources // peers if peers == 8 else 0
    points = (jnp.transpose(coords.reshape(3, tiles, LANES), (1, 0, 2)), charges.reshape(tiles, LANES))
    others = (
        near_list.T,
        *(x.reshape(entries // LANES, LANES) for x in (m2l_source, m2l_target, m2l_operator)),
        jnp.transpose(operators, (1, 0, 2)).reshape(ncoef * ops, ncoef),
    )
    table, same, other, near_list, m2l_source, m2l_target, m2l_operator, operators = pl.pallas_call(
        functools.partial(prep_kernel, others=len(others), cap=cap),
        name="prep",
        out_shape=(
            pltpu.VMEM((4 * PTS, leaves), f32),
            pltpu.VMEM((sources // 2, ncoef), f32),
            pltpu.VMEM((sources // 2, ncoef), f32),
            *(pltpu.VMEM(x.shape, x.dtype) for x in others),
        ),
        in_specs=[ANY] * (4 + len(others)),
        out_specs=(VMEM,) * (3 + len(others)),
        scratch_shapes=[
            pltpu.VMEM((tiles, 3, LANES), f32),
            pltpu.VMEM((tiles, LANES), f32),
            pltpu.VMEM((ncoef, leaves), f32),
            pltpu.VMEM((1, sources), jnp.int32),
            pltpu.VMEM((sources, ncoef), f32),
            pltpu.SemaphoreType.DMA((4 + len(others),)),
        ],
        compiler_params=PARAMS,
    )(*(pltpu.with_memory_space_constraint(x, pltpu.HBM) for x in (*points, multipoles, send_list, *others)))
    codes = ops // 4 * sources
    block = min(codes, 512)
    groups = leaves // LANES
    chunk = entries // 4
    places, parts, low, peak = pl.pallas_call(
        functools.partial(counts_kernel, ops=ops, sources=sources),
        name="counts",
        out_shape=(
            jax.ShapeDtypeStruct((groups, near, LANES), jnp.int32),
            jax.ShapeDtypeStruct((ops * LANES, 2 * LANES), bf16),
            jax.ShapeDtypeStruct((leaves, ops * sources), bf16),
            jax.ShapeDtypeStruct((8, codes), f32),
        ),
        in_specs=[VMEM] * 5,
        out_specs=(VMEM,) * 4,
        scratch_shapes=[
            pltpu.VMEM((ncoef * ops, LANES), f32),
            pltpu.VMEM((2, entries // LANES, LANES), jnp.int32),
            pltpu.VMEM((2, entries // LANES, LANES), f32),
            pltpu.VMEM((leaves // 2, codes), f32),
            pltpu.VMEM((2, block, chunk), bf16),
            pltpu.VMEM((2, leaves // 2, chunk), bf16),
        ],
        compiler_params=PARAMS,
    )(near_list, operators, m2l_source, m2l_target, m2l_operator)
    if cap:
        came = lax.ppermute(other, "grp", [(i, i ^ 1) for i in range(peers)])
        joins = pl.pallas_call(
            functools.partial(join_kernel, cap=cap),
            name="join",
            out_shape=(jax.ShapeDtypeStruct((2 * cap, ncoef), f32),) * (peers // 2),
            in_specs=[VMEM, VMEM, ANY],
            out_specs=(VMEM,) * (peers // 2),
            compiler_params=PARAMS,
        )(same, came, peak)
        received = [joins[0]] + [
            lax.ppermute(joins[m], "grp", [(i, i ^ (2 * m)) for i in range(peers)]) for m in range(1, peers // 2)
        ]
    else:
        received = [
            lax.all_to_all(
                jnp.concatenate([same, other]).reshape(peers, sources // peers, ncoef), "grp", split_axis=0, concat_axis=0, tiled=True
            ).reshape(sources, ncoef)
        ]
    slabs = lax.axis_size("slab")

    def exchange(start):
        to = {}
        for slab in range(slabs):
            other = slab + 1 if (slab - start) % 2 == 0 else slab - 1
            for peer in range(peers):
                if 0 <= other < slabs:
                    to[slab * peers + peer] = other * peers + peer
                else:
                    to[slab * peers + peer] = slab * peers + min(peer ^ 1, peers - 1)
        return lax.ppermute(table, ("slab", "grp"), sorted(to.items()))

    first = exchange(0)
    second = exchange(1)

    near_potential = pl.pallas_call(
        near_kernel,
        name="near",
        out_shape=jax.ShapeDtypeStruct((tiles, LANES), f32),
        in_specs=[VMEM] * 4,
        out_specs=VMEM,
        scratch_shapes=[
            pltpu.VMEM((2 * PTS, 3 * leaves), jnp.int32),
            pltpu.VMEM((PTS, 3 * leaves), f32),
            pltpu.VMEM((near, 5 * PTS, LANES), f32),
            pltpu.VMEM((groups, PTS, LANES), f32),
        ],
        compiler_params=PARAMS,
    )(first, table, second, places)

    local_exp = pl.pallas_call(
        functools.partial(far_kernel, ops=ops, cap=cap),
        name="far",
        out_shape=jax.ShapeDtypeStruct((ncoef, leaves), f32),
        in_specs=[VMEM] * 6 + [ANY] + [VMEM] * len(received),
        out_specs=VMEM,
        scratch_shapes=[
            pltpu.VMEM((sources, ncoef), f32),
            pltpu.VMEM((2 * LANES, ops * sources), bf16),
            pltpu.VMEM((leaves, 512), f32),
            pltpu.VMEM((512, 512), bf16),
            pltpu.VMEM((leaves, 512), bf16),
        ],
        compiler_params=PARAMS,
    )(parts, low, peak, m2l_source, m2l_target, m2l_operator, near_potential, *received)
    return (local_exp, near_potential.reshape(npoints))


def solution(mesh):
    both = ("slab", "grp")
    return jax.shard_map(
        shards,
        mesh=mesh,
        in_specs=(
            P(None, both),
            P(both),
            P(None, both),
            P(),
            P(both, None),
            P(both, None),
            P(both, None),
            P(both, None),
            P(both, None),
        ),
        out_specs=(P(None, both), P(both)),
        check_vma=False,
    )
```

```python
import functools

import jax
import jax.numpy as jnp
from jax import lax
from jax.experimental import pallas as pl
from jax.experimental.pallas import tpu as pltpu
from jax.sharding import PartitionSpec as P

SOFT2 = 0.0625
LANES = 128
PTS = 16
UNITS = 2.0**20
SCALE = 2.0**31
VMEM = pl.BlockSpec(memory_space=pltpu.VMEM)
ANY = pl.BlockSpec(memory_space=pl.ANY)
PARAMS = pltpu.CompilerParams(vmem_limit_bytes=48 * 1024 * 1024)
NT = (((1,), (1,)), ((), ()))


def lane_gather(x, idx):
    return jnp.take_along_axis(x, idx, axis=1, mode="promise_in_bounds")


def split(x):
    hi = x.astype(jnp.bfloat16)
    return hi, (x - hi.astype(jnp.float32)).astype(jnp.bfloat16)


def pad_lanes(x):
    return jnp.concatenate([x, jnp.zeros((x.shape[0], LANES - x.shape[1]), x.dtype)], axis=1)


def prep_kernel(coords_hbm, charges_hbm, multipoles_hbm, send_hbm, *refs, others, cap):
    sources, refs = refs[:others], refs[others:]
    (table_ref, same_ref, other_ref, *targets), refs = refs[: others + 3], refs[others + 3 :]
    coords_ref, charges_ref, multipoles_ref, send_ref, rows_ref, sems = refs
    pairs = (
        (coords_hbm, coords_ref),
        (charges_hbm, charges_ref),
        (send_hbm, send_ref),
        (multipoles_hbm, multipoles_ref),
        *zip(sources, targets),
    )
    copies = [pltpu.make_async_copy(src, dst, sems.at[i]) for i, (src, dst) in enumerate(pairs)]
    for copy in copies:
        copy.start()
    copies[0].wait()
    copies[1].wait()
    for c in range(4):
        rows = charges_ref[...] if c == 3 else coords_ref[:, c, :]
        cols = rows.T
        for pair in range(4):
            a = cols[32 * pair : 32 * pair + 16, :]
            b = cols[32 * pair + 16 : 32 * pair + 32, :]
            table_ref[16 * c : 16 * c + 16, LANES * pair : LANES * (pair + 1)] = jnp.concatenate([a, b], axis=1)
    copies[2].wait()
    copies[3].wait()
    ncoef, leaves = multipoles_ref.shape
    for sb in range(send_ref.shape[1] // LANES):
        send = send_ref[:, LANES * sb : LANES * (sb + 1)]
        lane = send & (LANES - 1)
        group = send >> 7
        idx = jnp.broadcast_to(lane, (ncoef, LANES))
        picked = jnp.zeros((ncoef, LANES), jnp.float32)
        for g in range(leaves // LANES):
            got = lane_gather(multipoles_ref[:, LANES * g : LANES * (g + 1)], idx)
            picked = jnp.where(group == g, got, picked)
        rows_ref[LANES * sb : LANES * (sb + 1), :] = picked.T
    side = lax.axis_index("grp") % 2 if cap else 0
    count = rows_ref.shape[0] // cap if cap else 0
    for k in range(count // 2):
        for ref, peer in ((same_ref, 2 * k + side), (other_ref, 2 * k + 1 - side)):
            ref[cap * k : cap * (k + 1), :] = rows_ref[pl.ds(pl.multiple_of(peer * cap, cap), cap), :]
    if not cap:
        same_ref[...] = rows_ref[: same_ref.shape[0], :]
        other_ref[...] = rows_ref[same_ref.shape[0] :, :]
    for copy in copies[4:]:
        copy.wait()


def join_kernel(out_ref, came_ref, digits_ref, *join_refs, cap):
    del digits_ref
    chip = lax.axis_index("grp") // 2
    for m, ref in enumerate(join_refs):
        at = pl.ds(pl.multiple_of((chip ^ m) * cap, cap), cap)
        ref[:cap, :] = out_ref[at, :]
        ref[cap:, :] = came_ref[at, :]


def placed(join_refs, rows_ref, cap):
    me = lax.axis_index("grp")
    for m, ref in enumerate(join_refs):
        peer = me ^ (2 * m)
        rows_ref[pl.ds(pl.multiple_of(peer * cap, cap), cap), :] = ref[:cap, :]
        rows_ref[pl.ds(pl.multiple_of((peer ^ 1) * cap, cap), cap), :] = ref[cap:, :]


def counts_kernel(
    list_ref, operators_ref, source_ref, target_ref, operator_ref, place_ref, parts_ref, acc_ref,
    wide_ref, code_ref, weight_ref, a_ref, b_ref, *, ops, sources,
):
    near, leaves = list_ref.shape
    ncoef = operators_ref.shape[1]
    groups = leaves // LANES
    half, codes = acc_ref.shape
    _, block, chunk = a_ref.shape
    f32 = jnp.float32
    even = lax.axis_index("slab") % 2 == 0
    lane = lax.broadcasted_iota(jnp.int32, (near, LANES), 1)
    for g in range(groups):
        idx = 8 * (lane & 15) + 2 * g + (lane >> 6)
        part = (lane & 63) >> 4
        row = jnp.zeros((near, LANES), jnp.int32)
        for s in range(groups):
            row = jnp.where(part == s, lane_gather(list_ref[:, LANES * s : LANES * (s + 1)], idx), row)
        side = row >> 9
        side = jnp.where(even, 2 - side, side)
        place_ref[g] = (side << 9) + ((row & 7) << 6) + ((row >> 3) & 63)

    leaf, op = target_ref[...], operator_ref[...]
    upper = leaf >= half
    code_ref[0] = (op >> 2) * sources + source_ref[...]
    weight_ref[0] = (1 << (3 * (op & 3))).astype(f32)
    code_ref[1] = jnp.where(leaf < leaves, jnp.where(upper, leaf - half, leaf), -1)
    weight_ref[1] = jnp.where(upper, 4096.0, 1.0)
    marks = Marks(max(block, half))
    for part in range(target_ref.shape[0] * LANES // chunk):
        turn = part % 2
        for c in range(chunk // LANES):
            at = slice(part * (chunk // LANES) + c, part * (chunk // LANES) + c + 1)
            marks.put(b_ref.at[turn], c, code_ref[1, at, :], weight_ref[1, at, :])
        for first in range(0, codes, block):
            for c in range(chunk // LANES):
                at = slice(part * (chunk // LANES) + c, part * (chunk // LANES) + c + 1)
                marks.put(a_ref.at[turn], c, code_ref[0, at, :] - first, weight_ref[0, at, :])
            product = lax.dot_general(b_ref[turn], a_ref[turn], NT, preferred_element_type=f32)
            if part == 0:
                acc_ref[:, first : first + block] = product
            else:
                acc_ref[:, first : first + block] += product

    wide_ref[...] = pad_lanes(operators_ref[...])
    for op in range(ops):
        matrix = wide_ref[pl.ds(op, ncoef, stride=ops), :]
        matrix = jnp.concatenate([matrix, jnp.zeros((LANES - ncoef, LANES), f32)], axis=0)
        hi, lo = split(matrix)
        parts_ref[LANES * spot(op, ops) : LANES * (spot(op, ops) + 1), :] = jnp.concatenate([hi, lo], axis=1)


def spot(op, ops):
    return (op % 4) * (ops // 4) + op // 4


class Marks:
    def __init__(self, rows):
        self.iota = lax.broadcasted_iota(jnp.int32, (rows, LANES), 0).astype(jnp.int16).reshape(-1, 16, LANES)

    def put(self, ref, c, code, weight):
        size = ref.shape[0]
        code, weight = (
            jnp.broadcast_to(x, (16, LANES)).astype(t)[None] for x, t in ((code, jnp.int16), (weight, jnp.bfloat16))
        )
        marks = jnp.where(self.iota[: size // 16] == code, weight, jnp.zeros((1, 16, LANES), jnp.bfloat16))
        ref[:, LANES * c : LANES * (c + 1)] = marks.reshape(size, LANES)


def near_kernel(
    second_ref, own_ref, first_ref, place_ref, acc_ref, near_ref, low_ref, peak_ref,
    packed_ref, charge_ref, picked_ref, pot_ref,
):
    groups, near, _ = place_ref.shape
    leaves = own_ref.shape[1]
    half, codes = acc_ref.shape
    f32 = jnp.float32
    value = acc_ref[...]
    peak_ref[...] = jnp.max(value.reshape(-1, 8, codes), axis=0)
    value = value.astype(jnp.int32)
    for digit in range(8):
        h, d = digit // 4, digit % 4
        here = (value >> (3 * digit)) & 7
        low_ref[half * h : half * (h + 1), codes * d : codes * (d + 1)] = here.astype(f32).astype(jnp.bfloat16)

    me = lax.axis_index("slab")
    last = lax.axis_size("slab") - 1
    from_right = me % 2 == 0
    ends = (jnp.logical_and(from_right, me == last), False, jnp.where(from_right, me == 0, me == last))
    for k, (ref, end) in enumerate(zip((first_ref, own_ref, second_ref), ends)):
        x, y, z = (
            jnp.minimum(jnp.floor(ref[PTS * c : PTS * (c + 1), :] * UNITS), UNITS - 1.0).astype(jnp.int32)
            for c in range(3)
        )
        at = slice(leaves * k, leaves * (k + 1))
        packed_ref[:PTS, at] = (x << 11) | ((y >> 10) & 2047)
        packed_ref[PTS:, at] = (z << 11) | ((y & 1023) << 1)
        charge_ref[:, at] = jnp.where(end, 0.0, ref[3 * PTS :, :])

    def gather(place):
        idx = place & (LANES - 1)
        group = place >> 7
        refs = [packed_ref.at[8 * r : 8 * r + 8] for r in range(2 * PTS // 8)]
        refs += [charge_ref.at[8 * r : 8 * r + 8] for r in range(PTS // 8)]
        found = [lane_gather(ref[:, :LANES], idx) for ref in refs]
        for s in range(1, 3 * groups):
            here = group == s
            for r, ref in enumerate(refs):
                found[r] = jnp.where(here, lane_gather(ref[:, LANES * s : LANES * (s + 1)], idx), found[r])
        return found

    def step(g, carry):
        at = pl.ds(pl.multiple_of(g * LANES, LANES), LANES)
        tx, ty, tz = (own_ref[PTS * c : PTS * (c + 1), at] * SCALE for c in range(3))
        square = tx * tx + ty * ty + (tz * tz + SOFT2 * SCALE * SCALE)
        tx, ty, tz = -2.0 * tx, -2.0 * ty, -2.0 * tz
        acc = jnp.zeros((PTS, LANES), f32)
        for n in range(near):
            found = gather(jnp.broadcast_to(place_ref[g, n : n + 1, :], (8, LANES)))
            for r in range(PTS // 8):
                first, second, charge = found[r :: PTS // 8]
                x = first.astype(f32)
                y = ((first << 21) | ((second & 2047) << 10)).astype(f32)
                z = second.astype(f32)
                for k, row in enumerate((x, y, z, charge, x * x + y * y + z * z)):
                    picked_ref[n, PTS * k + 8 * r : PTS * k + 8 * r + 8, :] = row
            for p in range(PTS):
                sx, sy, sz, q, far = (picked_ref[n, PTS * c + p : PTS * c + p + 1, :] for c in range(5))
                acc += q * lax.rsqrt((square + far) + tx * sx + (ty * sy + tz * sz))
        pot_ref[g] = acc * SCALE
        return carry

    lax.fori_loop(0, groups, step, 0)
    width = LANES // 2
    pieces = []
    for g in range(groups):
        pot = pot_ref[g]
        pieces += [pot[:, :width], pot[:, width:]]
    near_ref[...] = jnp.concatenate(pieces, axis=0).T


def far_kernel(
    parts_ref, low_ref, peak_ref, source_ref, target_ref, operator_ref, *refs, ops, cap,
):
    *join_refs, out_hbm, out_ref, received_ref, split_ref, pair_ref, a_ref, b_ref, sem = refs
    if cap:
        placed(join_refs, received_ref, cap)
    else:
        received_ref = join_refs[0]
    ncoef, leaves = out_ref.shape
    sources = received_ref.shape[0]
    f32 = jnp.float32
    hi, lo = split(pad_lanes(received_ref[...]))
    table = lax.dot_general(
        parts_ref[...], jnp.concatenate([hi, hi], axis=1), NT, preferred_element_type=f32
    ) + lax.dot_general(parts_ref[:, :LANES], lo, NT, preferred_element_type=f32)
    ones = jnp.where(lax.broadcasted_iota(jnp.int32, (LANES, sources), 0) == LANES - 1, 1.0, 0.0)
    for k in range(ops):
        hi, lo = split(table[LANES * k : LANES * (k + 1), :] + ones)
        split_ref[:LANES, sources * k : sources * (k + 1)] = hi
        split_ref[LANES:, sources * k : sources * (k + 1)] = lo
    both = lax.dot_general(split_ref[...], low_ref[...], NT, preferred_element_type=f32)
    out_ref[...] = both[:ncoef, :] + both[LANES : LANES + ncoef, :]
    result = pltpu.make_async_copy(out_ref, out_hbm, sem)
    result.start()

    used = jnp.sum(jnp.where(target_ref[...] < leaves, 1.0, 0.0))
    total = jnp.sum(both[LANES - 1 : LANES, :])
    carried = jnp.logical_or(total != used, jnp.max(peak_ref[...]) >= 2.0**24)
    result.wait()

    @pl.when(carried)
    def _():
        size, chunk = a_ref.shape
        marks = Marks(max(size, leaves))
        out_ref[...] = jnp.zeros_like(out_ref)
        for first in range(0, ops // 2 * sources, size):
            pair_ref[...] = jnp.full(pair_ref.shape, -(2.0**24), f32)

            def more(part, carry):
                for c in range(chunk // LANES):
                    at = pl.ds(part * (chunk // LANES) + c, 1)
                    op = operator_ref[at, :]
                    code = (op >> 1) * sources + source_ref[at, :] - first
                    marks.put(a_ref, c, code, jnp.where((op & 1) == 1, 8192.0, 1.0))
                    marks.put(b_ref, c, target_ref[at, :], jnp.ones((1, LANES), f32))
                pair_ref[...] += lax.dot_general(b_ref[...], a_ref[...], NT, preferred_element_type=f32)
                return carry

            lax.fori_loop(0, target_ref.shape[0] * LANES // chunk, more, 0)
            for lane in range(first, first + size, LANES):
                value = pair_ref[:, lane - first : lane - first + LANES]
                odd = jnp.floor(value * (1.0 / 8192.0))
                for parity, count in enumerate((value - 8192.0 * odd, odd + 2048.0)):
                    at = spot(2 * (lane // sources) + parity, ops) * sources + lane % sources
                    rows = split_ref[:, at : at + LANES].astype(f32)
                    rows = rows[:ncoef, :] + rows[LANES : LANES + ncoef, :]
                    out_ref[...] += lax.dot_general(
                        rows, count, NT, precision=lax.Precision.HIGHEST, preferred_element_type=f32
                    )
        again = pltpu.make_async_copy(out_ref, out_hbm, sem)
        again.start()
        again.wait()


def shards(
    coords,
    charges,
    multipoles,
    operators,
    send_list,
    near_list,
    m2l_source,
    m2l_target,
    m2l_operator,
):
    ncoef, leaves = multipoles.shape
    npoints = charges.shape[0]
    near = near_list.shape[1]
    entries = m2l_source.shape[1]
    ops = operators.shape[0]
    sources = send_list.shape[1]
    peers = lax.axis_size("grp")
    f32, bf16 = jnp.float32, jnp.bfloat16

    tiles = npoints // LANES
    cap = sources // peers if peers == 8 else 0
    points = (jnp.transpose(coords.reshape(3, tiles, LANES), (1, 0, 2)), charges.reshape(tiles, LANES))
    others = (
        near_list.T,
        *(x.reshape(entries // LANES, LANES) for x in (m2l_source, m2l_target, m2l_operator)),
        jnp.transpose(operators, (1, 0, 2)).reshape(ncoef * ops, ncoef),
    )
    table, same, other, near_list, m2l_source, m2l_target, m2l_operator, operators = pl.pallas_call(
        functools.partial(prep_kernel, others=len(others), cap=cap),
        name="prep",
        out_shape=(
            pltpu.VMEM((4 * PTS, leaves), f32),
            pltpu.VMEM((sources // 2, ncoef), f32),
            pltpu.VMEM((sources // 2, ncoef), f32),
            *(pltpu.VMEM(x.shape, x.dtype) for x in others),
        ),
        in_specs=[ANY] * (4 + len(others)),
        out_specs=(VMEM,) * (3 + len(others)),
        scratch_shapes=[
            pltpu.VMEM((tiles, 3, LANES), f32),
            pltpu.VMEM((tiles, LANES), f32),
            pltpu.VMEM((ncoef, leaves), f32),
            pltpu.VMEM((1, sources), jnp.int32),
            pltpu.VMEM((sources, ncoef), f32),
            pltpu.SemaphoreType.DMA((4 + len(others),)),
        ],
        compiler_params=PARAMS,
    )(*(pltpu.with_memory_space_constraint(x, pltpu.HBM) for x in (*points, multipoles, send_list, *others)))
    codes = ops // 4 * sources
    block = min(codes, 512)
    groups = leaves // LANES
    chunk = entries // 4
    places, parts, digits = pl.pallas_call(
        functools.partial(counts_kernel, ops=ops, sources=sources),
        name="counts",
        out_shape=(
            jax.ShapeDtypeStruct((groups, near, LANES), jnp.int32),
            jax.ShapeDtypeStruct((ops * LANES, 2 * LANES), bf16),
            jax.ShapeDtypeStruct((leaves // 2, codes), f32),
        ),
        in_specs=[VMEM] * 5,
        out_specs=(VMEM,) * 3,
        scratch_shapes=[
            pltpu.VMEM((ncoef * ops, LANES), f32),
            pltpu.VMEM((2, entries // LANES, LANES), jnp.int32),
            pltpu.VMEM((2, entries // LANES, LANES), f32),
            pltpu.VMEM((2, block, chunk), bf16),
            pltpu.VMEM((2, leaves // 2, chunk), bf16),
        ],
        compiler_params=PARAMS,
    )(near_list, operators, m2l_source, m2l_target, m2l_operator)
    if cap:
        came = lax.ppermute(other, "grp", [(i, i ^ 1) for i in range(peers)])
        joins = pl.pallas_call(
            functools.partial(join_kernel, cap=cap),
            name="join",
            out_shape=(jax.ShapeDtypeStruct((2 * cap, ncoef), f32),) * (peers // 2),
            in_specs=[VMEM, VMEM, ANY],
            out_specs=(VMEM,) * (peers // 2),
            compiler_params=PARAMS,
        )(same, came, digits)
        received = [joins[0]] + [
            lax.ppermute(joins[m], "grp", [(i, i ^ (2 * m)) for i in range(peers)]) for m in range(1, peers // 2)
        ]
    else:
        received = [
            lax.all_to_all(
                jnp.concatenate([same, other]).reshape(peers, sources // peers, ncoef), "grp", split_axis=0, concat_axis=0, tiled=True
            ).reshape(sources, ncoef)
        ]
    slabs = lax.axis_size("slab")

    def exchange(start):
        to = {}
        for slab in range(slabs):
            other = slab + 1 if (slab - start) % 2 == 0 else slab - 1
            for peer in range(peers):
                if 0 <= other < slabs:
                    to[slab * peers + peer] = other * peers + peer
                else:
                    to[slab * peers + peer] = slab * peers + min(peer ^ 1, peers - 1)
        return lax.ppermute(table, ("slab", "grp"), sorted(to.items()))

    first = exchange(0)
    second = exchange(1)

    near_potential, low, peak = pl.pallas_call(
        near_kernel,
        name="near",
        out_shape=(
            jax.ShapeDtypeStruct((tiles, LANES), f32),
            jax.ShapeDtypeStruct((leaves, ops * sources), bf16),
            jax.ShapeDtypeStruct((8, codes), f32),
        ),
        in_specs=[VMEM] * 5,
        out_specs=(VMEM,) * 3,
        scratch_shapes=[
            pltpu.VMEM((2 * PTS, 3 * leaves), jnp.int32),
            pltpu.VMEM((PTS, 3 * leaves), f32),
            pltpu.VMEM((near, 5 * PTS, LANES), f32),
            pltpu.VMEM((groups, PTS, LANES), f32),
        ],
        compiler_params=PARAMS,
    )(second, table, first, places, digits)

    local_exp = pl.pallas_call(
        functools.partial(far_kernel, ops=ops, cap=cap),
        name="far",
        out_shape=jax.ShapeDtypeStruct((ncoef, leaves), f32),
        in_specs=[VMEM] * (6 + len(received)),
        out_specs=ANY,
        scratch_shapes=[
            pltpu.VMEM((ncoef, leaves), f32),
            pltpu.VMEM((sources, ncoef), f32),
            pltpu.VMEM((2 * LANES, ops * sources), bf16),
            pltpu.VMEM((leaves, 512), f32),
            pltpu.VMEM((512, 512), bf16),
            pltpu.VMEM((leaves, 512), bf16),
            pltpu.SemaphoreType.DMA,
        ],
        compiler_params=PARAMS,
    )(parts, low, peak, m2l_source, m2l_target, m2l_operator, *received)
    return (local_exp, near_potential.reshape(npoints))


def solution(mesh):
    both = ("slab", "grp")
    return jax.shard_map(
        shards,
        mesh=mesh,
        in_specs=(
            P(None, both),
            P(both),
            P(None, both),
            P(),
            P(both, None),
            P(both, None),
            P(both, None),
            P(both, None),
            P(both, None),
        ),
        out_specs=(P(None, both), P(both)),
        check_vma=False,
    )
```

```python
import functools

import jax
import jax.numpy as jnp
from jax import lax
from jax.experimental import pallas as pl
from jax.experimental.pallas import tpu as pltpu
from jax.sharding import PartitionSpec as P

SOFT2 = 0.0625
LANES = 128
CHIPS = (0, 3, 1, 2)
PTS = 16
UNITS = 2.0**20
SCALE = 2.0**31
VMEM = pl.BlockSpec(memory_space=pltpu.VMEM)
ANY = pl.BlockSpec(memory_space=pl.ANY)
PARAMS = pltpu.CompilerParams(vmem_limit_bytes=48 * 1024 * 1024)
NT = (((1,), (1,)), ((), ()))


def lane_gather(x, idx):
    return jnp.take_along_axis(x, idx, axis=1, mode="promise_in_bounds")


def split(x):
    hi = x.astype(jnp.bfloat16)
    return hi, (x - hi.astype(jnp.float32)).astype(jnp.bfloat16)


def pad_lanes(x):
    return jnp.concatenate([x, jnp.zeros((x.shape[0], LANES - x.shape[1]), x.dtype)], axis=1)


def prep_kernel(coords_hbm, charges_hbm, multipoles_hbm, send_hbm, *refs, others, cap):
    sources, refs = refs[:others], refs[others:]
    (table_ref, same_ref, other_ref, *targets), refs = refs[: others + 3], refs[others + 3 :]
    coords_ref, charges_ref, multipoles_ref, send_ref, rows_ref, sems = refs
    pairs = (
        (coords_hbm, coords_ref),
        (charges_hbm, charges_ref),
        (send_hbm, send_ref),
        (multipoles_hbm, multipoles_ref),
        *zip(sources, targets),
    )
    copies = [pltpu.make_async_copy(src, dst, sems.at[i]) for i, (src, dst) in enumerate(pairs)]
    for copy in copies:
        copy.start()
    copies[0].wait()
    copies[1].wait()
    for c in range(4):
        rows = charges_ref[...] if c == 3 else coords_ref[:, c, :]
        cols = rows.T
        for pair in range(4):
            a = cols[32 * pair : 32 * pair + 16, :]
            b = cols[32 * pair + 16 : 32 * pair + 32, :]
            table_ref[16 * c : 16 * c + 16, LANES * pair : LANES * (pair + 1)] = jnp.concatenate([a, b], axis=1)
    copies[2].wait()
    copies[3].wait()
    ncoef, leaves = multipoles_ref.shape
    for sb in range(send_ref.shape[1] // LANES):
        send = send_ref[:, LANES * sb : LANES * (sb + 1)]
        lane = send & (LANES - 1)
        group = send >> 7
        idx = jnp.broadcast_to(lane, (ncoef, LANES))
        picked = jnp.zeros((ncoef, LANES), jnp.float32)
        for g in range(leaves // LANES):
            got = lane_gather(multipoles_ref[:, LANES * g : LANES * (g + 1)], idx)
            picked = jnp.where(group == g, got, picked)
        rows_ref[LANES * sb : LANES * (sb + 1), :] = picked.T
    side = lax.axis_index("grp") % 2 if cap else 0
    count = rows_ref.shape[0] // cap if cap else 0
    for k in range(count // 2):
        for ref, peer in ((same_ref, 2 * k + side), (other_ref, 2 * k + 1 - side)):
            ref[cap * k : cap * (k + 1), :] = rows_ref[pl.ds(pl.multiple_of(peer * cap, cap), cap), :]
    if not cap:
        same_ref[...] = rows_ref[: same_ref.shape[0], :]
        other_ref[...] = rows_ref[same_ref.shape[0] :, :]
    for copy in copies[4:]:
        copy.wait()


def join_kernel(out_ref, came_ref, digits_ref, *join_refs, cap):
    del digits_ref
    chip = lax.axis_index("grp") // 2
    for m, ref in enumerate(join_refs):
        at = pl.ds(pl.multiple_of((chip ^ m) * cap, cap), cap)
        ref[:cap, :] = out_ref[at, :]
        ref[cap:, :] = came_ref[at, :]


def placed(join_refs, rows_ref, cap):
    me = lax.axis_index("grp")
    for m, ref in zip(CHIPS, join_refs):
        peer = me ^ (2 * m)
        rows_ref[pl.ds(pl.multiple_of(peer * cap, cap), cap), :] = ref[:cap, :]
        rows_ref[pl.ds(pl.multiple_of((peer ^ 1) * cap, cap), cap), :] = ref[cap:, :]


def counts_kernel(
    list_ref, operators_ref, source_ref, target_ref, operator_ref, place_ref, parts_ref, acc_ref,
    wide_ref, code_ref, weight_ref, a_ref, b_ref, *, ops, sources,
):
    near, leaves = list_ref.shape
    ncoef = operators_ref.shape[1]
    groups = leaves // LANES
    half, codes = acc_ref.shape
    _, block, chunk = a_ref.shape
    f32 = jnp.float32
    even = lax.axis_index("slab") % 2 == 0
    lane = lax.broadcasted_iota(jnp.int32, (near, LANES), 1)
    for g in range(groups):
        idx = 8 * (lane & 15) + 2 * g + (lane >> 6)
        part = (lane & 63) >> 4
        row = jnp.zeros((near, LANES), jnp.int32)
        for s in range(groups):
            row = jnp.where(part == s, lane_gather(list_ref[:, LANES * s : LANES * (s + 1)], idx), row)
        side = row >> 9
        side = jnp.where(even, 2 - side, side)
        place_ref[g] = (side << 9) + ((row & 7) << 6) + ((row >> 3) & 63)

    leaf, op = target_ref[...], operator_ref[...]
    upper = leaf >= half
    code_ref[0] = (op >> 2) * sources + source_ref[...]
    weight_ref[0] = (1 << (3 * (op & 3))).astype(f32)
    code_ref[1] = jnp.where(leaf < leaves, jnp.where(upper, leaf - half, leaf), -1)
    weight_ref[1] = jnp.where(upper, 4096.0, 1.0)
    marks = Marks(max(block, half))
    for part in range(target_ref.shape[0] * LANES // chunk):
        turn = part % 2
        for c in range(chunk // LANES):
            at = slice(part * (chunk // LANES) + c, part * (chunk // LANES) + c + 1)
            marks.put(b_ref.at[turn], c, code_ref[1, at, :], weight_ref[1, at, :])
        for first in range(0, codes, block):
            for c in range(chunk // LANES):
                at = slice(part * (chunk // LANES) + c, part * (chunk // LANES) + c + 1)
                marks.put(a_ref.at[turn], c, code_ref[0, at, :] - first, weight_ref[0, at, :])
            product = lax.dot_general(b_ref[turn], a_ref[turn], NT, preferred_element_type=f32)
            if part == 0:
                acc_ref[:, first : first + block] = product
            else:
                acc_ref[:, first : first + block] += product

    wide_ref[...] = pad_lanes(operators_ref[...])
    for op in range(ops):
        matrix = wide_ref[pl.ds(op, ncoef, stride=ops), :]
        matrix = jnp.concatenate([matrix, jnp.zeros((LANES - ncoef, LANES), f32)], axis=0)
        hi, lo = split(matrix)
        parts_ref[LANES * spot(op, ops) : LANES * (spot(op, ops) + 1), :] = jnp.concatenate([hi, lo], axis=1)


def spot(op, ops):
    return (op % 4) * (ops // 4) + op // 4


class Marks:
    def __init__(self, rows):
        self.iota = lax.broadcasted_iota(jnp.int32, (rows, LANES), 0).astype(jnp.int16).reshape(-1, 16, LANES)

    def put(self, ref, c, code, weight):
        size = ref.shape[0]
        code, weight = (
            jnp.broadcast_to(x, (16, LANES)).astype(t)[None] for x, t in ((code, jnp.int16), (weight, jnp.bfloat16))
        )
        marks = jnp.where(self.iota[: size // 16] == code, weight, jnp.zeros((1, 16, LANES), jnp.bfloat16))
        ref[:, LANES * c : LANES * (c + 1)] = marks.reshape(size, LANES)


def near_kernel(
    second_ref, own_ref, first_ref, place_ref, acc_ref, near_ref, low_ref, peak_ref,
    packed_ref, charge_ref, picked_ref, pot_ref,
):
    groups, near, _ = place_ref.shape
    leaves = own_ref.shape[1]
    half, codes = acc_ref.shape
    f32 = jnp.float32
    value = acc_ref[...]
    peak_ref[...] = jnp.max(value.reshape(-1, 8, codes), axis=0)
    value = value.astype(jnp.int32)
    for digit in range(8):
        h, d = digit // 4, digit % 4
        here = (value >> (3 * digit)) & 7
        low_ref[half * h : half * (h + 1), codes * d : codes * (d + 1)] = here.astype(f32).astype(jnp.bfloat16)

    me = lax.axis_index("slab")
    last = lax.axis_size("slab") - 1
    from_right = me % 2 == 0
    ends = (jnp.logical_and(from_right, me == last), False, jnp.where(from_right, me == 0, me == last))
    for k, (ref, end) in enumerate(zip((first_ref, own_ref, second_ref), ends)):
        x, y, z = (
            jnp.minimum(jnp.floor(ref[PTS * c : PTS * (c + 1), :] * UNITS), UNITS - 1.0).astype(jnp.int32)
            for c in range(3)
        )
        at = slice(leaves * k, leaves * (k + 1))
        packed_ref[:PTS, at] = (x << 11) | ((y >> 10) & 2047)
        packed_ref[PTS:, at] = (z << 11) | ((y & 1023) << 1)
        charge_ref[:, at] = jnp.where(end, 0.0, ref[3 * PTS :, :])

    def gather(place):
        idx = place & (LANES - 1)
        group = place >> 7
        refs = [packed_ref.at[8 * r : 8 * r + 8] for r in range(2 * PTS // 8)]
        refs += [charge_ref.at[8 * r : 8 * r + 8] for r in range(PTS // 8)]
        found = [lane_gather(ref[:, :LANES], idx) for ref in refs]
        for s in range(1, 3 * groups):
            here = group == s
            for r, ref in enumerate(refs):
                found[r] = jnp.where(here, lane_gather(ref[:, LANES * s : LANES * (s + 1)], idx), found[r])
        return found

    def step(g, carry):
        at = pl.ds(pl.multiple_of(g * LANES, LANES), LANES)
        tx, ty, tz = (own_ref[PTS * c : PTS * (c + 1), at] * SCALE for c in range(3))
        square = tx * tx + ty * ty + (tz * tz + SOFT2 * SCALE * SCALE)
        tx, ty, tz = -2.0 * tx, -2.0 * ty, -2.0 * tz
        acc = jnp.zeros((PTS, LANES), f32)
        for n in range(near):
            found = gather(jnp.broadcast_to(place_ref[g, n : n + 1, :], (8, LANES)))
            for r in range(PTS // 8):
                first, second, charge = found[r :: PTS // 8]
                x = first.astype(f32)
                y = ((first << 21) | ((second & 2047) << 10)).astype(f32)
                z = second.astype(f32)
                for k, row in enumerate((x, y, z, charge, x * x + y * y + z * z)):
                    picked_ref[n, PTS * k + 8 * r : PTS * k + 8 * r + 8, :] = row
            for p in range(PTS):
                sx, sy, sz, q, far = (picked_ref[n, PTS * c + p : PTS * c + p + 1, :] for c in range(5))
                acc += q * lax.rsqrt((square + far) + tx * sx + (ty * sy + tz * sz))
        pot_ref[g] = acc * SCALE
        return carry

    lax.fori_loop(0, groups, step, 0)
    width = LANES // 2
    pieces = []
    for g in range(groups):
        pot = pot_ref[g]
        pieces += [pot[:, :width], pot[:, width:]]
    near_ref[...] = jnp.concatenate(pieces, axis=0).T


def far_kernel(
    parts_ref, low_ref, peak_ref, source_ref, target_ref, operator_ref, *refs, ops, cap,
):
    *join_refs, out_hbm, out_ref, received_ref, split_ref, pair_ref, a_ref, b_ref, sems = refs
    if cap:
        placed(join_refs, received_ref, cap)
    else:
        received_ref = join_refs[0]
    ncoef, leaves = out_ref.shape
    sources = received_ref.shape[0]
    f32 = jnp.float32
    hi, lo = split(pad_lanes(received_ref[...]))
    table = lax.dot_general(
        parts_ref[...], jnp.concatenate([hi, hi], axis=1), NT, preferred_element_type=f32
    ) + lax.dot_general(parts_ref[:, :LANES], lo, NT, preferred_element_type=f32)
    ones = jnp.where(lax.broadcasted_iota(jnp.int32, (LANES, sources), 0) == LANES - 1, 1.0, 0.0)
    for k in range(ops):
        hi, lo = split(table[LANES * k : LANES * (k + 1), :] + ones)
        split_ref[:LANES, sources * k : sources * (k + 1)] = hi
        split_ref[LANES:, sources * k : sources * (k + 1)] = lo
    results = []
    total = jnp.zeros((), f32)
    for part in range(2):
        at = pl.ds(leaves // 2 * part, leaves // 2)
        both = lax.dot_general(split_ref[...], low_ref[at, :], NT, preferred_element_type=f32)
        out_ref[:, at] = both[:ncoef, :] + both[LANES : LANES + ncoef, :]
        results.append(pltpu.make_async_copy(out_ref.at[:, at], out_hbm.at[:, at], sems.at[part]))
        results[part].start()
        total += jnp.sum(both[LANES - 1 : LANES, :])

    used = jnp.sum(jnp.where(target_ref[...] < leaves, 1.0, 0.0))
    carried = jnp.logical_or(total != used, jnp.max(peak_ref[...]) >= 2.0**24)
    for result in results:
        result.wait()

    @pl.when(carried)
    def _():
        size, chunk = a_ref.shape
        marks = Marks(max(size, leaves))
        out_ref[...] = jnp.zeros_like(out_ref)
        for first in range(0, ops // 2 * sources, size):
            pair_ref[...] = jnp.full(pair_ref.shape, -(2.0**24), f32)

            def more(part, carry):
                for c in range(chunk // LANES):
                    at = pl.ds(part * (chunk // LANES) + c, 1)
                    op = operator_ref[at, :]
                    code = (op >> 1) * sources + source_ref[at, :] - first
                    marks.put(a_ref, c, code, jnp.where((op & 1) == 1, 8192.0, 1.0))
                    marks.put(b_ref, c, target_ref[at, :], jnp.ones((1, LANES), f32))
                pair_ref[...] += lax.dot_general(b_ref[...], a_ref[...], NT, preferred_element_type=f32)
                return carry

            lax.fori_loop(0, target_ref.shape[0] * LANES // chunk, more, 0)
            for lane in range(first, first + size, LANES):
                value = pair_ref[:, lane - first : lane - first + LANES]
                odd = jnp.floor(value * (1.0 / 8192.0))
                for parity, count in enumerate((value - 8192.0 * odd, odd + 2048.0)):
                    at = spot(2 * (lane // sources) + parity, ops) * sources + lane % sources
                    rows = split_ref[:, at : at + LANES].astype(f32)
                    rows = rows[:ncoef, :] + rows[LANES : LANES + ncoef, :]
                    out_ref[...] += lax.dot_general(
                        rows, count, NT, precision=lax.Precision.HIGHEST, preferred_element_type=f32
                    )
        again = pltpu.make_async_copy(out_ref, out_hbm, sems.at[0])
        again.start()
        again.wait()


def shards(
    coords,
    charges,
    multipoles,
    operators,
    send_list,
    near_list,
    m2l_source,
    m2l_target,
    m2l_operator,
):
    ncoef, leaves = multipoles.shape
    npoints = charges.shape[0]
    near = near_list.shape[1]
    entries = m2l_source.shape[1]
    ops = operators.shape[0]
    sources = send_list.shape[1]
    peers = lax.axis_size("grp")
    f32, bf16 = jnp.float32, jnp.bfloat16

    tiles = npoints // LANES
    cap = sources // peers if peers == 8 else 0
    points = (jnp.transpose(coords.reshape(3, tiles, LANES), (1, 0, 2)), charges.reshape(tiles, LANES))
    others = (
        near_list.T,
        *(x.reshape(entries // LANES, LANES) for x in (m2l_source, m2l_target, m2l_operator)),
        jnp.transpose(operators, (1, 0, 2)).reshape(ncoef * ops, ncoef),
    )
    table, same, other, near_list, m2l_source, m2l_target, m2l_operator, operators = pl.pallas_call(
        functools.partial(prep_kernel, others=len(others), cap=cap),
        name="prep",
        out_shape=(
            pltpu.VMEM((4 * PTS, leaves), f32),
            pltpu.VMEM((sources // 2, ncoef), f32),
            pltpu.VMEM((sources // 2, ncoef), f32),
            *(pltpu.VMEM(x.shape, x.dtype) for x in others),
        ),
        in_specs=[ANY] * (4 + len(others)),
        out_specs=(VMEM,) * (3 + len(others)),
        scratch_shapes=[
            pltpu.VMEM((tiles, 3, LANES), f32),
            pltpu.VMEM((tiles, LANES), f32),
            pltpu.VMEM((ncoef, leaves), f32),
            pltpu.VMEM((1, sources), jnp.int32),
            pltpu.VMEM((sources, ncoef), f32),
            pltpu.SemaphoreType.DMA((4 + len(others),)),
        ],
        compiler_params=PARAMS,
    )(*(pltpu.with_memory_space_constraint(x, pltpu.HBM) for x in (*points, multipoles, send_list, *others)))
    codes = ops // 4 * sources
    block = min(codes, 512)
    groups = leaves // LANES
    chunk = entries // 4
    places, parts, digits = pl.pallas_call(
        functools.partial(counts_kernel, ops=ops, sources=sources),
        name="counts",
        out_shape=(
            jax.ShapeDtypeStruct((groups, near, LANES), jnp.int32),
            jax.ShapeDtypeStruct((ops * LANES, 2 * LANES), bf16),
            jax.ShapeDtypeStruct((leaves // 2, codes), f32),
        ),
        in_specs=[VMEM] * 5,
        out_specs=(VMEM,) * 3,
        scratch_shapes=[
            pltpu.VMEM((ncoef * ops, LANES), f32),
            pltpu.VMEM((2, entries // LANES, LANES), jnp.int32),
            pltpu.VMEM((2, entries // LANES, LANES), f32),
            pltpu.VMEM((2, block, chunk), bf16),
            pltpu.VMEM((2, leaves // 2, chunk), bf16),
        ],
        compiler_params=PARAMS,
    )(near_list, operators, m2l_source, m2l_target, m2l_operator)
    if cap:
        came = lax.ppermute(other, "grp", [(i, i ^ 1) for i in range(peers)])
        joins = pl.pallas_call(
            functools.partial(join_kernel, cap=cap),
            name="join",
            out_shape=(jax.ShapeDtypeStruct((2 * cap, ncoef), f32),) * (peers // 2),
            in_specs=[VMEM, VMEM, ANY],
            out_specs=(VMEM,) * (peers // 2),
            compiler_params=PARAMS,
        )(same, came, digits)
        received = [joins[0]] + [
            lax.ppermute(joins[m], "grp", [(i, i ^ (2 * m)) for i in range(peers)]) for m in CHIPS[1:]
        ]
    else:
        received = [
            lax.all_to_all(
                jnp.concatenate([same, other]).reshape(peers, sources // peers, ncoef), "grp", split_axis=0, concat_axis=0, tiled=True
            ).reshape(sources, ncoef)
        ]
    slabs = lax.axis_size("slab")

    def exchange(start):
        to = {}
        for slab in range(slabs):
            other = slab + 1 if (slab - start) % 2 == 0 else slab - 1
            for peer in range(peers):
                if 0 <= other < slabs:
                    to[slab * peers + peer] = other * peers + peer
                else:
                    to[slab * peers + peer] = slab * peers + min(peer ^ 1, peers - 1)
        return lax.ppermute(table, ("slab", "grp"), sorted(to.items()))

    first = exchange(0)
    second = exchange(1)

    near_potential, low, peak = pl.pallas_call(
        near_kernel,
        name="near",
        out_shape=(
            jax.ShapeDtypeStruct((tiles, LANES), f32),
            jax.ShapeDtypeStruct((leaves, ops * sources), bf16),
            jax.ShapeDtypeStruct((8, codes), f32),
        ),
        in_specs=[VMEM] * 5,
        out_specs=(VMEM,) * 3,
        scratch_shapes=[
            pltpu.VMEM((2 * PTS, 3 * leaves), jnp.int32),
            pltpu.VMEM((PTS, 3 * leaves), f32),
            pltpu.VMEM((near, 5 * PTS, LANES), f32),
            pltpu.VMEM((groups, PTS, LANES), f32),
        ],
        compiler_params=PARAMS,
    )(second, table, first, places, digits)

    local_exp = pl.pallas_call(
        functools.partial(far_kernel, ops=ops, cap=cap),
        name="far",
        out_shape=jax.ShapeDtypeStruct((ncoef, leaves), f32),
        in_specs=[VMEM] * (6 + len(received)),
        out_specs=ANY,
        scratch_shapes=[
            pltpu.VMEM((ncoef, leaves), f32),
            pltpu.VMEM((sources, ncoef), f32),
            pltpu.VMEM((2 * LANES, ops * sources), bf16),
            pltpu.VMEM((leaves, 512), f32),
            pltpu.VMEM((512, 512), bf16),
            pltpu.VMEM((leaves, 512), bf16),
            pltpu.SemaphoreType.DMA((2,)),
        ],
        compiler_params=PARAMS,
    )(parts, low, peak, m2l_source, m2l_target, m2l_operator, *received)
    return (local_exp, near_potential.reshape(npoints))


def solution(mesh):
    both = ("slab", "grp")
    return jax.shard_map(
        shards,
        mesh=mesh,
        in_specs=(
            P(None, both),
            P(both),
            P(None, both),
            P(),
            P(both, None),
            P(both, None),
            P(both, None),
            P(both, None),
            P(both, None),
        ),
        out_specs=(P(None, both), P(both)),
        check_vma=False,
    )
```

```python
import functools

import jax
import jax.numpy as jnp
from jax import lax
from jax.experimental import pallas as pl
from jax.experimental.pallas import tpu as pltpu
from jax.sharding import PartitionSpec as P

SOFT2 = 0.0625
LANES = 128
CHIPS = (0, 3, 1, 2)
PTS = 16
UNITS = 2.0**20
SCALE = 2.0**31
VMEM = pl.BlockSpec(memory_space=pltpu.VMEM)
ANY = pl.BlockSpec(memory_space=pl.ANY)
PARAMS = pltpu.CompilerParams(vmem_limit_bytes=48 * 1024 * 1024)
NT = (((1,), (1,)), ((), ()))


def lane_gather(x, idx):
    return jnp.take_along_axis(x, idx, axis=1, mode="promise_in_bounds")


def split(x):
    hi = x.astype(jnp.bfloat16)
    return hi, (x - hi.astype(jnp.float32)).astype(jnp.bfloat16)


def pad_lanes(x):
    return jnp.concatenate([x, jnp.zeros((x.shape[0], LANES - x.shape[1]), x.dtype)], axis=1)


def prep_kernel(coords_hbm, charges_hbm, multipoles_hbm, send_hbm, *refs, others, cap):
    sources, refs = refs[:others], refs[others:]
    (table_ref, same_ref, other_ref, *targets), refs = refs[: others + 3], refs[others + 3 :]
    coords_ref, charges_ref, multipoles_ref, send_ref, rows_ref, sems = refs
    pairs = (
        (coords_hbm, coords_ref),
        (charges_hbm, charges_ref),
        (send_hbm, send_ref),
        (multipoles_hbm, multipoles_ref),
        *zip(sources, targets),
    )
    copies = [pltpu.make_async_copy(src, dst, sems.at[i]) for i, (src, dst) in enumerate(pairs)]
    for copy in copies:
        copy.start()
    copies[0].wait()
    copies[1].wait()
    for c in range(4):
        rows = charges_ref[...] if c == 3 else coords_ref[:, c, :]
        cols = rows.T
        for pair in range(4):
            a = cols[32 * pair : 32 * pair + 16, :]
            b = cols[32 * pair + 16 : 32 * pair + 32, :]
            table_ref[16 * c : 16 * c + 16, LANES * pair : LANES * (pair + 1)] = jnp.concatenate([a, b], axis=1)
    copies[2].wait()
    copies[3].wait()
    ncoef, leaves = multipoles_ref.shape
    for sb in range(send_ref.shape[1] // LANES):
        send = send_ref[:, LANES * sb : LANES * (sb + 1)]
        lane = send & (LANES - 1)
        group = send >> 7
        idx = jnp.broadcast_to(lane, (ncoef, LANES))
        picked = jnp.zeros((ncoef, LANES), jnp.float32)
        for g in range(leaves // LANES):
            got = lane_gather(multipoles_ref[:, LANES * g : LANES * (g + 1)], idx)
            picked = jnp.where(group == g, got, picked)
        rows_ref[LANES * sb : LANES * (sb + 1), :] = picked.T
    side = lax.axis_index("grp") % 2 if cap else 0
    count = rows_ref.shape[0] // cap if cap else 0
    for k in range(count // 2):
        for ref, peer in ((same_ref, 2 * k + side), (other_ref, 2 * k + 1 - side)):
            ref[cap * k : cap * (k + 1), :] = rows_ref[pl.ds(pl.multiple_of(peer * cap, cap), cap), :]
    if not cap:
        same_ref[...] = rows_ref[: same_ref.shape[0], :]
        other_ref[...] = rows_ref[same_ref.shape[0] :, :]
    for copy in copies[4:]:
        copy.wait()


def join_kernel(out_ref, came_ref, digits_ref, *join_refs, cap):
    del digits_ref
    chip = lax.axis_index("grp") // 2
    for m, ref in enumerate(join_refs):
        at = pl.ds(pl.multiple_of((chip ^ m) * cap, cap), cap)
        ref[:cap, :] = out_ref[at, :]
        ref[cap:, :] = came_ref[at, :]


def placed(join_refs, rows_ref, cap):
    me = lax.axis_index("grp")
    for m, ref in zip(CHIPS, join_refs):
        peer = me ^ (2 * m)
        rows_ref[pl.ds(pl.multiple_of(peer * cap, cap), cap), :] = ref[:cap, :]
        rows_ref[pl.ds(pl.multiple_of((peer ^ 1) * cap, cap), cap), :] = ref[cap:, :]


def counts_kernel(
    list_ref, operators_ref, source_ref, target_ref, operator_ref, place_ref, parts_ref, acc_ref,
    wide_ref, code_ref, weight_ref, a_ref, b_ref, *, ops, sources,
):
    near, leaves = list_ref.shape
    ncoef = operators_ref.shape[1]
    groups = leaves // LANES
    half, codes = acc_ref.shape
    _, block, chunk = a_ref.shape
    f32 = jnp.float32
    even = lax.axis_index("slab") % 2 == 0
    lane = lax.broadcasted_iota(jnp.int32, (near, LANES), 1)
    for g in range(groups):
        idx = 8 * (lane & 15) + 2 * g + (lane >> 6)
        part = (lane & 63) >> 4
        row = jnp.zeros((near, LANES), jnp.int32)
        for s in range(groups):
            row = jnp.where(part == s, lane_gather(list_ref[:, LANES * s : LANES * (s + 1)], idx), row)
        side = row >> 9
        side = jnp.where(even, 2 - side, side)
        place_ref[g] = (side << 9) + ((row & 7) << 6) + ((row >> 3) & 63)

    leaf, op = target_ref[...], operator_ref[...]
    upper = leaf >= half
    code_ref[0] = (op >> 2) * sources + source_ref[...]
    weight_ref[0] = (1 << (3 * (op & 3))).astype(f32)
    code_ref[1] = jnp.where(leaf < leaves, jnp.where(upper, leaf - half, leaf), -1)
    weight_ref[1] = jnp.where(upper, 4096.0, 1.0)
    marks = Marks(max(block, half))
    for part in range(target_ref.shape[0] * LANES // chunk):
        turn = part % 2
        for c in range(chunk // LANES):
            at = slice(part * (chunk // LANES) + c, part * (chunk // LANES) + c + 1)
            marks.put(b_ref.at[turn], c, code_ref[1, at, :], weight_ref[1, at, :])
        for first in range(0, codes, block):
            for c in range(chunk // LANES):
                at = slice(part * (chunk // LANES) + c, part * (chunk // LANES) + c + 1)
                marks.put(a_ref.at[turn], c, code_ref[0, at, :] - first, weight_ref[0, at, :])
            product = lax.dot_general(b_ref[turn], a_ref[turn], NT, preferred_element_type=f32)
            if part == 0:
                acc_ref[:, first : first + block] = product
            else:
                acc_ref[:, first : first + block] += product

    wide_ref[...] = pad_lanes(operators_ref[...])
    for op in range(ops):
        matrix = wide_ref[pl.ds(op, ncoef, stride=ops), :]
        matrix = jnp.concatenate([matrix, jnp.zeros((LANES - ncoef, LANES), f32)], axis=0)
        hi, lo = split(matrix)
        parts_ref[LANES * spot(op, ops) : LANES * (spot(op, ops) + 1), :] = jnp.concatenate([hi, lo], axis=1)


def spot(op, ops):
    return (op % 4) * (ops // 4) + op // 4


class Marks:
    def __init__(self, rows):
        self.iota = lax.broadcasted_iota(jnp.int32, (rows, LANES), 0).astype(jnp.int16).reshape(-1, 16, LANES)

    def put(self, ref, c, code, weight):
        size = ref.shape[0]
        code, weight = (
            jnp.broadcast_to(x, (16, LANES)).astype(t)[None] for x, t in ((code, jnp.int16), (weight, jnp.bfloat16))
        )
        marks = jnp.where(self.iota[: size // 16] == code, weight, jnp.zeros((1, 16, LANES), jnp.bfloat16))
        ref[:, LANES * c : LANES * (c + 1)] = marks.reshape(size, LANES)


def near_kernel(
    second_ref, own_ref, first_ref, place_ref, acc_ref, near_ref, low_ref, peak_ref,
    packed_ref, charge_ref, picked_ref, pot_ref,
):
    groups, near, _ = place_ref.shape
    leaves = own_ref.shape[1]
    half, codes = acc_ref.shape
    f32 = jnp.float32
    value = acc_ref[...]
    peak_ref[...] = jnp.max(value.reshape(-1, 8, codes), axis=0)
    value = value.astype(jnp.int32)
    for digit in range(8):
        h, d = digit // 4, digit % 4
        here = (value >> (3 * digit)) & 7
        low_ref[half * h : half * (h + 1), codes * d : codes * (d + 1)] = here.astype(f32).astype(jnp.bfloat16)

    me = lax.axis_index("slab")
    last = lax.axis_size("slab") - 1
    from_right = me % 2 == 0
    ends = (jnp.logical_and(from_right, me == last), False, jnp.where(from_right, me == 0, me == last))
    for k, (ref, end) in enumerate(zip((first_ref, own_ref, second_ref), ends)):
        x, y, z = (
            jnp.minimum(jnp.floor(ref[PTS * c : PTS * (c + 1), :] * UNITS), UNITS - 1.0).astype(jnp.int32)
            for c in range(3)
        )
        at = slice(leaves * k, leaves * (k + 1))
        packed_ref[:PTS, at] = (x << 11) | ((y >> 10) & 2047)
        packed_ref[PTS:, at] = (z << 11) | ((y & 1023) << 1)
        charge_ref[:, at] = jnp.where(end, 0.0, ref[3 * PTS :, :])

    def gather(place):
        idx = place & (LANES - 1)
        group = place >> 7
        refs = [packed_ref.at[8 * r : 8 * r + 8] for r in range(2 * PTS // 8)]
        refs += [charge_ref.at[8 * r : 8 * r + 8] for r in range(PTS // 8)]
        found = [lane_gather(ref[:, :LANES], idx) for ref in refs]
        for s in range(1, 3 * groups):
            here = group == s
            for r, ref in enumerate(refs):
                found[r] = jnp.where(here, lane_gather(ref[:, LANES * s : LANES * (s + 1)], idx), found[r])
        return found

    def step(g, carry):
        at = pl.ds(pl.multiple_of(g * LANES, LANES), LANES)
        tx, ty, tz = (own_ref[PTS * c : PTS * (c + 1), at] * SCALE for c in range(3))
        square = tx * tx + ty * ty + (tz * tz + SOFT2 * SCALE * SCALE)
        tx, ty, tz = -2.0 * tx, -2.0 * ty, -2.0 * tz
        acc = jnp.zeros((PTS, LANES), f32)
        for n in range(near):
            found = gather(jnp.broadcast_to(place_ref[g, n : n + 1, :], (8, LANES)))
            for r in range(PTS // 8):
                first, second, charge = found[r :: PTS // 8]
                x = first.astype(f32)
                y = ((first << 21) | ((second & 2047) << 10)).astype(f32)
                z = second.astype(f32)
                for k, row in enumerate((x, y, z, charge, x * x + y * y + z * z)):
                    picked_ref[n, PTS * k + 8 * r : PTS * k + 8 * r + 8, :] = row
            for p in range(PTS):
                sx, sy, sz, q, far = (picked_ref[n, PTS * c + p : PTS * c + p + 1, :] for c in range(5))
                acc += q * lax.rsqrt((square + far) + tx * sx + (ty * sy + tz * sz))
        pot_ref[g] = acc * SCALE
        return carry

    lax.fori_loop(0, groups, step, 0)
    width = LANES // 2
    pieces = []
    for g in range(groups):
        pot = pot_ref[g]
        pieces += [pot[:, :width], pot[:, width:]]
    near_ref[...] = jnp.concatenate(pieces, axis=0).T


def far_kernel(
    parts_ref, low_ref, peak_ref, source_ref, target_ref, operator_ref, near_ref, *refs, ops, cap,
):
    *join_refs, out_hbm, near_hbm, out_ref, received_ref, split_ref, pair_ref, a_ref, b_ref, sems = refs
    results = [pltpu.make_async_copy(near_ref, near_hbm, sems.at[2])]
    results[0].start()
    if cap:
        placed(join_refs, received_ref, cap)
    else:
        received_ref = join_refs[0]
    ncoef, leaves = out_ref.shape
    sources = received_ref.shape[0]
    f32 = jnp.float32
    hi, lo = split(pad_lanes(received_ref[...]))
    both = jnp.concatenate(
        [jnp.concatenate([hi, hi], axis=1), jnp.concatenate([lo, jnp.zeros_like(lo)], axis=1)], axis=0
    )
    table = lax.dot_general(parts_ref[...], both, NT, preferred_element_type=f32)
    table = table[:, :sources] + table[:, sources:]
    ones = jnp.where(lax.broadcasted_iota(jnp.int32, (LANES, sources), 0) == LANES - 1, 1.0, 0.0)
    for k in range(ops):
        hi, lo = split(table[LANES * k : LANES * (k + 1), :] + ones)
        split_ref[:LANES, sources * k : sources * (k + 1)] = hi
        split_ref[LANES:, sources * k : sources * (k + 1)] = lo
    total = jnp.zeros((), f32)
    for part in range(2):
        at = pl.ds(leaves // 2 * part, leaves // 2)
        both = lax.dot_general(split_ref[...], low_ref[at, :], NT, preferred_element_type=f32)
        out_ref[:, at] = both[:ncoef, :] + both[LANES : LANES + ncoef, :]
        results.append(pltpu.make_async_copy(out_ref.at[:, at], out_hbm.at[:, at], sems.at[part]))
        results[-1].start()
        total += jnp.sum(both[LANES - 1 : LANES, :])

    used = jnp.sum(jnp.where(target_ref[...] < leaves, 1.0, 0.0))
    carried = jnp.logical_or(total != used, jnp.max(peak_ref[...]) >= 2.0**24)
    for result in results:
        result.wait()

    @pl.when(carried)
    def _():
        size, chunk = a_ref.shape
        marks = Marks(max(size, leaves))
        out_ref[...] = jnp.zeros_like(out_ref)
        for first in range(0, ops // 2 * sources, size):
            pair_ref[...] = jnp.full(pair_ref.shape, -(2.0**24), f32)

            def more(part, carry):
                for c in range(chunk // LANES):
                    at = pl.ds(part * (chunk // LANES) + c, 1)
                    op = operator_ref[at, :]
                    code = (op >> 1) * sources + source_ref[at, :] - first
                    marks.put(a_ref, c, code, jnp.where((op & 1) == 1, 8192.0, 1.0))
                    marks.put(b_ref, c, target_ref[at, :], jnp.ones((1, LANES), f32))
                pair_ref[...] += lax.dot_general(b_ref[...], a_ref[...], NT, preferred_element_type=f32)
                return carry

            lax.fori_loop(0, target_ref.shape[0] * LANES // chunk, more, 0)
            for lane in range(first, first + size, LANES):
                value = pair_ref[:, lane - first : lane - first + LANES]
                odd = jnp.floor(value * (1.0 / 8192.0))
                for parity, count in enumerate((value - 8192.0 * odd, odd + 2048.0)):
                    at = spot(2 * (lane // sources) + parity, ops) * sources + lane % sources
                    rows = split_ref[:, at : at + LANES].astype(f32)
                    rows = rows[:ncoef, :] + rows[LANES : LANES + ncoef, :]
                    out_ref[...] += lax.dot_general(
                        rows, count, NT, precision=lax.Precision.HIGHEST, preferred_element_type=f32
                    )
        again = pltpu.make_async_copy(out_ref, out_hbm, sems.at[0])
        again.start()
        again.wait()


def shards(
    coords,
    charges,
    multipoles,
    operators,
    send_list,
    near_list,
    m2l_source,
    m2l_target,
    m2l_operator,
):
    ncoef, leaves = multipoles.shape
    npoints = charges.shape[0]
    near = near_list.shape[1]
    entries = m2l_source.shape[1]
    ops = operators.shape[0]
    sources = send_list.shape[1]
    peers = lax.axis_size("grp")
    f32, bf16 = jnp.float32, jnp.bfloat16

    tiles = npoints // LANES
    cap = sources // peers if peers == 8 else 0
    points = (jnp.transpose(coords.reshape(3, tiles, LANES), (1, 0, 2)), charges.reshape(tiles, LANES))
    others = (
        near_list.T,
        *(x.reshape(entries // LANES, LANES) for x in (m2l_source, m2l_target, m2l_operator)),
        jnp.transpose(operators, (1, 0, 2)).reshape(ncoef * ops, ncoef),
    )
    table, same, other, near_list, m2l_source, m2l_target, m2l_operator, operators = pl.pallas_call(
        functools.partial(prep_kernel, others=len(others), cap=cap),
        name="prep",
        out_shape=(
            pltpu.VMEM((4 * PTS, leaves), f32),
            pltpu.VMEM((sources // 2, ncoef), f32),
            pltpu.VMEM((sources // 2, ncoef), f32),
            *(pltpu.VMEM(x.shape, x.dtype) for x in others),
        ),
        in_specs=[ANY] * (4 + len(others)),
        out_specs=(VMEM,) * (3 + len(others)),
        scratch_shapes=[
            pltpu.VMEM((tiles, 3, LANES), f32),
            pltpu.VMEM((tiles, LANES), f32),
            pltpu.VMEM((ncoef, leaves), f32),
            pltpu.VMEM((1, sources), jnp.int32),
            pltpu.VMEM((sources, ncoef), f32),
            pltpu.SemaphoreType.DMA((4 + len(others),)),
        ],
        compiler_params=PARAMS,
    )(*(pltpu.with_memory_space_constraint(x, pltpu.HBM) for x in (*points, multipoles, send_list, *others)))
    codes = ops // 4 * sources
    block = min(codes, 512)
    groups = leaves // LANES
    chunk = entries // 4
    places, parts, digits = pl.pallas_call(
        functools.partial(counts_kernel, ops=ops, sources=sources),
        name="counts",
        out_shape=(
            jax.ShapeDtypeStruct((groups, near, LANES), jnp.int32),
            jax.ShapeDtypeStruct((ops * LANES, 2 * LANES), bf16),
            jax.ShapeDtypeStruct((leaves // 2, codes), f32),
        ),
        in_specs=[VMEM] * 5,
        out_specs=(VMEM,) * 3,
        scratch_shapes=[
            pltpu.VMEM((ncoef * ops, LANES), f32),
            pltpu.VMEM((2, entries // LANES, LANES), jnp.int32),
            pltpu.VMEM((2, entries // LANES, LANES), f32),
            pltpu.VMEM((2, block, chunk), bf16),
            pltpu.VMEM((2, leaves // 2, chunk), bf16),
        ],
        compiler_params=PARAMS,
    )(near_list, operators, m2l_source, m2l_target, m2l_operator)
    if cap:
        came = lax.ppermute(other, "grp", [(i, i ^ 1) for i in range(peers)])
        joins = pl.pallas_call(
            functools.partial(join_kernel, cap=cap),
            name="join",
            out_shape=(jax.ShapeDtypeStruct((2 * cap, ncoef), f32),) * (peers // 2),
            in_specs=[VMEM, VMEM, ANY],
            out_specs=(VMEM,) * (peers // 2),
            compiler_params=PARAMS,
        )(same, came, digits)
        received = [joins[0]] + [
            lax.ppermute(joins[m], "grp", [(i, i ^ (2 * m)) for i in range(peers)]) for m in CHIPS[1:]
        ]
    else:
        received = [
            lax.all_to_all(
                jnp.concatenate([same, other]).reshape(peers, sources // peers, ncoef), "grp", split_axis=0, concat_axis=0, tiled=True
            ).reshape(sources, ncoef)
        ]
    slabs = lax.axis_size("slab")

    def exchange(start):
        to = {}
        for slab in range(slabs):
            other = slab + 1 if (slab - start) % 2 == 0 else slab - 1
            for peer in range(peers):
                if 0 <= other < slabs:
                    to[slab * peers + peer] = other * peers + peer
                else:
                    to[slab * peers + peer] = slab * peers + min(peer ^ 1, peers - 1)
        return lax.ppermute(table, ("slab", "grp"), sorted(to.items()))

    first = exchange(0)
    second = exchange(1)

    near_potential, low, peak = pl.pallas_call(
        near_kernel,
        name="near",
        out_shape=(
            pltpu.VMEM((tiles, LANES), f32),
            jax.ShapeDtypeStruct((leaves, ops * sources), bf16),
            jax.ShapeDtypeStruct((8, codes), f32),
        ),
        in_specs=[VMEM] * 5,
        out_specs=(VMEM,) * 3,
        scratch_shapes=[
            pltpu.VMEM((2 * PTS, 3 * leaves), jnp.int32),
            pltpu.VMEM((PTS, 3 * leaves), f32),
            pltpu.VMEM((near, 5 * PTS, LANES), f32),
            pltpu.VMEM((groups, PTS, LANES), f32),
        ],
        compiler_params=PARAMS,
    )(second, table, first, places, digits)

    local_exp, near_potential = pl.pallas_call(
        functools.partial(far_kernel, ops=ops, cap=cap),
        name="far",
        out_shape=(jax.ShapeDtypeStruct((ncoef, leaves), f32), jax.ShapeDtypeStruct((tiles, LANES), f32)),
        in_specs=[VMEM] * (7 + len(received)),
        out_specs=(ANY, ANY),
        scratch_shapes=[
            pltpu.VMEM((ncoef, leaves), f32),
            pltpu.VMEM((sources, ncoef), f32),
            pltpu.VMEM((2 * LANES, ops * sources), bf16),
            pltpu.VMEM((leaves, 512), f32),
            pltpu.VMEM((512, 512), bf16),
            pltpu.VMEM((leaves, 512), bf16),
            pltpu.SemaphoreType.DMA((3,)),
        ],
        compiler_params=PARAMS,
    )(parts, low, peak, m2l_source, m2l_target, m2l_operator, near_potential, *received)
    return (local_exp, near_potential.reshape(npoints))


def solution(mesh):
    both = ("slab", "grp")
    return jax.shard_map(
        shards,
        mesh=mesh,
        in_specs=(
            P(None, both),
            P(both),
            P(None, both),
            P(),
            P(both, None),
            P(both, None),
            P(both, None),
            P(both, None),
            P(both, None),
        ),
        out_specs=(P(None, both), P(both)),
        check_vma=False,
    )
```

```python
import functools

import jax
import jax.numpy as jnp
from jax import lax
from jax.experimental import pallas as pl
from jax.experimental.pallas import tpu as pltpu
from jax.sharding import PartitionSpec as P

SOFT2 = 0.0625
LANES = 128
PTS = 16
UNITS = 2.0**20
SCALE = 2.0**31
VMEM = pl.BlockSpec(memory_space=pltpu.VMEM)
ANY = pl.BlockSpec(memory_space=pl.ANY)
PARAMS = pltpu.CompilerParams(vmem_limit_bytes=48 * 1024 * 1024)
NT = (((1,), (1,)), ((), ()))


def lane_gather(x, idx):
    return jnp.take_along_axis(x, idx, axis=1, mode="promise_in_bounds")


def split(x):
    hi = x.astype(jnp.bfloat16)
    return hi, (x - hi.astype(jnp.float32)).astype(jnp.bfloat16)


def pad_lanes(x):
    return jnp.concatenate([x, jnp.zeros((x.shape[0], LANES - x.shape[1]), x.dtype)], axis=1)


def prep_kernel(coords_hbm, charges_hbm, multipoles_hbm, send_hbm, *refs, others, cap):
    sources, refs = refs[:others], refs[others:]
    (table_ref, same_ref, other_ref, *targets), refs = refs[: others + 3], refs[others + 3 :]
    coords_ref, charges_ref, multipoles_ref, send_ref, rows_ref, sems = refs
    pairs = (
        (coords_hbm, coords_ref),
        (charges_hbm, charges_ref),
        (send_hbm, send_ref),
        (multipoles_hbm, multipoles_ref),
        *zip(sources, targets),
    )
    copies = [pltpu.make_async_copy(src, dst, sems.at[i]) for i, (src, dst) in enumerate(pairs)]
    for copy in copies:
        copy.start()
    copies[0].wait()
    copies[1].wait()
    for c in range(4):
        rows = charges_ref[...] if c == 3 else coords_ref[:, c, :]
        cols = rows.T
        for pair in range(4):
            a = cols[32 * pair : 32 * pair + 16, :]
            b = cols[32 * pair + 16 : 32 * pair + 32, :]
            table_ref[16 * c : 16 * c + 16, LANES * pair : LANES * (pair + 1)] = jnp.concatenate([a, b], axis=1)
    copies[2].wait()
    copies[3].wait()
    ncoef, leaves = multipoles_ref.shape
    for sb in range(send_ref.shape[1] // LANES):
        send = send_ref[:, LANES * sb : LANES * (sb + 1)]
        lane = send & (LANES - 1)
        group = send >> 7
        idx = jnp.broadcast_to(lane, (ncoef, LANES))
        picked = jnp.zeros((ncoef, LANES), jnp.float32)
        for g in range(leaves // LANES):
            got = lane_gather(multipoles_ref[:, LANES * g : LANES * (g + 1)], idx)
            picked = jnp.where(group == g, got, picked)
        rows_ref[LANES * sb : LANES * (sb + 1), :] = picked.T
    side = lax.axis_index("grp") % 2 if cap else 0
    count = rows_ref.shape[0] // cap if cap else 0
    for k in range(count // 2):
        for ref, peer in ((same_ref, 2 * k + side), (other_ref, 2 * k + 1 - side)):
            ref[cap * k : cap * (k + 1), :] = rows_ref[pl.ds(pl.multiple_of(peer * cap, cap), cap), :]
    if not cap:
        same_ref[...] = rows_ref[: same_ref.shape[0], :]
        other_ref[...] = rows_ref[same_ref.shape[0] :, :]
    for copy in copies[4:]:
        copy.wait()


def join_kernel(out_ref, came_ref, digits_ref, join_ref, *, cap):
    del digits_ref
    for chip in range(join_ref.shape[0] // (2 * cap)):
        join_ref[2 * cap * chip : 2 * cap * chip + cap, :] = out_ref[cap * chip : cap * (chip + 1), :]
        join_ref[2 * cap * chip + cap : 2 * cap * (chip + 1), :] = came_ref[cap * chip : cap * (chip + 1), :]


def placed(joined_ref, rows_ref, cap):
    side = lax.axis_index("grp") % 2
    for chip in range(joined_ref.shape[0] // (2 * cap)):
        for other in range(2):
            peer = 2 * chip + (side if other == 0 else 1 - side)
            rows_ref[pl.ds(pl.multiple_of(peer * cap, cap), cap), :] = joined_ref[
                cap * (2 * chip + other) : cap * (2 * chip + other + 1), :
            ]


def counts_kernel(
    list_ref, operators_ref, source_ref, target_ref, operator_ref, place_ref, parts_ref, acc_ref,
    wide_ref, code_ref, weight_ref, a_ref, b_ref, *, ops, sources,
):
    near, leaves = list_ref.shape
    ncoef = operators_ref.shape[1]
    groups = leaves // LANES
    half, codes = acc_ref.shape
    _, block, chunk = a_ref.shape
    f32 = jnp.float32
    even = lax.axis_index("slab") % 2 == 0
    lane = lax.broadcasted_iota(jnp.int32, (near, LANES), 1)
    for g in range(groups):
        idx = 8 * (lane & 15) + 2 * g + (lane >> 6)
        part = (lane & 63) >> 4
        row = jnp.zeros((near, LANES), jnp.int32)
        for s in range(groups):
            row = jnp.where(part == s, lane_gather(list_ref[:, LANES * s : LANES * (s + 1)], idx), row)
        side = row >> 9
        side = jnp.where(even, 2 - side, side)
        place_ref[g] = (side << 9) + ((row & 7) << 6) + ((row >> 3) & 63)

    leaf, op = target_ref[...], operator_ref[...]
    upper = leaf >= half
    code_ref[0] = (op >> 2) * sources + source_ref[...]
    weight_ref[0] = (1 << (3 * (op & 3))).astype(f32)
    code_ref[1] = jnp.where(leaf < leaves, jnp.where(upper, leaf - half, leaf), -1)
    weight_ref[1] = jnp.where(upper, 4096.0, 1.0)
    marks = Marks(max(block, half))
    for part in range(target_ref.shape[0] * LANES // chunk):
        turn = part % 2
        for c in range(chunk // LANES):
            at = slice(part * (chunk // LANES) + c, part * (chunk // LANES) + c + 1)
            marks.put(b_ref.at[turn], c, code_ref[1, at, :], weight_ref[1, at, :])
        for first in range(0, codes, block):
            for c in range(chunk // LANES):
                at = slice(part * (chunk // LANES) + c, part * (chunk // LANES) + c + 1)
                marks.put(a_ref.at[turn], c, code_ref[0, at, :] - first, weight_ref[0, at, :])
            product = lax.dot_general(b_ref[turn], a_ref[turn], NT, preferred_element_type=f32)
            if part == 0:
                acc_ref[:, first : first + block] = product
            else:
                acc_ref[:, first : first + block] += product

    wide_ref[...] = pad_lanes(operators_ref[...])
    for op in range(ops):
        matrix = wide_ref[pl.ds(op, ncoef, stride=ops), :]
        matrix = jnp.concatenate([matrix, jnp.zeros((LANES - ncoef, LANES), f32)], axis=0)
        hi, lo = split(matrix)
        parts_ref[LANES * spot(op, ops) : LANES * (spot(op, ops) + 1), :] = jnp.concatenate([hi, lo], axis=1)


def spot(op, ops):
    return (op % 4) * (ops // 4) + op // 4


class Marks:
    def __init__(self, rows):
        self.iota = lax.broadcasted_iota(jnp.int32, (rows, LANES), 0).astype(jnp.int16).reshape(-1, 16, LANES)

    def put(self, ref, c, code, weight):
        size = ref.shape[0]
        code, weight = (
            jnp.broadcast_to(x, (16, LANES)).astype(t)[None] for x, t in ((code, jnp.int16), (weight, jnp.bfloat16))
        )
        marks = jnp.where(self.iota[: size // 16] == code, weight, jnp.zeros((1, 16, LANES), jnp.bfloat16))
        ref[:, LANES * c : LANES * (c + 1)] = marks.reshape(size, LANES)


def near_kernel(
    second_ref, own_ref, first_ref, place_ref, acc_ref, near_ref, low_ref, peak_ref,
    packed_ref, charge_ref, picked_ref, pot_ref,
):
    groups, near, _ = place_ref.shape
    leaves = own_ref.shape[1]
    half, codes = acc_ref.shape
    f32 = jnp.float32
    value = acc_ref[...]
    peak_ref[...] = jnp.max(value.reshape(-1, 8, codes), axis=0)
    value = value.astype(jnp.int32)
    for digit in range(8):
        h, d = digit // 4, digit % 4
        here = (value >> (3 * digit)) & 7
        low_ref[half * h : half * (h + 1), codes * d : codes * (d + 1)] = here.astype(f32).astype(jnp.bfloat16)

    me = lax.axis_index("slab")
    last = lax.axis_size("slab") - 1
    from_right = me % 2 == 0
    ends = (jnp.logical_and(from_right, me == last), False, jnp.where(from_right, me == 0, me == last))
    for k, (ref, end) in enumerate(zip((first_ref, own_ref, second_ref), ends)):
        x, y, z = (
            jnp.minimum(jnp.floor(ref[PTS * c : PTS * (c + 1), :] * UNITS), UNITS - 1.0).astype(jnp.int32)
            for c in range(3)
        )
        at = slice(leaves * k, leaves * (k + 1))
        packed_ref[:PTS, at] = (x << 11) | ((y >> 10) & 2047)
        packed_ref[PTS:, at] = (z << 11) | ((y & 1023) << 1)
        charge_ref[:, at] = jnp.where(end, 0.0, ref[3 * PTS :, :])

    def gather(place):
        idx = place & (LANES - 1)
        bits = [(place >> (7 + level)) & 1 == 1 for level in range(4)]
        refs = [packed_ref.at[8 * r : 8 * r + 8] for r in range(2 * PTS // 8)]
        refs += [charge_ref.at[8 * r : 8 * r + 8] for r in range(PTS // 8)]
        found = []
        for ref in refs:
            layer = [lane_gather(ref[:, LANES * s : LANES * (s + 1)], idx) for s in range(3 * groups)]
            for bit in bits:
                layer = [
                    jnp.where(bit, layer[i + 1], layer[i]) if i + 1 < len(layer) else layer[i]
                    for i in range(0, len(layer), 2)
                ]
            found.append(layer[0])
        return found

    def step(g, carry):
        at = pl.ds(pl.multiple_of(g * LANES, LANES), LANES)
        tx, ty, tz = (own_ref[PTS * c : PTS * (c + 1), at] * SCALE for c in range(3))
        square = tx * tx + ty * ty + (tz * tz + SOFT2 * SCALE * SCALE)
        tx, ty, tz = -2.0 * tx, -2.0 * ty, -2.0 * tz
        acc = jnp.zeros((PTS, LANES), f32)
        for n in range(near):
            found = gather(jnp.broadcast_to(place_ref[g, n : n + 1, :], (8, LANES)))
            for r in range(PTS // 8):
                first, second, charge = found[r :: PTS // 8]
                x = first.astype(f32)
                y = ((first << 21) | ((second & 2047) << 10)).astype(f32)
                z = second.astype(f32)
                for k, row in enumerate((x, y, z, charge, x * x + y * y + z * z)):
                    picked_ref[n, PTS * k + 8 * r : PTS * k + 8 * r + 8, :] = row
            for p in range(PTS):
                sx, sy, sz, q, far = (picked_ref[n, PTS * c + p : PTS * c + p + 1, :] for c in range(5))
                acc += q * lax.rsqrt((square + far) + tx * sx + (ty * sy + tz * sz))
        pot_ref[g] = acc * SCALE
        return carry

    lax.fori_loop(0, groups, step, 0)
    width = LANES // 2
    pieces = []
    for g in range(groups):
        pot = pot_ref[g]
        pieces += [pot[:, :width], pot[:, width:]]
    near_ref[...] = jnp.concatenate(pieces, axis=0).T


def far_kernel(
    parts_ref, low_ref, peak_ref, source_ref, target_ref, operator_ref, near_ref, *refs, ops, cap,
):
    *join_refs, out_hbm, near_hbm, out_ref, received_ref, split_ref, pair_ref, a_ref, b_ref, sems = refs
    results = [pltpu.make_async_copy(near_ref, near_hbm, sems.at[2])]
    results[0].start()
    if cap:
        placed(join_refs[0], received_ref, cap)
    else:
        received_ref = join_refs[0]
    ncoef, leaves = out_ref.shape
    sources = received_ref.shape[0]
    f32 = jnp.float32
    hi, lo = split(pad_lanes(received_ref[...]))
    both = jnp.concatenate(
        [jnp.concatenate([hi, hi], axis=1), jnp.concatenate([lo, jnp.zeros_like(lo)], axis=1)], axis=0
    )
    table = lax.dot_general(parts_ref[...], both, NT, preferred_element_type=f32)
    table = table[:, :sources] + table[:, sources:]
    ones = jnp.where(lax.broadcasted_iota(jnp.int32, (LANES, sources), 0) == LANES - 1, 1.0, 0.0)
    for k in range(ops):
        hi, lo = split(table[LANES * k : LANES * (k + 1), :] + ones)
        split_ref[:LANES, sources * k : sources * (k + 1)] = hi
        split_ref[LANES:, sources * k : sources * (k + 1)] = lo
    total = jnp.zeros((), f32)
    for part in range(2):
        at = pl.ds(leaves // 2 * part, leaves // 2)
        both = lax.dot_general(split_ref[...], low_ref[at, :], NT, preferred_element_type=f32)
        out_ref[:, at] = both[:ncoef, :] + both[LANES : LANES + ncoef, :]
        results.append(pltpu.make_async_copy(out_ref.at[:, at], out_hbm.at[:, at], sems.at[part]))
        results[-1].start()
        total += jnp.sum(both[LANES - 1 : LANES, :])

    used = jnp.sum(jnp.where(target_ref[...] < leaves, 1.0, 0.0))
    carried = jnp.logical_or(total != used, jnp.max(peak_ref[...]) >= 2.0**24)
    for result in results:
        result.wait()

    @pl.when(carried)
    def _():
        size, chunk = a_ref.shape
        marks = Marks(max(size, leaves))
        out_ref[...] = jnp.zeros_like(out_ref)
        for first in range(0, ops // 2 * sources, size):
            pair_ref[...] = jnp.full(pair_ref.shape, -(2.0**24), f32)

            def more(part, carry):
                for c in range(chunk // LANES):
                    at = pl.ds(part * (chunk // LANES) + c, 1)
                    op = operator_ref[at, :]
                    code = (op >> 1) * sources + source_ref[at, :] - first
                    marks.put(a_ref, c, code, jnp.where((op & 1) == 1, 8192.0, 1.0))
                    marks.put(b_ref, c, target_ref[at, :], jnp.ones((1, LANES), f32))
                pair_ref[...] += lax.dot_general(b_ref[...], a_ref[...], NT, preferred_element_type=f32)
                return carry

            lax.fori_loop(0, target_ref.shape[0] * LANES // chunk, more, 0)
            for lane in range(first, first + size, LANES):
                value = pair_ref[:, lane - first : lane - first + LANES]
                odd = jnp.floor(value * (1.0 / 8192.0))
                for parity, count in enumerate((value - 8192.0 * odd, odd + 2048.0)):
                    at = spot(2 * (lane // sources) + parity, ops) * sources + lane % sources
                    rows = split_ref[:, at : at + LANES].astype(f32)
                    rows = rows[:ncoef, :] + rows[LANES : LANES + ncoef, :]
                    out_ref[...] += lax.dot_general(
                        rows, count, NT, precision=lax.Precision.HIGHEST, preferred_element_type=f32
                    )
        again = pltpu.make_async_copy(out_ref, out_hbm, sems.at[0])
        again.start()
        again.wait()


def shards(
    coords,
    charges,
    multipoles,
    operators,
    send_list,
    near_list,
    m2l_source,
    m2l_target,
    m2l_operator,
):
    ncoef, leaves = multipoles.shape
    npoints = charges.shape[0]
    near = near_list.shape[1]
    entries = m2l_source.shape[1]
    ops = operators.shape[0]
    sources = send_list.shape[1]
    peers = lax.axis_size("grp")
    f32, bf16 = jnp.float32, jnp.bfloat16

    tiles = npoints // LANES
    cap = sources // peers if peers == 8 else 0
    points = (jnp.transpose(coords.reshape(3, tiles, LANES), (1, 0, 2)), charges.reshape(tiles, LANES))
    others = (
        near_list.T,
        *(x.reshape(entries // LANES, LANES) for x in (m2l_source, m2l_target, m2l_operator)),
        jnp.transpose(operators, (1, 0, 2)).reshape(ncoef * ops, ncoef),
    )
    table, same, other, near_list, m2l_source, m2l_target, m2l_operator, operators = pl.pallas_call(
        functools.partial(prep_kernel, others=len(others), cap=cap),
        name="prep",
        out_shape=(
            pltpu.VMEM((4 * PTS, leaves), f32),
            pltpu.VMEM((sources // 2, ncoef), f32),
            pltpu.VMEM((sources // 2, ncoef), f32),
            *(pltpu.VMEM(x.shape, x.dtype) for x in others),
        ),
        in_specs=[ANY] * (4 + len(others)),
        out_specs=(VMEM,) * (3 + len(others)),
        scratch_shapes=[
            pltpu.VMEM((tiles, 3, LANES), f32),
            pltpu.VMEM((tiles, LANES), f32),
            pltpu.VMEM((ncoef, leaves), f32),
            pltpu.VMEM((1, sources), jnp.int32),
            pltpu.VMEM((sources, ncoef), f32),
            pltpu.SemaphoreType.DMA((4 + len(others),)),
        ],
        compiler_params=PARAMS,
    )(*(pltpu.with_memory_space_constraint(x, pltpu.HBM) for x in (*points, multipoles, send_list, *others)))
    codes = ops // 4 * sources
    block = min(codes, 512)
    groups = leaves // LANES
    chunk = entries // 4
    places, parts, digits = pl.pallas_call(
        functools.partial(counts_kernel, ops=ops, sources=sources),
        name="counts",
        out_shape=(
            jax.ShapeDtypeStruct((groups, near, LANES), jnp.int32),
            jax.ShapeDtypeStruct((ops * LANES, 2 * LANES), bf16),
            jax.ShapeDtypeStruct((leaves // 2, codes), f32),
        ),
        in_specs=[VMEM] * 5,
        out_specs=(VMEM,) * 3,
        scratch_shapes=[
            pltpu.VMEM((ncoef * ops, LANES), f32),
            pltpu.VMEM((2, entries // LANES, LANES), jnp.int32),
            pltpu.VMEM((2, entries // LANES, LANES), f32),
            pltpu.VMEM((2, block, chunk), bf16),
            pltpu.VMEM((2, leaves // 2, chunk), bf16),
        ],
        compiler_params=PARAMS,
    )(near_list, operators, m2l_source, m2l_target, m2l_operator)
    if cap:
        came = lax.ppermute(other, "grp", [(i, i ^ 1) for i in range(peers)])
        joined = pl.pallas_call(
            functools.partial(join_kernel, cap=cap),
            name="join",
            out_shape=jax.ShapeDtypeStruct((sources, ncoef), f32),
            in_specs=[VMEM, VMEM, ANY],
            out_specs=VMEM,
            compiler_params=PARAMS,
        )(same, came, digits)
        sides = [[2 * chip + side for chip in range(peers // 2)] for side in range(2)]
        received = [
            lax.all_to_all(
                joined.reshape(peers // 2, 2 * cap, ncoef),
                "grp",
                split_axis=0,
                concat_axis=0,
                axis_index_groups=sides,
                tiled=True,
            ).reshape(sources, ncoef)
        ]
    else:
        received = [
            lax.all_to_all(
                jnp.concatenate([same, other]).reshape(peers, sources // peers, ncoef), "grp", split_axis=0, concat_axis=0, tiled=True
            ).reshape(sources, ncoef)
        ]
    slabs = lax.axis_size("slab")

    def exchange(start):
        to = {}
        for slab in range(slabs):
            other = slab + 1 if (slab - start) % 2 == 0 else slab - 1
            for peer in range(peers):
                if 0 <= other < slabs:
                    to[slab * peers + peer] = other * peers + peer
                else:
                    to[slab * peers + peer] = slab * peers + min(peer ^ 1, peers - 1)
        return lax.ppermute(table, ("slab", "grp"), sorted(to.items()))

    first = exchange(0)
    second = exchange(1)

    near_potential, low, peak = pl.pallas_call(
        near_kernel,
        name="near",
        out_shape=(
            pltpu.VMEM((tiles, LANES), f32),
            jax.ShapeDtypeStruct((leaves, ops * sources), bf16),
            jax.ShapeDtypeStruct((8, codes), f32),
        ),
        in_specs=[VMEM] * 5,
        out_specs=(VMEM,) * 3,
        scratch_shapes=[
            pltpu.VMEM((2 * PTS, 3 * leaves), jnp.int32),
            pltpu.VMEM((PTS, 3 * leaves), f32),
            pltpu.VMEM((near, 5 * PTS, LANES), f32),
            pltpu.VMEM((groups, PTS, LANES), f32),
        ],
        compiler_params=PARAMS,
    )(second, table, first, places, digits)

    local_exp, near_potential = pl.pallas_call(
        functools.partial(far_kernel, ops=ops, cap=cap),
        name="far",
        out_shape=(jax.ShapeDtypeStruct((ncoef, leaves), f32), jax.ShapeDtypeStruct((tiles, LANES), f32)),
        in_specs=[VMEM] * (7 + len(received)),
        out_specs=(ANY, ANY),
        scratch_shapes=[
            pltpu.VMEM((ncoef, leaves), f32),
            pltpu.VMEM((sources, ncoef), f32),
            pltpu.VMEM((2 * LANES, ops * sources), bf16),
            pltpu.VMEM((leaves, 512), f32),
            pltpu.VMEM((512, 512), bf16),
            pltpu.VMEM((leaves, 512), bf16),
            pltpu.SemaphoreType.DMA((3,)),
        ],
        compiler_params=PARAMS,
    )(parts, low, peak, m2l_source, m2l_target, m2l_operator, near_potential, *received)
    return (local_exp, near_potential.reshape(npoints))


def solution(mesh):
    both = ("slab", "grp")
    return jax.shard_map(
        shards,
        mesh=mesh,
        in_specs=(
            P(None, both),
            P(both),
            P(None, both),
            P(),
            P(both, None),
            P(both, None),
            P(both, None),
            P(both, None),
            P(both, None),
        ),
        out_specs=(P(None, both), P(both)),
        check_vma=False,
    )
```

```python
import functools

import jax
import jax.numpy as jnp
from jax import lax
from jax.experimental import pallas as pl
from jax.experimental.pallas import tpu as pltpu
from jax.sharding import PartitionSpec as P

SOFT2 = 0.0625
LANES = 128
CHIPS = (0, 3, 1, 2)
PTS = 16
UNITS = 2.0**20
SCALE = 2.0**31
VMEM = pl.BlockSpec(memory_space=pltpu.VMEM)
ANY = pl.BlockSpec(memory_space=pl.ANY)
PARAMS = pltpu.CompilerParams(vmem_limit_bytes=48 * 1024 * 1024)
NT = (((1,), (1,)), ((), ()))


def lane_gather(x, idx):
    return jnp.take_along_axis(x, idx, axis=1, mode="promise_in_bounds")


def split(x):
    hi = x.astype(jnp.bfloat16)
    return hi, (x - hi.astype(jnp.float32)).astype(jnp.bfloat16)


def pad_lanes(x):
    return jnp.concatenate([x, jnp.zeros((x.shape[0], LANES - x.shape[1]), x.dtype)], axis=1)


def prep_kernel(coords_hbm, charges_hbm, multipoles_hbm, send_hbm, *refs, others, cap):
    sources, refs = refs[:others], refs[others:]
    (table_ref, same_ref, other_ref, *targets), refs = refs[: others + 3], refs[others + 3 :]
    coords_ref, charges_ref, multipoles_ref, send_ref, rows_ref, sems = refs
    pairs = (
        (coords_hbm, coords_ref),
        (charges_hbm, charges_ref),
        (send_hbm, send_ref),
        (multipoles_hbm, multipoles_ref),
        *zip(sources, targets),
    )
    copies = [pltpu.make_async_copy(src, dst, sems.at[i]) for i, (src, dst) in enumerate(pairs)]
    for copy in copies:
        copy.start()
    copies[0].wait()
    copies[1].wait()
    for c in range(4):
        rows = charges_ref[...] if c == 3 else coords_ref[:, c, :]
        cols = rows.T
        for pair in range(4):
            a = cols[32 * pair : 32 * pair + 16, :]
            b = cols[32 * pair + 16 : 32 * pair + 32, :]
            table_ref[16 * c : 16 * c + 16, LANES * pair : LANES * (pair + 1)] = jnp.concatenate([a, b], axis=1)
    copies[2].wait()
    copies[3].wait()
    ncoef, leaves = multipoles_ref.shape
    for sb in range(send_ref.shape[1] // LANES):
        send = send_ref[:, LANES * sb : LANES * (sb + 1)]
        lane = send & (LANES - 1)
        group = send >> 7
        idx = jnp.broadcast_to(lane, (ncoef, LANES))
        picked = lane_gather(multipoles_ref[:, :LANES], idx)
        for g in range(1, leaves // LANES):
            got = lane_gather(multipoles_ref[:, LANES * g : LANES * (g + 1)], idx)
            picked = jnp.where(group == g, got, picked)
        rows_ref[LANES * sb : LANES * (sb + 1), :] = picked.T
    side = lax.axis_index("grp") % 2 if cap else 0
    count = rows_ref.shape[0] // cap if cap else 0
    for k in range(count // 2):
        for ref, peer in ((same_ref, 2 * k + side), (other_ref, 2 * k + 1 - side)):
            ref[cap * k : cap * (k + 1), :] = rows_ref[pl.ds(pl.multiple_of(peer * cap, cap), cap), :]
    if not cap:
        same_ref[...] = rows_ref[: same_ref.shape[0], :]
        other_ref[...] = rows_ref[same_ref.shape[0] :, :]
    for copy in copies[4:]:
        copy.wait()


def join_kernel(out_ref, came_ref, digits_ref, *join_refs, cap):
    del digits_ref
    chip = lax.axis_index("grp") // 2
    for m, ref in enumerate(join_refs):
        at = pl.ds(pl.multiple_of((chip ^ m) * cap, cap), cap)
        ref[:cap, :] = out_ref[at, :]
        ref[cap:, :] = came_ref[at, :]


def placed(join_refs, rows_ref, cap):
    me = lax.axis_index("grp")
    for m, ref in zip(CHIPS, join_refs):
        peer = me ^ (2 * m)
        rows_ref[pl.ds(pl.multiple_of(peer * cap, cap), cap), :] = ref[:cap, :]
        rows_ref[pl.ds(pl.multiple_of((peer ^ 1) * cap, cap), cap), :] = ref[cap:, :]


def counts_kernel(
    list_ref, operators_ref, source_ref, target_ref, operator_ref, place_ref, parts_ref, acc_ref,
    wide_ref, code_ref, weight_ref, a_ref, b_ref, *, ops, sources,
):
    near, leaves = list_ref.shape
    ncoef = operators_ref.shape[1]
    groups = leaves // LANES
    half, codes = acc_ref.shape
    _, block, chunk = a_ref.shape
    f32 = jnp.float32
    even = lax.axis_index("slab") % 2 == 0
    lane = lax.broadcasted_iota(jnp.int32, (near, LANES), 1)
    for g in range(groups):
        idx = 8 * (lane & 15) + 2 * g + (lane >> 6)
        part = (lane & 63) >> 4
        row = jnp.zeros((near, LANES), jnp.int32)
        for s in range(groups):
            row = jnp.where(part == s, lane_gather(list_ref[:, LANES * s : LANES * (s + 1)], idx), row)
        side = row >> 9
        side = jnp.where(even, 2 - side, side)
        place_ref[g] = (side << 9) + ((row & 7) << 6) + ((row >> 3) & 63)

    leaf, op = target_ref[...], operator_ref[...]
    upper = leaf >= half
    code_ref[0] = (op >> 2) * sources + source_ref[...]
    weight_ref[0] = (1 << (3 * (op & 3))).astype(f32)
    code_ref[1] = jnp.where(leaf < leaves, jnp.where(upper, leaf - half, leaf), -1)
    weight_ref[1] = jnp.where(upper, 4096.0, 1.0)
    marks = Marks(max(block, half))
    for part in range(target_ref.shape[0] * LANES // chunk):
        turn = part % 2
        for c in range(chunk // LANES):
            at = slice(part * (chunk // LANES) + c, part * (chunk // LANES) + c + 1)
            marks.put(b_ref.at[turn], c, code_ref[1, at, :], weight_ref[1, at, :])
        for first in range(0, codes, block):
            for c in range(chunk // LANES):
                at = slice(part * (chunk // LANES) + c, part * (chunk // LANES) + c + 1)
                marks.put(a_ref.at[turn], c, code_ref[0, at, :] - first, weight_ref[0, at, :])
            product = lax.dot_general(b_ref[turn], a_ref[turn], NT, preferred_element_type=f32)
            if part == 0:
                acc_ref[:, first : first + block] = product
            else:
                acc_ref[:, first : first + block] += product

    wide_ref[...] = pad_lanes(operators_ref[...])
    for op in range(ops):
        matrix = wide_ref[pl.ds(op, ncoef, stride=ops), :]
        matrix = jnp.concatenate([matrix, jnp.zeros((LANES - ncoef, LANES), f32)], axis=0)
        hi, lo = split(matrix)
        parts_ref[LANES * spot(op, ops) : LANES * (spot(op, ops) + 1), :] = jnp.concatenate([hi, lo], axis=1)


def spot(op, ops):
    return (op % 4) * (ops // 4) + op // 4


class Marks:
    def __init__(self, rows):
        self.iota = lax.broadcasted_iota(jnp.int32, (rows, LANES), 0).astype(jnp.int16).reshape(-1, 16, LANES)

    def put(self, ref, c, code, weight):
        size = ref.shape[0]
        code, weight = (
            jnp.broadcast_to(x, (16, LANES)).astype(t)[None] for x, t in ((code, jnp.int16), (weight, jnp.bfloat16))
        )
        marks = jnp.where(self.iota[: size // 16] == code, weight, jnp.zeros((1, 16, LANES), jnp.bfloat16))
        ref[:, LANES * c : LANES * (c + 1)] = marks.reshape(size, LANES)


def near_kernel(
    second_ref, own_ref, first_ref, place_ref, acc_ref, near_ref, low_ref, peak_ref,
    packed_ref, charge_ref, picked_ref, pot_ref,
):
    groups, near, _ = place_ref.shape
    leaves = own_ref.shape[1]
    half, codes = acc_ref.shape
    f32 = jnp.float32
    value = acc_ref[...]
    peak_ref[...] = jnp.max(value.reshape(-1, 8, codes), axis=0)
    value = value.astype(jnp.int32)
    for digit in range(8):
        h, d = digit // 4, digit % 4
        here = (value >> (3 * digit)) & 7
        low_ref[half * h : half * (h + 1), codes * d : codes * (d + 1)] = here.astype(f32).astype(jnp.bfloat16)

    me = lax.axis_index("slab")
    last = lax.axis_size("slab") - 1
    from_right = me % 2 == 0
    ends = (jnp.logical_and(from_right, me == last), False, jnp.where(from_right, me == 0, me == last))
    for k, (ref, end) in enumerate(zip((first_ref, own_ref, second_ref), ends)):
        x, y, z = (
            jnp.minimum(jnp.floor(ref[PTS * c : PTS * (c + 1), :] * UNITS), UNITS - 1.0).astype(jnp.int32)
            for c in range(3)
        )
        at = slice(leaves * k, leaves * (k + 1))
        packed_ref[:PTS, at] = (x << 11) | ((y >> 10) & 2047)
        packed_ref[PTS:, at] = (z << 11) | ((y & 1023) << 1)
        charge_ref[:, at] = jnp.where(end, 0.0, ref[3 * PTS :, :])

    def gather(place):
        idx = place & (LANES - 1)
        bits = [place & (LANES << level) != 0 for level in range(4)]
        refs = [packed_ref.at[8 * r : 8 * r + 8] for r in range(2 * PTS // 8)]
        refs += [charge_ref.at[8 * r : 8 * r + 8] for r in range(PTS // 8)]
        found = []
        for ref in refs:
            layer = [lane_gather(ref[:, LANES * s : LANES * (s + 1)], idx) for s in range(3 * groups)]
            for bit in bits:
                layer = [
                    jnp.where(bit, layer[i + 1], layer[i]) if i + 1 < len(layer) else layer[i]
                    for i in range(0, len(layer), 2)
                ]
            found.append(layer[0])
        return found

    def step(g, carry):
        at = pl.ds(pl.multiple_of(g * LANES, LANES), LANES)
        tx, ty, tz = (own_ref[PTS * c : PTS * (c + 1), at] * SCALE for c in range(3))
        square = tx * tx + ty * ty + (tz * tz + SOFT2 * SCALE * SCALE)
        tx, ty, tz = -2.0 * tx, -2.0 * ty, -2.0 * tz
        acc = jnp.zeros((PTS, LANES), f32)
        for n in range(near):
            found = gather(jnp.broadcast_to(place_ref[g, n : n + 1, :], (8, LANES)))
            for r in range(PTS // 8):
                first, second, charge = found[r :: PTS // 8]
                x = first.astype(f32)
                y = ((first << 21) | ((second & 2047) << 10)).astype(f32)
                z = second.astype(f32)
                for k, row in enumerate((x, y, z, charge, x * x + y * y + z * z)):
                    picked_ref[n, PTS * k + 8 * r : PTS * k + 8 * r + 8, :] = row
            for p in range(PTS):
                sx, sy, sz, q, far = (picked_ref[n, PTS * c + p : PTS * c + p + 1, :] for c in range(5))
                acc += q * lax.rsqrt((square + far) + tx * sx + (ty * sy + tz * sz))
        pot_ref[g] = acc * SCALE
        return carry

    lax.fori_loop(0, groups, step, 0)
    width = LANES // 2
    pieces = []
    for g in range(groups):
        pot = pot_ref[g]
        pieces += [pot[:, :width], pot[:, width:]]
    near_ref[...] = jnp.concatenate(pieces, axis=0).T


def far_kernel(
    parts_ref, low_ref, peak_ref, source_ref, target_ref, operator_ref, near_ref, *refs, ops, cap,
):
    *join_refs, out_hbm, near_hbm, out_ref, received_ref, split_ref, pair_ref, a_ref, b_ref, sems = refs
    results = [pltpu.make_async_copy(near_ref, near_hbm, sems.at[2])]
    results[0].start()
    if cap:
        placed(join_refs, received_ref, cap)
    else:
        received_ref = join_refs[0]
    ncoef, leaves = out_ref.shape
    sources = received_ref.shape[0]
    f32 = jnp.float32
    hi, lo = split(pad_lanes(received_ref[...]))
    both = jnp.concatenate(
        [jnp.concatenate([hi, hi], axis=1), jnp.concatenate([lo, jnp.zeros_like(lo)], axis=1)], axis=0
    )
    table = lax.dot_general(parts_ref[...], both, NT, preferred_element_type=f32)
    table = table[:, :sources] + table[:, sources:]
    ones = jnp.where(lax.broadcasted_iota(jnp.int32, (LANES, sources), 0) == LANES - 1, 1.0, 0.0)
    for k in range(ops):
        hi, lo = split(table[LANES * k : LANES * (k + 1), :] + ones)
        split_ref[:LANES, sources * k : sources * (k + 1)] = hi
        split_ref[LANES:, sources * k : sources * (k + 1)] = lo
    total = jnp.zeros((), f32)
    for part in range(2):
        at = pl.ds(leaves // 2 * part, leaves // 2)
        both = lax.dot_general(split_ref[...], low_ref[at, :], NT, preferred_element_type=f32)
        out_ref[:, at] = both[:ncoef, :] + both[LANES : LANES + ncoef, :]
        results.append(pltpu.make_async_copy(out_ref.at[:, at], out_hbm.at[:, at], sems.at[part]))
        results[-1].start()
        total += jnp.sum(both[LANES - 1 : LANES, :])

    used = jnp.sum(jnp.where(target_ref[...] < leaves, 1.0, 0.0))
    carried = jnp.logical_or(total != used, jnp.max(peak_ref[...]) >= 2.0**24)
    for result in results:
        result.wait()

    @pl.when(carried)
    def _():
        size, chunk = a_ref.shape
        marks = Marks(max(size, leaves))
        out_ref[...] = jnp.zeros_like(out_ref)
        for first in range(0, ops // 2 * sources, size):
            pair_ref[...] = jnp.full(pair_ref.shape, -(2.0**24), f32)

            def more(part, carry):
                for c in range(chunk // LANES):
                    at = pl.ds(part * (chunk // LANES) + c, 1)
                    op = operator_ref[at, :]
                    code = (op >> 1) * sources + source_ref[at, :] - first
                    marks.put(a_ref, c, code, jnp.where((op & 1) == 1, 8192.0, 1.0))
                    marks.put(b_ref, c, target_ref[at, :], jnp.ones((1, LANES), f32))
                pair_ref[...] += lax.dot_general(b_ref[...], a_ref[...], NT, preferred_element_type=f32)
                return carry

            lax.fori_loop(0, target_ref.shape[0] * LANES // chunk, more, 0)
            for lane in range(first, first + size, LANES):
                value = pair_ref[:, lane - first : lane - first + LANES]
                odd = jnp.floor(value * (1.0 / 8192.0))
                for parity, count in enumerate((value - 8192.0 * odd, odd + 2048.0)):
                    at = spot(2 * (lane // sources) + parity, ops) * sources + lane % sources
                    rows = split_ref[:, at : at + LANES].astype(f32)
                    rows = rows[:ncoef, :] + rows[LANES : LANES + ncoef, :]
                    out_ref[...] += lax.dot_general(
                        rows, count, NT, precision=lax.Precision.HIGHEST, preferred_element_type=f32
                    )
        again = pltpu.make_async_copy(out_ref, out_hbm, sems.at[0])
        again.start()
        again.wait()


def shards(
    coords,
    charges,
    multipoles,
    operators,
    send_list,
    near_list,
    m2l_source,
    m2l_target,
    m2l_operator,
):
    ncoef, leaves = multipoles.shape
    npoints = charges.shape[0]
    near = near_list.shape[1]
    entries = m2l_source.shape[1]
    ops = operators.shape[0]
    sources = send_list.shape[1]
    peers = lax.axis_size("grp")
    f32, bf16 = jnp.float32, jnp.bfloat16

    tiles = npoints // LANES
    cap = sources // peers if peers == 8 else 0
    points = (jnp.transpose(coords.reshape(3, tiles, LANES), (1, 0, 2)), charges.reshape(tiles, LANES))
    others = (
        near_list.T,
        *(x.reshape(entries // LANES, LANES) for x in (m2l_source, m2l_target, m2l_operator)),
        jnp.transpose(operators, (1, 0, 2)).reshape(ncoef * ops, ncoef),
    )
    table, same, other, near_list, m2l_source, m2l_target, m2l_operator, operators = pl.pallas_call(
        functools.partial(prep_kernel, others=len(others), cap=cap),
        name="prep",
        out_shape=(
            pltpu.VMEM((4 * PTS, leaves), f32),
            pltpu.VMEM((sources // 2, ncoef), f32),
            pltpu.VMEM((sources // 2, ncoef), f32),
            *(pltpu.VMEM(x.shape, x.dtype) for x in others),
        ),
        in_specs=[ANY] * (4 + len(others)),
        out_specs=(VMEM,) * (3 + len(others)),
        scratch_shapes=[
            pltpu.VMEM((tiles, 3, LANES), f32),
            pltpu.VMEM((tiles, LANES), f32),
            pltpu.VMEM((ncoef, leaves), f32),
            pltpu.VMEM((1, sources), jnp.int32),
            pltpu.VMEM((sources, ncoef), f32),
            pltpu.SemaphoreType.DMA((4 + len(others),)),
        ],
        compiler_params=PARAMS,
    )(*(pltpu.with_memory_space_constraint(x, pltpu.HBM) for x in (*points, multipoles, send_list, *others)))
    codes = ops // 4 * sources
    block = min(codes, 512)
    groups = leaves // LANES
    chunk = entries // 4
    places, parts, digits = pl.pallas_call(
        functools.partial(counts_kernel, ops=ops, sources=sources),
        name="counts",
        out_shape=(
            jax.ShapeDtypeStruct((groups, near, LANES), jnp.int32),
            jax.ShapeDtypeStruct((ops * LANES, 2 * LANES), bf16),
            jax.ShapeDtypeStruct((leaves // 2, codes), f32),
        ),
        in_specs=[VMEM] * 5,
        out_specs=(VMEM,) * 3,
        scratch_shapes=[
            pltpu.VMEM((ncoef * ops, LANES), f32),
            pltpu.VMEM((2, entries // LANES, LANES), jnp.int32),
            pltpu.VMEM((2, entries // LANES, LANES), f32),
            pltpu.VMEM((2, block, chunk), bf16),
            pltpu.VMEM((2, leaves // 2, chunk), bf16),
        ],
        compiler_params=PARAMS,
    )(near_list, operators, m2l_source, m2l_target, m2l_operator)
    if cap:
        came = lax.ppermute(other, "grp", [(i, i ^ 1) for i in range(peers)])
        joins = pl.pallas_call(
            functools.partial(join_kernel, cap=cap),
            name="join",
            out_shape=(jax.ShapeDtypeStruct((2 * cap, ncoef), f32),) * (peers // 2),
            in_specs=[VMEM, VMEM, ANY],
            out_specs=(VMEM,) * (peers // 2),
            compiler_params=PARAMS,
        )(same, came, digits)
        received = [joins[0]] + [
            lax.ppermute(joins[m], "grp", [(i, i ^ (2 * m)) for i in range(peers)]) for m in CHIPS[1:]
        ]
    else:
        received = [
            lax.all_to_all(
                jnp.concatenate([same, other]).reshape(peers, sources // peers, ncoef), "grp", split_axis=0, concat_axis=0, tiled=True
            ).reshape(sources, ncoef)
        ]
    slabs = lax.axis_size("slab")

    def exchange(start):
        to = {}
        for slab in range(slabs):
            other = slab + 1 if (slab - start) % 2 == 0 else slab - 1
            for peer in range(peers):
                if 0 <= other < slabs:
                    to[slab * peers + peer] = other * peers + peer
                else:
                    to[slab * peers + peer] = slab * peers + min(peer ^ 1, peers - 1)
        return lax.ppermute(table, ("slab", "grp"), sorted(to.items()))

    first = exchange(0)
    second = exchange(1)

    near_potential, low, peak = pl.pallas_call(
        near_kernel,
        name="near",
        out_shape=(
            pltpu.VMEM((tiles, LANES), f32),
            jax.ShapeDtypeStruct((leaves, ops * sources), bf16),
            jax.ShapeDtypeStruct((8, codes), f32),
        ),
        in_specs=[VMEM] * 5,
        out_specs=(VMEM,) * 3,
        scratch_shapes=[
            pltpu.VMEM((2 * PTS, 3 * leaves), jnp.int32),
            pltpu.VMEM((PTS, 3 * leaves), f32),
            pltpu.VMEM((near, 5 * PTS, LANES), f32),
            pltpu.VMEM((groups, PTS, LANES), f32),
        ],
        compiler_params=PARAMS,
    )(second, table, first, places, digits)

    local_exp, near_potential = pl.pallas_call(
        functools.partial(far_kernel, ops=ops, cap=cap),
        name="far",
        out_shape=(jax.ShapeDtypeStruct((ncoef, leaves), f32), jax.ShapeDtypeStruct((tiles, LANES), f32)),
        in_specs=[VMEM] * (7 + len(received)),
        out_specs=(ANY, ANY),
        scratch_shapes=[
            pltpu.VMEM((ncoef, leaves), f32),
            pltpu.VMEM((sources, ncoef), f32),
            pltpu.VMEM((2 * LANES, ops * sources), bf16),
            pltpu.VMEM((leaves, 512), f32),
            pltpu.VMEM((512, 512), bf16),
            pltpu.VMEM((leaves, 512), bf16),
            pltpu.SemaphoreType.DMA((3,)),
        ],
        compiler_params=PARAMS,
    )(parts, low, peak, m2l_source, m2l_target, m2l_operator, near_potential, *received)
    return (local_exp, near_potential.reshape(npoints))


def solution(mesh):
    both = ("slab", "grp")
    return jax.shard_map(
        shards,
        mesh=mesh,
        in_specs=(
            P(None, both),
            P(both),
            P(None, both),
            P(),
            P(both, None),
            P(both, None),
            P(both, None),
            P(both, None),
            P(both, None),
        ),
        out_specs=(P(None, both), P(both)),
        check_vma=False,
    )
```

```python
import functools

import jax
import jax.numpy as jnp
from jax import lax
from jax.experimental import pallas as pl
from jax.experimental.pallas import tpu as pltpu
from jax.sharding import PartitionSpec as P

SOFT2 = 0.0625
LANES = 128
CHIPS = (0, 3, 1, 2)
PTS = 16
UNITS = 2.0**20
SCALE = 2.0**31
VMEM = pl.BlockSpec(memory_space=pltpu.VMEM)
ANY = pl.BlockSpec(memory_space=pl.ANY)
PARAMS = pltpu.CompilerParams(vmem_limit_bytes=48 * 1024 * 1024)
NT = (((1,), (1,)), ((), ()))


def lane_gather(x, idx):
    return jnp.take_along_axis(x, idx, axis=1, mode="promise_in_bounds")


def split(x):
    hi = x.astype(jnp.bfloat16)
    return hi, (x - hi.astype(jnp.float32)).astype(jnp.bfloat16)


def pad_lanes(x):
    return jnp.concatenate([x, jnp.zeros((x.shape[0], LANES - x.shape[1]), x.dtype)], axis=1)


def prep_kernel(coords_hbm, charges_hbm, multipoles_hbm, send_hbm, *refs, others, cap):
    sources, refs = refs[:others], refs[others:]
    (table_ref, same_ref, other_ref, *targets), refs = refs[: others + 3], refs[others + 3 :]
    coords_ref, charges_ref, multipoles_ref, send_ref, rows_ref, sems = refs
    pairs = (
        (coords_hbm, coords_ref),
        (charges_hbm, charges_ref),
        (send_hbm, send_ref),
        (multipoles_hbm, multipoles_ref),
        *zip(sources, targets),
    )
    copies = [pltpu.make_async_copy(src, dst, sems.at[i]) for i, (src, dst) in enumerate(pairs)]
    for copy in copies:
        copy.start()
    copies[0].wait()
    copies[1].wait()
    for c in range(4):
        rows = charges_ref[...] if c == 3 else coords_ref[:, c, :]
        cols = rows.T
        for pair in range(4):
            a = cols[32 * pair : 32 * pair + 16, :]
            b = cols[32 * pair + 16 : 32 * pair + 32, :]
            table_ref[16 * c : 16 * c + 16, LANES * pair : LANES * (pair + 1)] = jnp.concatenate([a, b], axis=1)
    copies[2].wait()
    copies[3].wait()
    ncoef, leaves = multipoles_ref.shape
    for sb in range(send_ref.shape[1] // LANES):
        send = send_ref[:, LANES * sb : LANES * (sb + 1)]
        lane = send & (LANES - 1)
        group = send >> 7
        idx = jnp.broadcast_to(lane, (ncoef, LANES))
        picked = lane_gather(multipoles_ref[:, :LANES], idx)
        for g in range(1, leaves // LANES):
            got = lane_gather(multipoles_ref[:, LANES * g : LANES * (g + 1)], idx)
            picked = jnp.where(group == g, got, picked)
        rows_ref[LANES * sb : LANES * (sb + 1), :] = picked.T
    side = lax.axis_index("grp") % 2 if cap else 0
    count = rows_ref.shape[0] // cap if cap else 0
    for k in range(count // 2):
        for ref, peer in ((same_ref, 2 * k + side), (other_ref, 2 * k + 1 - side)):
            ref[cap * k : cap * (k + 1), :] = rows_ref[pl.ds(pl.multiple_of(peer * cap, cap), cap), :]
    if not cap:
        same_ref[...] = rows_ref[: same_ref.shape[0], :]
        other_ref[...] = rows_ref[same_ref.shape[0] :, :]
    for copy in copies[4:]:
        copy.wait()


def join_kernel(out_ref, came_ref, digits_ref, *join_refs, cap):
    del digits_ref
    chip = lax.axis_index("grp") // 2
    for m, ref in enumerate(join_refs):
        at = pl.ds(pl.multiple_of((chip ^ m) * cap, cap), cap)
        ref[:cap, :] = out_ref[at, :]
        ref[cap:, :] = came_ref[at, :]


def placed(join_refs, rows_ref, cap):
    me = lax.axis_index("grp")
    for m, ref in zip(CHIPS, join_refs):
        peer = me ^ (2 * m)
        rows_ref[pl.ds(pl.multiple_of(peer * cap, cap), cap), :] = ref[:cap, :]
        rows_ref[pl.ds(pl.multiple_of((peer ^ 1) * cap, cap), cap), :] = ref[cap:, :]


def counts_kernel(
    list_ref, source_ref, target_ref, operator_ref, place_ref, acc_ref,
    code_ref, weight_ref, a_ref, b_ref, *, sources,
):
    near, leaves = list_ref.shape
    groups = leaves // LANES
    half, codes = acc_ref.shape
    _, block, chunk = a_ref.shape
    f32 = jnp.float32
    even = lax.axis_index("slab") % 2 == 0
    lane = lax.broadcasted_iota(jnp.int32, (near, LANES), 1)
    for g in range(groups):
        idx = 8 * (lane & 15) + 2 * g + (lane >> 6)
        part = (lane & 63) >> 4
        row = jnp.zeros((near, LANES), jnp.int32)
        for s in range(groups):
            row = jnp.where(part == s, lane_gather(list_ref[:, LANES * s : LANES * (s + 1)], idx), row)
        side = row >> 9
        side = jnp.where(even, 2 - side, side)
        place_ref[g] = (side << 9) + ((row & 7) << 6) + ((row >> 3) & 63)

    leaf, op = target_ref[...], operator_ref[...]
    upper = leaf >= half
    code_ref[0] = (op >> 2) * sources + source_ref[...]
    weight_ref[0] = (1 << (3 * (op & 3))).astype(f32)
    code_ref[1] = jnp.where(leaf < leaves, jnp.where(upper, leaf - half, leaf), -1)
    weight_ref[1] = jnp.where(upper, 4096.0, 1.0)
    marks = Marks(max(block, half))
    for part in range(target_ref.shape[0] * LANES // chunk):
        turn = part % 2
        for c in range(chunk // LANES):
            at = slice(part * (chunk // LANES) + c, part * (chunk // LANES) + c + 1)
            marks.put(b_ref.at[turn], c, code_ref[1, at, :], weight_ref[1, at, :])
        for first in range(0, codes, block):
            for c in range(chunk // LANES):
                at = slice(part * (chunk // LANES) + c, part * (chunk // LANES) + c + 1)
                marks.put(a_ref.at[turn], c, code_ref[0, at, :] - first, weight_ref[0, at, :])
            product = lax.dot_general(b_ref[turn], a_ref[turn], NT, preferred_element_type=f32)
            if part == 0:
                acc_ref[:, first : first + block] = product
            else:
                acc_ref[:, first : first + block] += product


def spot(op, ops):
    return (op % 4) * (ops // 4) + op // 4


class Marks:
    def __init__(self, rows):
        self.iota = lax.broadcasted_iota(jnp.int32, (rows, LANES), 0).astype(jnp.int16).reshape(-1, 16, LANES)

    def put(self, ref, c, code, weight):
        size = ref.shape[0]
        code, weight = (
            jnp.broadcast_to(x, (16, LANES)).astype(t)[None] for x, t in ((code, jnp.int16), (weight, jnp.bfloat16))
        )
        marks = jnp.where(self.iota[: size // 16] == code, weight, jnp.zeros((1, 16, LANES), jnp.bfloat16))
        ref[:, LANES * c : LANES * (c + 1)] = marks.reshape(size, LANES)


def near_kernel(
    second_ref, own_ref, first_ref, place_ref, acc_ref, operators_ref, near_ref, low_ref, peak_ref, parts_ref,
    packed_ref, charge_ref, picked_ref, pot_ref, wide_ref, *, ops,
):
    groups, near, _ = place_ref.shape
    leaves = own_ref.shape[1]
    half, codes = acc_ref.shape
    f32 = jnp.float32
    value = acc_ref[...]
    peak_ref[...] = jnp.max(value.reshape(-1, 8, codes), axis=0)
    value = value.astype(jnp.int32)
    for digit in range(8):
        h, d = digit // 4, digit % 4
        here = (value >> (3 * digit)) & 7
        low_ref[half * h : half * (h + 1), codes * d : codes * (d + 1)] = here.astype(f32).astype(jnp.bfloat16)

    me = lax.axis_index("slab")
    last = lax.axis_size("slab") - 1
    from_right = me % 2 == 0
    ends = (jnp.logical_and(from_right, me == last), False, jnp.where(from_right, me == 0, me == last))
    for k, (ref, end) in enumerate(zip((first_ref, own_ref, second_ref), ends)):
        x, y, z = (
            jnp.minimum(jnp.floor(ref[PTS * c : PTS * (c + 1), :] * UNITS), UNITS - 1.0).astype(jnp.int32)
            for c in range(3)
        )
        at = slice(leaves * k, leaves * (k + 1))
        packed_ref[:PTS, at] = (x << 11) | ((y >> 10) & 2047)
        packed_ref[PTS:, at] = (z << 11) | ((y & 1023) << 1)
        charge_ref[:, at] = jnp.where(end, 0.0, ref[3 * PTS :, :])

    def gather(place):
        idx = place & (LANES - 1)
        bits = [place & (LANES << level) != 0 for level in range(4)]
        refs = [packed_ref.at[8 * r : 8 * r + 8] for r in range(2 * PTS // 8)]
        refs += [charge_ref.at[8 * r : 8 * r + 8] for r in range(PTS // 8)]
        found = []
        for ref in refs:
            layer = [lane_gather(ref[:, LANES * s : LANES * (s + 1)], idx) for s in range(3 * groups)]
            for bit in bits:
                layer = [
                    jnp.where(bit, layer[i + 1], layer[i]) if i + 1 < len(layer) else layer[i]
                    for i in range(0, len(layer), 2)
                ]
            found.append(layer[0])
        return found

    wide_ref[...] = pad_lanes(operators_ref[...])
    ncoef = operators_ref.shape[1]
    each = ops // groups

    def cut(g):
        for j in range(each):
            place = each * g + j
            op = 4 * lax.rem(place, ops // 4) + lax.div(place, ops // 4)
            matrix = wide_ref[pl.ds(op, ncoef, stride=ops), :]
            matrix = jnp.concatenate([matrix, jnp.zeros((LANES - ncoef, LANES), f32)], axis=0)
            hi, lo = split(matrix)
            parts_ref[pl.ds(pl.multiple_of(place * LANES, LANES), LANES), :] = jnp.concatenate([hi, lo], axis=1)

    def step(g, carry):
        cut(g)
        at = pl.ds(pl.multiple_of(g * LANES, LANES), LANES)
        tx, ty, tz = (own_ref[PTS * c : PTS * (c + 1), at] * SCALE for c in range(3))
        square = tx * tx + ty * ty + (tz * tz + SOFT2 * SCALE * SCALE)
        tx, ty, tz = -2.0 * tx, -2.0 * ty, -2.0 * tz
        acc = jnp.zeros((PTS, LANES), f32)
        for n in range(near):
            found = gather(jnp.broadcast_to(place_ref[g, n : n + 1, :], (8, LANES)))
            for r in range(PTS // 8):
                first, second, charge = found[r :: PTS // 8]
                x = first.astype(f32)
                y = ((first << 21) | ((second & 2047) << 10)).astype(f32)
                z = second.astype(f32)
                for k, row in enumerate((x, y, z, charge, x * x + y * y + z * z)):
                    picked_ref[n, PTS * k + 8 * r : PTS * k + 8 * r + 8, :] = row
            for p in range(PTS):
                sx, sy, sz, q, far = (picked_ref[n, PTS * c + p : PTS * c + p + 1, :] for c in range(5))
                acc += q * lax.rsqrt((square + far) + tx * sx + (ty * sy + tz * sz))
        pot_ref[g] = acc * SCALE
        return carry

    lax.fori_loop(0, groups, step, 0)
    width = LANES // 2
    pieces = []
    for g in range(groups):
        pot = pot_ref[g]
        pieces += [pot[:, :width], pot[:, width:]]
    near_ref[...] = jnp.concatenate(pieces, axis=0).T


def far_kernel(
    parts_ref, low_ref, peak_ref, source_ref, target_ref, operator_ref, near_ref, *refs, ops, cap,
):
    *join_refs, out_hbm, near_hbm, out_ref, received_ref, split_ref, pair_ref, a_ref, b_ref, sems = refs
    results = [pltpu.make_async_copy(near_ref, near_hbm, sems.at[2])]
    results[0].start()
    if cap:
        placed(join_refs, received_ref, cap)
    else:
        received_ref = join_refs[0]
    ncoef, leaves = out_ref.shape
    sources = received_ref.shape[0]
    f32 = jnp.float32
    hi, lo = split(pad_lanes(received_ref[...]))
    both = jnp.concatenate(
        [jnp.concatenate([hi, hi], axis=1), jnp.concatenate([lo, jnp.zeros_like(lo)], axis=1)], axis=0
    )
    table = lax.dot_general(parts_ref[...], both, NT, preferred_element_type=f32)
    table = table[:, :sources] + table[:, sources:]
    ones = jnp.where(lax.broadcasted_iota(jnp.int32, (LANES, sources), 0) == LANES - 1, 1.0, 0.0)
    for k in range(ops):
        hi, lo = split(table[LANES * k : LANES * (k + 1), :] + ones)
        split_ref[:LANES, sources * k : sources * (k + 1)] = hi
        split_ref[LANES:, sources * k : sources * (k + 1)] = lo
    total = jnp.zeros((), f32)
    for part in range(2):
        at = pl.ds(leaves // 2 * part, leaves // 2)
        both = lax.dot_general(split_ref[...], low_ref[at, :], NT, preferred_element_type=f32)
        out_ref[:, at] = both[:ncoef, :] + both[LANES : LANES + ncoef, :]
        results.append(pltpu.make_async_copy(out_ref.at[:, at], out_hbm.at[:, at], sems.at[part]))
        results[-1].start()
        total += jnp.sum(both[LANES - 1 : LANES, :])

    used = jnp.sum(jnp.where(target_ref[...] < leaves, 1.0, 0.0))
    carried = jnp.logical_or(total != used, jnp.max(peak_ref[...]) >= 2.0**24)
    for result in results:
        result.wait()

    @pl.when(carried)
    def _():
        size, chunk = a_ref.shape
        marks = Marks(max(size, leaves))
        out_ref[...] = jnp.zeros_like(out_ref)
        for first in range(0, ops // 2 * sources, size):
            pair_ref[...] = jnp.full(pair_ref.shape, -(2.0**24), f32)

            def more(part, carry):
                for c in range(chunk // LANES):
                    at = pl.ds(part * (chunk // LANES) + c, 1)
                    op = operator_ref[at, :]
                    code = (op >> 1) * sources + source_ref[at, :] - first
                    marks.put(a_ref, c, code, jnp.where((op & 1) == 1, 8192.0, 1.0))
                    marks.put(b_ref, c, target_ref[at, :], jnp.ones((1, LANES), f32))
                pair_ref[...] += lax.dot_general(b_ref[...], a_ref[...], NT, preferred_element_type=f32)
                return carry

            lax.fori_loop(0, target_ref.shape[0] * LANES // chunk, more, 0)
            for lane in range(first, first + size, LANES):
                value = pair_ref[:, lane - first : lane - first + LANES]
                odd = jnp.floor(value * (1.0 / 8192.0))
                for parity, count in enumerate((value - 8192.0 * odd, odd + 2048.0)):
                    at = spot(2 * (lane // sources) + parity, ops) * sources + lane % sources
                    rows = split_ref[:, at : at + LANES].astype(f32)
                    rows = rows[:ncoef, :] + rows[LANES : LANES + ncoef, :]
                    out_ref[...] += lax.dot_general(
                        rows, count, NT, precision=lax.Precision.HIGHEST, preferred_element_type=f32
                    )
        again = pltpu.make_async_copy(out_ref, out_hbm, sems.at[0])
        again.start()
        again.wait()


def shards(
    coords,
    charges,
    multipoles,
    operators,
    send_list,
    near_list,
    m2l_source,
    m2l_target,
    m2l_operator,
):
    ncoef, leaves = multipoles.shape
    npoints = charges.shape[0]
    near = near_list.shape[1]
    entries = m2l_source.shape[1]
    ops = operators.shape[0]
    sources = send_list.shape[1]
    peers = lax.axis_size("grp")
    f32, bf16 = jnp.float32, jnp.bfloat16

    tiles = npoints // LANES
    cap = sources // peers if peers == 8 else 0
    points = (jnp.transpose(coords.reshape(3, tiles, LANES), (1, 0, 2)), charges.reshape(tiles, LANES))
    others = (
        near_list.T,
        *(x.reshape(entries // LANES, LANES) for x in (m2l_source, m2l_target, m2l_operator)),
        jnp.transpose(operators, (1, 0, 2)).reshape(ncoef * ops, ncoef),
    )
    table, same, other, near_list, m2l_source, m2l_target, m2l_operator, operators = pl.pallas_call(
        functools.partial(prep_kernel, others=len(others), cap=cap),
        name="prep",
        out_shape=(
            pltpu.VMEM((4 * PTS, leaves), f32),
            pltpu.VMEM((sources // 2, ncoef), f32),
            pltpu.VMEM((sources // 2, ncoef), f32),
            *(pltpu.VMEM(x.shape, x.dtype) for x in others),
        ),
        in_specs=[ANY] * (4 + len(others)),
        out_specs=(VMEM,) * (3 + len(others)),
        scratch_shapes=[
            pltpu.VMEM((tiles, 3, LANES), f32),
            pltpu.VMEM((tiles, LANES), f32),
            pltpu.VMEM((ncoef, leaves), f32),
            pltpu.VMEM((1, sources), jnp.int32),
            pltpu.VMEM((sources, ncoef), f32),
            pltpu.SemaphoreType.DMA((4 + len(others),)),
        ],
        compiler_params=PARAMS,
    )(*(pltpu.with_memory_space_constraint(x, pltpu.HBM) for x in (*points, multipoles, send_list, *others)))
    codes = ops // 4 * sources
    block = min(codes, 512)
    groups = leaves // LANES
    chunk = entries // 4
    places, digits = pl.pallas_call(
        functools.partial(counts_kernel, sources=sources),
        name="counts",
        out_shape=(
            jax.ShapeDtypeStruct((groups, near, LANES), jnp.int32),
            jax.ShapeDtypeStruct((leaves // 2, codes), f32),
        ),
        in_specs=[VMEM] * 4,
        out_specs=(VMEM,) * 2,
        scratch_shapes=[
            pltpu.VMEM((2, entries // LANES, LANES), jnp.int32),
            pltpu.VMEM((2, entries // LANES, LANES), f32),
            pltpu.VMEM((2, block, chunk), bf16),
            pltpu.VMEM((2, leaves // 2, chunk), bf16),
        ],
        compiler_params=PARAMS,
    )(near_list, m2l_source, m2l_target, m2l_operator)
    if cap:
        came = lax.ppermute(other, "grp", [(i, i ^ 1) for i in range(peers)])
        joins = pl.pallas_call(
            functools.partial(join_kernel, cap=cap),
            name="join",
            out_shape=(jax.ShapeDtypeStruct((2 * cap, ncoef), f32),) * (peers // 2),
            in_specs=[VMEM, VMEM, ANY],
            out_specs=(VMEM,) * (peers // 2),
            compiler_params=PARAMS,
        )(same, came, digits)
        received = [joins[0]] + [
            lax.ppermute(joins[m], "grp", [(i, i ^ (2 * m)) for i in range(peers)]) for m in CHIPS[1:]
        ]
    else:
        received = [
            lax.all_to_all(
                jnp.concatenate([same, other]).reshape(peers, sources // peers, ncoef), "grp", split_axis=0, concat_axis=0, tiled=True
            ).reshape(sources, ncoef)
        ]
    slabs = lax.axis_size("slab")

    def exchange(start):
        to = {}
        for slab in range(slabs):
            other = slab + 1 if (slab - start) % 2 == 0 else slab - 1
            for peer in range(peers):
                if 0 <= other < slabs:
                    to[slab * peers + peer] = other * peers + peer
                else:
                    to[slab * peers + peer] = slab * peers + min(peer ^ 1, peers - 1)
        return lax.ppermute(table, ("slab", "grp"), sorted(to.items()))

    first = exchange(0)
    second = exchange(1)

    near_potential, low, peak, parts = pl.pallas_call(
        functools.partial(near_kernel, ops=ops),
        name="near",
        out_shape=(
            pltpu.VMEM((tiles, LANES), f32),
            jax.ShapeDtypeStruct((leaves, ops * sources), bf16),
            jax.ShapeDtypeStruct((8, codes), f32),
            jax.ShapeDtypeStruct((ops * LANES, 2 * LANES), bf16),
        ),
        in_specs=[VMEM] * 6,
        out_specs=(VMEM,) * 4,
        scratch_shapes=[
            pltpu.VMEM((2 * PTS, 3 * leaves), jnp.int32),
            pltpu.VMEM((PTS, 3 * leaves), f32),
            pltpu.VMEM((near, 5 * PTS, LANES), f32),
            pltpu.VMEM((groups, PTS, LANES), f32),
            pltpu.VMEM((ncoef * ops, LANES), f32),
        ],
        compiler_params=PARAMS,
    )(second, table, first, places, digits, operators)

    local_exp, near_potential = pl.pallas_call(
        functools.partial(far_kernel, ops=ops, cap=cap),
        name="far",
        out_shape=(jax.ShapeDtypeStruct((ncoef, leaves), f32), jax.ShapeDtypeStruct((tiles, LANES), f32)),
        in_specs=[VMEM] * (7 + len(received)),
        out_specs=(ANY, ANY),
        scratch_shapes=[
            pltpu.VMEM((ncoef, leaves), f32),
            pltpu.VMEM((sources, ncoef), f32),
            pltpu.VMEM((2 * LANES, ops * sources), bf16),
            pltpu.VMEM((leaves, 512), f32),
            pltpu.VMEM((512, 512), bf16),
            pltpu.VMEM((leaves, 512), bf16),
            pltpu.SemaphoreType.DMA((3,)),
        ],
        compiler_params=PARAMS,
    )(parts, low, peak, m2l_source, m2l_target, m2l_operator, near_potential, *received)
    return (local_exp, near_potential.reshape(npoints))


def solution(mesh):
    both = ("slab", "grp")
    return jax.shard_map(
        shards,
        mesh=mesh,
        in_specs=(
            P(None, both),
            P(both),
            P(None, both),
            P(),
            P(both, None),
            P(both, None),
            P(both, None),
            P(both, None),
            P(both, None),
        ),
        out_specs=(P(None, both), P(both)),
        check_vma=False,
    )
```

```python
import functools

import jax
import jax.numpy as jnp
from jax import lax
from jax.experimental import pallas as pl
from jax.experimental.pallas import tpu as pltpu
from jax.sharding import PartitionSpec as P

SOFT2 = 0.0625
LANES = 128
CHIPS = (0, 3, 1, 2)
PTS = 16
UNITS = 2.0**20
SCALE = 2.0**31
VMEM = pl.BlockSpec(memory_space=pltpu.VMEM)
ANY = pl.BlockSpec(memory_space=pl.ANY)
PARAMS = pltpu.CompilerParams(vmem_limit_bytes=48 * 1024 * 1024)
NT = (((1,), (1,)), ((), ()))


def lane_gather(x, idx):
    return jnp.take_along_axis(x, idx, axis=1, mode="promise_in_bounds")


def split(x):
    hi = x.astype(jnp.bfloat16)
    return hi, (x - hi.astype(jnp.float32)).astype(jnp.bfloat16)


def pad_lanes(x):
    return jnp.concatenate([x, jnp.zeros((x.shape[0], LANES - x.shape[1]), x.dtype)], axis=1)


def prep_kernel(coords_hbm, charges_hbm, multipoles_hbm, send_hbm, *refs, others, cap):
    sources, refs = refs[:others], refs[others:]
    (table_ref, same_ref, other_ref, *targets), refs = refs[: others + 3], refs[others + 3 :]
    coords_ref, charges_ref, multipoles_ref, send_ref, rows_ref, sems = refs
    pairs = (
        (coords_hbm, coords_ref),
        (charges_hbm, charges_ref),
        (send_hbm, send_ref),
        (multipoles_hbm, multipoles_ref),
        *zip(sources, targets),
    )
    copies = [pltpu.make_async_copy(src, dst, sems.at[i]) for i, (src, dst) in enumerate(pairs)]
    for copy in copies:
        copy.start()
    copies[0].wait()
    copies[1].wait()
    for c in range(4):
        rows = charges_ref[...] if c == 3 else coords_ref[:, c, :]
        cols = rows.T
        for pair in range(4):
            a = cols[32 * pair : 32 * pair + 16, :]
            b = cols[32 * pair + 16 : 32 * pair + 32, :]
            table_ref[16 * c : 16 * c + 16, LANES * pair : LANES * (pair + 1)] = jnp.concatenate([a, b], axis=1)
    copies[2].wait()
    copies[3].wait()
    ncoef, leaves = multipoles_ref.shape
    for sb in range(send_ref.shape[1] // LANES):
        send = send_ref[:, LANES * sb : LANES * (sb + 1)]
        lane = send & (LANES - 1)
        group = send >> 7
        idx = jnp.broadcast_to(lane, (ncoef, LANES))
        picked = lane_gather(multipoles_ref[:, :LANES], idx)
        for g in range(1, leaves // LANES):
            got = lane_gather(multipoles_ref[:, LANES * g : LANES * (g + 1)], idx)
            picked = jnp.where(group == g, got, picked)
        rows_ref[LANES * sb : LANES * (sb + 1), :] = picked.T
    side = lax.axis_index("grp") % 2 if cap else 0
    count = rows_ref.shape[0] // cap if cap else 0
    for k in range(count // 2):
        for ref, peer in ((same_ref, 2 * k + side), (other_ref, 2 * k + 1 - side)):
            ref[cap * k : cap * (k + 1), :] = rows_ref[pl.ds(pl.multiple_of(peer * cap, cap), cap), :]
    if not cap:
        same_ref[...] = rows_ref[: same_ref.shape[0], :]
        other_ref[...] = rows_ref[same_ref.shape[0] :, :]
    for copy in copies[4:]:
        copy.wait()


def join_kernel(out_ref, came_ref, digits_ref, *join_refs, cap):
    del digits_ref
    chip = lax.axis_index("grp") // 2
    for m, ref in enumerate(join_refs):
        at = pl.ds(pl.multiple_of((chip ^ m) * cap, cap), cap)
        ref[:cap, :] = out_ref[at, :]
        ref[cap:, :] = came_ref[at, :]


def placed(join_refs, rows_ref, cap):
    me = lax.axis_index("grp")
    for m, ref in zip(CHIPS, join_refs):
        peer = me ^ (2 * m)
        rows_ref[pl.ds(pl.multiple_of(peer * cap, cap), cap), :] = ref[:cap, :]
        rows_ref[pl.ds(pl.multiple_of((peer ^ 1) * cap, cap), cap), :] = ref[cap:, :]


def counts_kernel(
    list_ref, source_ref, target_ref, operator_ref, place_ref, acc_ref,
    code_ref, weight_ref, a_ref, b_ref, *, sources,
):
    near, leaves = list_ref.shape
    groups = leaves // LANES
    half, codes = acc_ref.shape
    _, block, chunk = a_ref.shape
    f32 = jnp.float32
    even = lax.axis_index("slab") % 2 == 0
    lane = lax.broadcasted_iota(jnp.int32, (near, LANES), 1)
    for g in range(groups):
        idx = 8 * (lane & 15) + 2 * g + (lane >> 6)
        part = (lane & 63) >> 4
        row = jnp.zeros((near, LANES), jnp.int32)
        for s in range(groups):
            row = jnp.where(part == s, lane_gather(list_ref[:, LANES * s : LANES * (s + 1)], idx), row)
        side = row >> 9
        side = jnp.where(even, 2 - side, side)
        place_ref[g] = (side << 9) + ((row & 7) << 6) + ((row >> 3) & 63)

    leaf, op = target_ref[...], operator_ref[...]
    upper = leaf >= half
    code_ref[0] = (op >> 2) * sources + source_ref[...]
    weight_ref[0] = (1 << (3 * (op & 3))).astype(f32)
    code_ref[1] = jnp.where(leaf < leaves, jnp.where(upper, leaf - half, leaf), -1)
    weight_ref[1] = jnp.where(upper, 4096.0, 1.0)
    marks = Marks(max(block, half))
    for part in range(target_ref.shape[0] * LANES // chunk):
        turn = part % 2
        for c in range(chunk // LANES):
            at = slice(part * (chunk // LANES) + c, part * (chunk // LANES) + c + 1)
            marks.put(b_ref.at[turn], c, code_ref[1, at, :], weight_ref[1, at, :])
        for first in range(0, codes, block):
            for c in range(chunk // LANES):
                at = slice(part * (chunk // LANES) + c, part * (chunk // LANES) + c + 1)
                marks.put(a_ref.at[turn], c, code_ref[0, at, :] - first, weight_ref[0, at, :])
            product = lax.dot_general(b_ref[turn], a_ref[turn], NT, preferred_element_type=f32)
            if part == 0:
                acc_ref[:, first : first + block] = product
            else:
                acc_ref[:, first : first + block] += product


def spot(op, ops):
    return (op % 4) * (ops // 4) + op // 4


class Marks:
    def __init__(self, rows):
        self.iota = lax.broadcasted_iota(jnp.int32, (rows, LANES), 0).astype(jnp.int16).reshape(-1, 16, LANES)

    def put(self, ref, c, code, weight):
        size = ref.shape[0]
        code, weight = (
            jnp.broadcast_to(x, (16, LANES)).astype(t)[None] for x, t in ((code, jnp.int16), (weight, jnp.bfloat16))
        )
        marks = jnp.where(self.iota[: size // 16] == code, weight, jnp.zeros((1, 16, LANES), jnp.bfloat16))
        ref[:, LANES * c : LANES * (c + 1)] = marks.reshape(size, LANES)


def near_kernel(
    second_ref, own_ref, first_ref, place_ref, acc_ref, operators_ref, near_ref, low_ref, peak_ref, parts_ref,
    packed_ref, charge_ref, picked_ref, pot_ref, wide_ref, *, ops,
):
    groups, near, _ = place_ref.shape
    leaves = own_ref.shape[1]
    half, codes = acc_ref.shape
    f32 = jnp.float32
    value = acc_ref[...]
    peak_ref[...] = jnp.max(value.reshape(-1, 8, codes), axis=0)

    def digits(g):
        value = acc_ref[...].astype(jnp.int32)
        for j in range(8 // groups):
            digit = 8 // groups * g + j
            rows = pl.ds(pl.multiple_of(half * lax.div(digit, 4), half), half)
            lanes = pl.ds(pl.multiple_of(codes * lax.rem(digit, 4), codes), codes)
            low_ref[rows, lanes] = ((value >> (3 * digit)) & 7).astype(f32).astype(jnp.bfloat16)

    me = lax.axis_index("slab")
    last = lax.axis_size("slab") - 1
    from_right = me % 2 == 0
    ends = (jnp.logical_and(from_right, me == last), False, jnp.where(from_right, me == 0, me == last))
    for k, (ref, end) in enumerate(zip((first_ref, own_ref, second_ref), ends)):
        x, y, z = (
            jnp.minimum(jnp.floor(ref[PTS * c : PTS * (c + 1), :] * UNITS), UNITS - 1.0).astype(jnp.int32)
            for c in range(3)
        )
        at = slice(leaves * k, leaves * (k + 1))
        packed_ref[:PTS, at] = (x << 11) | ((y >> 10) & 2047)
        packed_ref[PTS:, at] = (z << 11) | ((y & 1023) << 1)
        charge_ref[:, at] = jnp.where(end, 0.0, ref[3 * PTS :, :])

    def gather(place):
        idx = place & (LANES - 1)
        bits = [place & (LANES << level) != 0 for level in range(4)]
        refs = [packed_ref.at[8 * r : 8 * r + 8] for r in range(2 * PTS // 8)]
        refs += [charge_ref.at[8 * r : 8 * r + 8] for r in range(PTS // 8)]
        found = []
        for ref in refs:
            layer = [lane_gather(ref[:, LANES * s : LANES * (s + 1)], idx) for s in range(3 * groups)]
            for bit in bits:
                layer = [
                    jnp.where(bit, layer[i + 1], layer[i]) if i + 1 < len(layer) else layer[i]
                    for i in range(0, len(layer), 2)
                ]
            found.append(layer[0])
        return found

    wide_ref[...] = pad_lanes(operators_ref[...])
    ncoef = operators_ref.shape[1]
    each = ops // groups

    def cut(g):
        for j in range(each):
            place = each * g + j
            op = 4 * lax.rem(place, ops // 4) + lax.div(place, ops // 4)
            matrix = wide_ref[pl.ds(op, ncoef, stride=ops), :]
            matrix = jnp.concatenate([matrix, jnp.zeros((LANES - ncoef, LANES), f32)], axis=0)
            hi, lo = split(matrix)
            parts_ref[pl.ds(pl.multiple_of(place * LANES, LANES), LANES), :] = jnp.concatenate([hi, lo], axis=1)

    def step(g, carry):
        cut(g)
        digits(g)
        at = pl.ds(pl.multiple_of(g * LANES, LANES), LANES)
        tx, ty, tz = (own_ref[PTS * c : PTS * (c + 1), at] * SCALE for c in range(3))
        square = tx * tx + ty * ty + (tz * tz + SOFT2 * SCALE * SCALE)
        tx, ty, tz = -2.0 * tx, -2.0 * ty, -2.0 * tz
        acc = jnp.zeros((PTS, LANES), f32)
        for n in range(near):
            found = gather(jnp.broadcast_to(place_ref[g, n : n + 1, :], (8, LANES)))
            for r in range(PTS // 8):
                first, second, charge = found[r :: PTS // 8]
                x = first.astype(f32)
                y = ((first << 21) | ((second & 2047) << 10)).astype(f32)
                z = second.astype(f32)
                for k, row in enumerate((x, y, z, charge, x * x + y * y + z * z)):
                    picked_ref[n, PTS * k + 8 * r : PTS * k + 8 * r + 8, :] = row
            for p in range(PTS):
                sx, sy, sz, q, far = (picked_ref[n, PTS * c + p : PTS * c + p + 1, :] for c in range(5))
                acc += q * lax.rsqrt((square + far) + tx * sx + (ty * sy + tz * sz))
        pot_ref[g] = acc * SCALE
        return carry

    lax.fori_loop(0, groups, step, 0)
    width = LANES // 2
    pieces = []
    for g in range(groups):
        pot = pot_ref[g]
        pieces += [pot[:, :width], pot[:, width:]]
    near_ref[...] = jnp.concatenate(pieces, axis=0).T


def far_kernel(
    parts_ref, low_ref, peak_ref, source_ref, target_ref, operator_ref, near_ref, *refs, ops, cap,
):
    *join_refs, out_hbm, near_hbm, out_ref, received_ref, split_ref, pair_ref, a_ref, b_ref, sems = refs
    results = [pltpu.make_async_copy(near_ref, near_hbm, sems.at[2])]
    results[0].start()
    if cap:
        placed(join_refs, received_ref, cap)
    else:
        received_ref = join_refs[0]
    ncoef, leaves = out_ref.shape
    sources = received_ref.shape[0]
    f32 = jnp.float32
    hi, lo = split(pad_lanes(received_ref[...]))
    both = jnp.concatenate(
        [jnp.concatenate([hi, hi], axis=1), jnp.concatenate([lo, jnp.zeros_like(lo)], axis=1)], axis=0
    )
    table = lax.dot_general(parts_ref[...], both, NT, preferred_element_type=f32)
    table = table[:, :sources] + table[:, sources:]
    ones = jnp.where(lax.broadcasted_iota(jnp.int32, (LANES, sources), 0) == LANES - 1, 1.0, 0.0)
    for k in range(ops):
        hi, lo = split(table[LANES * k : LANES * (k + 1), :] + ones)
        split_ref[:LANES, sources * k : sources * (k + 1)] = hi
        split_ref[LANES:, sources * k : sources * (k + 1)] = lo
    total = jnp.zeros((), f32)
    for part in range(2):
        at = pl.ds(leaves // 2 * part, leaves // 2)
        both = lax.dot_general(split_ref[...], low_ref[at, :], NT, preferred_element_type=f32)
        out_ref[:, at] = both[:ncoef, :] + both[LANES : LANES + ncoef, :]
        results.append(pltpu.make_async_copy(out_ref.at[:, at], out_hbm.at[:, at], sems.at[part]))
        results[-1].start()
        total += jnp.sum(both[LANES - 1 : LANES, :])

    used = jnp.sum(jnp.where(target_ref[...] < leaves, 1.0, 0.0))
    carried = jnp.logical_or(total != used, jnp.max(peak_ref[...]) >= 2.0**24)
    for result in results:
        result.wait()

    @pl.when(carried)
    def _():
        size, chunk = a_ref.shape
        marks = Marks(max(size, leaves))
        out_ref[...] = jnp.zeros_like(out_ref)
        for first in range(0, ops // 2 * sources, size):
            pair_ref[...] = jnp.full(pair_ref.shape, -(2.0**24), f32)

            def more(part, carry):
                for c in range(chunk // LANES):
                    at = pl.ds(part * (chunk // LANES) + c, 1)
                    op = operator_ref[at, :]
                    code = (op >> 1) * sources + source_ref[at, :] - first
                    marks.put(a_ref, c, code, jnp.where((op & 1) == 1, 8192.0, 1.0))
                    marks.put(b_ref, c, target_ref[at, :], jnp.ones((1, LANES), f32))
                pair_ref[...] += lax.dot_general(b_ref[...], a_ref[...], NT, preferred_element_type=f32)
                return carry

            lax.fori_loop(0, target_ref.shape[0] * LANES // chunk, more, 0)
            for lane in range(first, first + size, LANES):
                value = pair_ref[:, lane - first : lane - first + LANES]
                odd = jnp.floor(value * (1.0 / 8192.0))
                for parity, count in enumerate((value - 8192.0 * odd, odd + 2048.0)):
                    at = spot(2 * (lane // sources) + parity, ops) * sources + lane % sources
                    rows = split_ref[:, at : at + LANES].astype(f32)
                    rows = rows[:ncoef, :] + rows[LANES : LANES + ncoef, :]
                    out_ref[...] += lax.dot_general(
                        rows, count, NT, precision=lax.Precision.HIGHEST, preferred_element_type=f32
                    )
        again = pltpu.make_async_copy(out_ref, out_hbm, sems.at[0])
        again.start()
        again.wait()


def shards(
    coords,
    charges,
    multipoles,
    operators,
    send_list,
    near_list,
    m2l_source,
    m2l_target,
    m2l_operator,
):
    ncoef, leaves = multipoles.shape
    npoints = charges.shape[0]
    near = near_list.shape[1]
    entries = m2l_source.shape[1]
    ops = operators.shape[0]
    sources = send_list.shape[1]
    peers = lax.axis_size("grp")
    f32, bf16 = jnp.float32, jnp.bfloat16

    tiles = npoints // LANES
    cap = sources // peers if peers == 8 else 0
    points = (jnp.transpose(coords.reshape(3, tiles, LANES), (1, 0, 2)), charges.reshape(tiles, LANES))
    others = (
        near_list.T,
        *(x.reshape(entries // LANES, LANES) for x in (m2l_source, m2l_target, m2l_operator)),
        jnp.transpose(operators, (1, 0, 2)).reshape(ncoef * ops, ncoef),
    )
    table, same, other, near_list, m2l_source, m2l_target, m2l_operator, operators = pl.pallas_call(
        functools.partial(prep_kernel, others=len(others), cap=cap),
        name="prep",
        out_shape=(
            pltpu.VMEM((4 * PTS, leaves), f32),
            pltpu.VMEM((sources // 2, ncoef), f32),
            pltpu.VMEM((sources // 2, ncoef), f32),
            *(pltpu.VMEM(x.shape, x.dtype) for x in others),
        ),
        in_specs=[ANY] * (4 + len(others)),
        out_specs=(VMEM,) * (3 + len(others)),
        scratch_shapes=[
            pltpu.VMEM((tiles, 3, LANES), f32),
            pltpu.VMEM((tiles, LANES), f32),
            pltpu.VMEM((ncoef, leaves), f32),
            pltpu.VMEM((1, sources), jnp.int32),
            pltpu.VMEM((sources, ncoef), f32),
            pltpu.SemaphoreType.DMA((4 + len(others),)),
        ],
        compiler_params=PARAMS,
    )(*(pltpu.with_memory_space_constraint(x, pltpu.HBM) for x in (*points, multipoles, send_list, *others)))
    codes = ops // 4 * sources
    block = min(codes, 512)
    groups = leaves // LANES
    chunk = entries // 4
    places, digits = pl.pallas_call(
        functools.partial(counts_kernel, sources=sources),
        name="counts",
        out_shape=(
            jax.ShapeDtypeStruct((groups, near, LANES), jnp.int32),
            jax.ShapeDtypeStruct((leaves // 2, codes), f32),
        ),
        in_specs=[VMEM] * 4,
        out_specs=(VMEM,) * 2,
        scratch_shapes=[
            pltpu.VMEM((2, entries // LANES, LANES), jnp.int32),
            pltpu.VMEM((2, entries // LANES, LANES), f32),
            pltpu.VMEM((2, block, chunk), bf16),
            pltpu.VMEM((2, leaves // 2, chunk), bf16),
        ],
        compiler_params=PARAMS,
    )(near_list, m2l_source, m2l_target, m2l_operator)
    if cap:
        came = lax.ppermute(other, "grp", [(i, i ^ 1) for i in range(peers)])
        joins = pl.pallas_call(
            functools.partial(join_kernel, cap=cap),
            name="join",
            out_shape=(jax.ShapeDtypeStruct((2 * cap, ncoef), f32),) * (peers // 2),
            in_specs=[VMEM, VMEM, ANY],
            out_specs=(VMEM,) * (peers // 2),
            compiler_params=PARAMS,
        )(same, came, digits)
        received = [joins[0]] + [
            lax.ppermute(joins[m], "grp", [(i, i ^ (2 * m)) for i in range(peers)]) for m in CHIPS[1:]
        ]
    else:
        received = [
            lax.all_to_all(
                jnp.concatenate([same, other]).reshape(peers, sources // peers, ncoef), "grp", split_axis=0, concat_axis=0, tiled=True
            ).reshape(sources, ncoef)
        ]
    slabs = lax.axis_size("slab")

    def exchange(start):
        to = {}
        for slab in range(slabs):
            other = slab + 1 if (slab - start) % 2 == 0 else slab - 1
            for peer in range(peers):
                if 0 <= other < slabs:
                    to[slab * peers + peer] = other * peers + peer
                else:
                    to[slab * peers + peer] = slab * peers + min(peer ^ 1, peers - 1)
        return lax.ppermute(table, ("slab", "grp"), sorted(to.items()))

    first = exchange(0)
    second = exchange(1)

    near_potential, low, peak, parts = pl.pallas_call(
        functools.partial(near_kernel, ops=ops),
        name="near",
        out_shape=(
            pltpu.VMEM((tiles, LANES), f32),
            jax.ShapeDtypeStruct((leaves, ops * sources), bf16),
            jax.ShapeDtypeStruct((8, codes), f32),
            jax.ShapeDtypeStruct((ops * LANES, 2 * LANES), bf16),
        ),
        in_specs=[VMEM] * 6,
        out_specs=(VMEM,) * 4,
        scratch_shapes=[
            pltpu.VMEM((2 * PTS, 3 * leaves), jnp.int32),
            pltpu.VMEM((PTS, 3 * leaves), f32),
            pltpu.VMEM((near, 5 * PTS, LANES), f32),
            pltpu.VMEM((groups, PTS, LANES), f32),
            pltpu.VMEM((ncoef * ops, LANES), f32),
        ],
        compiler_params=PARAMS,
    )(second, table, first, places, digits, operators)

    local_exp, near_potential = pl.pallas_call(
        functools.partial(far_kernel, ops=ops, cap=cap),
        name="far",
        out_shape=(jax.ShapeDtypeStruct((ncoef, leaves), f32), jax.ShapeDtypeStruct((tiles, LANES), f32)),
        in_specs=[VMEM] * (7 + len(received)),
        out_specs=(ANY, ANY),
        scratch_shapes=[
            pltpu.VMEM((ncoef, leaves), f32),
            pltpu.VMEM((sources, ncoef), f32),
            pltpu.VMEM((2 * LANES, ops * sources), bf16),
            pltpu.VMEM((leaves, 512), f32),
            pltpu.VMEM((512, 512), bf16),
            pltpu.VMEM((leaves, 512), bf16),
            pltpu.SemaphoreType.DMA((3,)),
        ],
        compiler_params=PARAMS,
    )(parts, low, peak, m2l_source, m2l_target, m2l_operator, near_potential, *received)
    return (local_exp, near_potential.reshape(npoints))


def solution(mesh):
    both = ("slab", "grp")
    return jax.shard_map(
        shards,
        mesh=mesh,
        in_specs=(
            P(None, both),
            P(both),
            P(None, both),
            P(),
            P(both, None),
            P(both, None),
            P(both, None),
            P(both, None),
            P(both, None),
        ),
        out_specs=(P(None, both), P(both)),
        check_vma=False,
    )
```
